32 devices in a mesh: seq: 8 (over z, x), ch: 4 (over y, core).
Axes of the slice: x: 2, y: 2, z: 4, core: 2. Of those that a mesh axis runs over, the one named last changes fastest.
Arguments:
- proj: bfloat16 [3, 128, 8192], P(None, 'ch', 'seq'), may hold values from -6 to 6
- cotangent: bfloat16 [128, 8192], P('ch', 'seq'), may hold values from -6 to 6
- short_w: float32 [3, 128, 3], P(None, 'ch'), may hold values from -3.5 to 3.5
- filter_in: float32 [32, 64], replicated, may hold values from -5 to 5
- filter_out: float32 [64, 128], P(None, 'ch'), may hold values from -0.75 to 0.75
- rates: float32 [128], P('ch'), may hold values from 0.25 to 273
Outputs:
- grad_proj: bfloat16 [3, 128, 8192], P(None, 'ch', 'seq')
- grad_short: float32 [3, 128, 3], P(None, 'ch')
- grad_filter_out: float32 [64, 128], P(None, 'ch')
- grad_filter_in: float32 [32, 64], replicated
The draws below stay inside these ranges and needn't reach their ends.
All inputs are finite; a program needn't handle non-finite values.
Results may differ from the reference program's by a relative error of at most 0.0013.
Values may be sent and summed in bfloat16 or wider, within the bound.
No kernel may reach another device: no remote copies, remote signals or barrier semaphores. Data moves between devices by JAX's collectives and lax.ppermute only.
A program may use at most 64 MiB of HBM per device.

```python
import math
import jax
import jax.numpy as jnp
from jax import lax

CH = 128
ORDER = 64
FEAT = 32
TAPS = 3
SEQ_LEN = 8192


def draw_rates(key, part):
    key_choose, key_slow, key_fast = jax.random.split(key, 3)
    slow_share = 0.5
    slow_mask = jax.random.uniform(key_choose, (CH,), jnp.float32) < slow_share
    low_log = math.log(0.25)
    mid_log = math.log(2.3)
    top_log = math.log(SEQ_LEN // 30)
    slow_rate = jnp.exp(low_log + (mid_log - low_log) * jax.random.uniform(key_slow, (CH,), jnp.float32))
    fast_rate = jnp.exp(mid_log + (top_log - mid_log) * jax.random.uniform(key_fast, (CH,), jnp.float32))
    picked = jnp.where(slow_mask, slow_rate, fast_rate)
    return jnp.clip(picked, 0.25, SEQ_LEN // 30).astype(jnp.float32)


def steps_of(stream_key, extent, pieces, least, high):
    level, own = 1.0, jax.random.fold_in(stream_key, 6)
    for axis_at, blocks in pieces:
        heights = jnp.exp(jax.random.uniform(jax.random.fold_in(own, axis_at), (blocks,), jnp.float32, least / len(pieces), high / len(pieces)))
        level = level * jnp.repeat(heights, extent[axis_at] // blocks).reshape([-1 if axis == axis_at else 1 for axis in range(len(extent))])
    return level


def scatter_about(stream_key, dims, scale, reach, pieces=(), kind=jnp.bfloat16):
    array = jax.random.normal(stream_key, dims, jnp.float32) * scale
    if len(pieces) > 0:
        array = steps_of(stream_key, dims, pieces, -0.22, 0.18) * array
    return jnp.clip(array, min=-reach, max=reach).astype(kind)


def setup_inputs(seed: int = 0) -> dict:
    key_list = jax.random.split(jax.random.key(seed), 7)
    return {
        "proj": scatter_about(key_list[0], (3, CH, SEQ_LEN), 1.0, 6.0, ((1, 4), (2, 8))),
        "cotangent": scatter_about(key_list[1], (CH, SEQ_LEN), 1.0, 6.0, ((0, 4), (1, 8))),
        "short_w": scatter_about(key_list[2], (3, CH, TAPS), TAPS ** -0.5, 3.5, ((1, 4),), jnp.float32),
        "filter_in": scatter_about(key_list[3], (FEAT, ORDER), 1.0, 5.0, (), jnp.float32),
        "filter_out": scatter_about(key_list[4], (ORDER, CH), ORDER ** -0.5, 0.75, ((1, 4),), jnp.float32),
        "rates": draw_rates(jax.random.fold_in(key_list[6], 71), 0),
    }


PRECISE = lax.Precision.HIGHEST

def position_features(positions, length, feature_count):
    feature_index = jnp.arange(feature_count, dtype=jnp.int32)
    multiplier = (1 + feature_index // 2 * 499) % length
    upper = positions // 1024
    lower = positions % 1024
    phases = (upper[:, None] * (multiplier * 1024 % length)[None, :] + lower[:, None] * multiplier[None, :]) % length
    angles = phases.astype(jnp.float32) * (2.0 * math.pi / length)
    return jnp.where((feature_index % 2 == 0)[None, :], jnp.cos(angles), jnp.sin(angles))

def reference(proj, cotangent, short_w, filter_in, filter_out, rates):
    length = SEQ_LEN
    tap_count = TAPS
    norm_scale = 1.0 / math.sqrt(length)
    positions = jnp.arange(length, dtype=jnp.int32)
    features = position_features(positions, length, FEAT)
    preact = jnp.dot(features, filter_in, precision=PRECISE, preferred_element_type=jnp.float32)
    hidden = jnp.sin(preact)
    relative = positions.astype(jnp.float32) / length
    block = min(CH, 32)
    blocks = CH // block
    proj_blocks = proj.reshape(3, blocks, block, length).transpose(1, 0, 2, 3)
    cot_blocks = cotangent.reshape(blocks, block, length)
    short_blocks = short_w.reshape(3, blocks, block, tap_count).transpose(1, 0, 2, 3)
    out_blocks = filter_out.reshape(ORDER, blocks, block).transpose(1, 0, 2)
    rate_blocks = rates.reshape(blocks, block)

    def one_block(items):
        proj_part, cot_part, short_part, out_part, rate_part = items
        padded = jnp.pad(proj_part.astype(jnp.float32), ((0, 0), (0, 0), (tap_count - 1, 0)))

        def delayed(offset):
            return padded[:, :, tap_count - 1 - offset:tap_count - 1 - offset + length]
        mixed_all = short_part[:, :, 0, None] * delayed(0)
        for offset in range(1, tap_count):
            mixed_all = mixed_all + short_part[:, :, offset, None] * delayed(offset)
        query_part, key_part, value_part = (mixed_all[0], mixed_all[1], mixed_all[2])
        gated_prod = key_part * value_part
        modulated = jnp.einsum('to,oc->ct', hidden, out_part, precision=PRECISE)
        spread = jnp.sqrt(jnp.expm1(-2.0 * rate_part) / jnp.expm1(-2.0 * rate_part / length))
        envelope = jnp.exp(-rate_part[:, None] * relative[None, :]) / spread[:, None]
        kernel = envelope * modulated
        cotangent_full = cot_part.astype(jnp.float32)
        grad_conv = cotangent_full * query_part
        points = 2 * length
        gated_spec = jnp.fft.rfft(gated_prod, n=points, axis=-1)
        kernel_spec = jnp.fft.rfft(kernel, n=points, axis=-1)
        grad_spec = jnp.fft.rfft(grad_conv, n=points, axis=-1)
        conv_out = jnp.fft.irfft(gated_spec * kernel_spec, n=points, axis=-1)[:, :length].astype(jnp.float32)
        grad_gated = jnp.fft.irfft(grad_spec * jnp.conj(kernel_spec), n=points, axis=-1)[:, :length].astype(jnp.float32)
        grad_kernel = jnp.fft.irfft(grad_spec * jnp.conj(gated_spec), n=points, axis=-1)[:, :length].astype(jnp.float32)
        grad_mixed = jnp.stack([cotangent_full * conv_out, grad_gated * value_part, grad_gated * key_part])
        tail_padded = jnp.pad(grad_mixed, ((0, 0), (0, 0), (0, tap_count - 1)))
        result = short_part[:, :, 0, None] * tail_padded[:, :, 0:length]
        for offset in range(1, tap_count):
            result = result + short_part[:, :, offset, None] * tail_padded[:, :, offset:offset + length]
        grad_proj = result.astype(jnp.bfloat16)
        grad_short = jnp.stack([lax.optimization_barrier(jnp.sum(grad_mixed * delayed(offset), axis=2)) for offset in range(tap_count)], axis=2) * norm_scale
        weighted = envelope * grad_kernel
        grad_out = jnp.einsum('to,ct->oc', hidden, weighted, precision=PRECISE) * norm_scale
        grad_hidden = jnp.einsum('ct,oc->to', weighted, out_part, precision=PRECISE)
        grad_in = jnp.einsum('tf,to->fo', features, grad_hidden * jnp.cos(preact), precision=PRECISE)
        return (grad_proj, grad_short, grad_out, grad_in)
    results = lax.map(one_block, (proj_blocks, cot_blocks, short_blocks, out_blocks, rate_blocks))
    grad_proj = results[0].transpose(1, 0, 2, 3).reshape(3, CH, length)
    grad_short = results[1].transpose(1, 0, 2, 3).reshape(3, CH, tap_count)
    grad_filter_out = results[2].transpose(1, 0, 2).reshape(ORDER, CH)
    grad_filter_in = lax.optimization_barrier(jnp.sum(results[3], axis=0)) * norm_scale
    return (grad_proj, grad_short, grad_filter_out, grad_filter_in)
```

```python
import functools
import math

import jax
import jax.numpy as jnp
import ml_dtypes
import numpy as np
from jax import lax
from jax.experimental import pallas as pl
from jax.experimental.pallas import tpu as pltpu
from jax.sharding import PartitionSpec as P

F32 = jnp.float32
BF16 = jnp.bfloat16
LANES = 128
VMEM_BYTES = 56 * 1024 * 1024


def split(value):
    high = value.astype(BF16)
    return high, (value - high.astype(F32)).astype(BF16)


def split_outside(value):
    high = lax.reduce_precision(value, 8, 7)
    return high.astype(BF16), (value - high).astype(BF16)


def np_split(value):
    high = value.astype(ml_dtypes.bfloat16)
    return high, (value - high.astype(np.float64)).astype(ml_dtypes.bfloat16)


def dot(left, right):
    return jnp.dot(left, right, preferred_element_type=F32)


def dot_last(left, right):
    return lax.dot_general(left, right, (((1,), (1,)), ((), ())), preferred_element_type=F32)


@functools.lru_cache(maxsize=None)
def transform_tables(length):
    rows = length // LANES
    points = 2 * length
    lows = rows + 8
    low = np.arange(lows)
    row = np.arange(rows)
    lane = np.arange(LANES)
    angle = 2.0 * np.pi * ((low[:, None] * row[None, :]) % (2 * rows)) / (2 * rows)
    kept = (low <= rows)[:, None]
    first = np.concatenate([np.cos(angle) * kept, -np.sin(angle) * kept], 0)
    weight = np.where((low == 0) | (low == rows), 1.0, 2.0)[:, None] / points
    last = np.concatenate([np.cos(angle) * kept * weight, -np.sin(angle) * kept * weight], 0).T
    turn = 2.0 * np.pi * ((low[:, None] * lane[None, :]) % points) / points
    lane_angle = 2.0 * np.pi * ((lane[:, None] * lane[None, :]) % LANES) / LANES
    cosine, sine = np.cos(lane_angle), np.sin(lane_angle)
    middle = np.block([[cosine, -sine], [sine, cosine]])
    first_high, first_low = np_split(first)
    last_high, last_low = np_split(last)
    middle_high, middle_low = np_split(middle)
    return dict(
        first=np.concatenate([first_high, first_high, first_low], 1),
        last=np.concatenate([last_high, last_high, last_low], 1),
        middle=np.concatenate([middle_high, middle_low], 0),
        turn=np.concatenate([np.cos(turn), np.sin(turn)], 0).astype(np.float32),
    )


@functools.lru_cache(maxsize=None)
def feature_tables(length, feature_count):
    rows = length // LANES
    feature = np.arange(feature_count)
    multiplier = (1 + feature // 2 * 499) % length
    row_angle = 2.0 * np.pi * ((multiplier[:, None] * LANES * np.arange(rows)[None, :]) % length) / length
    lane_angle = 2.0 * np.pi * ((multiplier[:, None] * np.arange(LANES)[None, :]) % length) / length
    even = (feature % 2 == 0)[:, None]
    near = np.where(even, np.cos(row_angle), np.sin(row_angle))
    far = np.where(even, -np.sin(row_angle), np.cos(row_angle))
    return (
        np.concatenate([near, far], 0).astype(np.float32),
        np.concatenate([np.cos(lane_angle), np.sin(lane_angle)], 0).astype(np.float32),
    )


def middle_dot(value, middle_ref):
    high, low = split(value)
    size = 2 * LANES
    table_high, table_low = middle_ref[:size, :], middle_ref[size:, :]
    return dot(high, table_high) + dot(high, table_low) + dot(low, table_high)


def forward(signals, first_ref, middle_ref, turn_ref):
    lows = turn_ref.shape[0] // 2
    high, low = split(jnp.concatenate(signals, 1))
    partial = dot(first_ref[...], jnp.concatenate([high, low, high], 0))
    cosine, sine = turn_ref[:lows, :], turn_ref[lows:, :]
    turned = []
    for index in range(len(signals)):
        real = partial[:lows, index * LANES : (index + 1) * LANES]
        imag = partial[lows:, index * LANES : (index + 1) * LANES]
        turned.append(
            jnp.concatenate([real * cosine + imag * sine, imag * cosine - real * sine], 1)
        )
    return middle_dot(jnp.concatenate(turned, 0), middle_ref)


def backward(spectra, last_ref, middle_ref, turn_ref):
    lows = turn_ref.shape[0] // 2
    swapped = jnp.concatenate([jnp.concatenate([imag, real], 1) for real, imag in spectra], 0)
    partial = middle_dot(swapped, middle_ref)
    cosine, sine = turn_ref[:lows, :], turn_ref[lows:, :]
    turned = []
    for index in range(len(spectra)):
        imag = partial[index * lows : (index + 1) * lows, :LANES]
        real = partial[index * lows : (index + 1) * lows, LANES:]
        turned.append(
            jnp.concatenate([real * cosine - imag * sine, imag * cosine + real * sine], 0)
        )
    high, low = split(jnp.concatenate(turned, 1))
    result = dot(last_ref[...], jnp.concatenate([high, low, high], 0))
    return [result[:, index * LANES : (index + 1) * LANES] for index in range(len(spectra))]


def later(value):
    turned = pltpu.roll(value, 1, 1)
    carried = pltpu.roll(turned, 1, 0)
    row = lax.broadcasted_iota(jnp.int32, value.shape, 0)
    lane = lax.broadcasted_iota(jnp.int32, value.shape, 1)
    carried = jnp.where(row == 0, 0.0, carried)
    return jnp.where(lane == 0, carried, turned)


def sooner(value):
    rows = value.shape[0]
    turned = pltpu.roll(value, LANES - 1, 1)
    carried = pltpu.roll(turned, rows - 1, 0)
    row = lax.broadcasted_iota(jnp.int32, value.shape, 0)
    lane = lax.broadcasted_iota(jnp.int32, value.shape, 1)
    carried = jnp.where(row == rows - 1, 0.0, carried)
    return jnp.where(lane == LANES - 1, carried, turned)


def sine_cosine(angle):
    turns = jnp.round(angle * (1.0 / math.pi))
    rest = angle - turns * 3.140625
    rest = rest - turns * 9.67502593994140625e-4
    rest = rest - turns * 1.509957990978376432e-7
    half = turns * 0.5
    sign = 1.0 - 4.0 * jnp.abs(half - jnp.round(half))
    square = rest * rest
    sine = -1.0 / 39916800.0
    for coefficient in (1.0 / 362880.0, -1.0 / 5040.0, 1.0 / 120.0, -1.0 / 6.0, 1.0):
        sine = sine * square + coefficient
    cosine = 1.0 / 479001600.0
    for coefficient in (-1.0 / 3628800.0, 1.0 / 40320.0, -1.0 / 720.0, 1.0 / 24.0, -0.5, 1.0):
        cosine = cosine * square + coefficient
    return sine * (rest * sign), cosine * sign


def pack_kernel(per, proj_ref, cot_ref, out_ref):
    channels = cot_ref.shape[0]
    whole = [proj_ref[index].astype(F32) for index in range(3)] + [cot_ref[...].astype(F32)]
    for device in range(out_ref.shape[0]):
        start = device * per % channels
        rows = jnp.concatenate([part[start : start + per, :] for part in whole], 0)
        out_ref[device] = rows.astype(BF16)


def block_features(near_ref, lane_ref):
    count = lane_ref.shape[0] // 2
    lane_cos, lane_sin = lane_ref[:count, :], lane_ref[count:, :]
    near, far = near_ref[0, :count, :], near_ref[0, count:, :]
    rows = range(near_ref.shape[2])
    blocks = [near[:, row : row + 1] * lane_cos + far[:, row : row + 1] * lane_sin for row in rows]
    return split(jnp.concatenate(blocks, 1))


def hidden_kernel(
    near_ref, lane_ref, in_ref, out_ref, sine_high_ref, sine_low_ref, cosine_ref, mod_ref
):
    high, low = block_features(near_ref, lane_ref)
    preact = dot(in_ref[...], jnp.concatenate([high, low, high], 0))
    sine, cosine = sine_cosine(preact)
    cosine_ref[...] = cosine
    high, low = split(sine)
    sine_high_ref[...] = high
    sine_low_ref[...] = low
    mod_ref[...] = dot(out_ref[...], jnp.concatenate([high, low, high], 0))


def filter_kernel(
    per, length, rates_ref, scale_ref, mod_ref, first_ref, middle_ref, turn_ref, env_ref, spec_ref, stage_ref
):
    rows = length // LANES
    for row in range(rows):
        stage_ref[row * 8 : (row + 1) * 8, :] = mod_ref[:, row * LANES : (row + 1) * LANES]
    position = lax.broadcasted_iota(jnp.int32, (rows, LANES), 0) * LANES
    position = position + lax.broadcasted_iota(jnp.int32, (rows, LANES), 1)
    relative = position.astype(F32) * (1.0 / length)
    kernels = []
    for channel in range(per):
        envelope = jnp.exp(-rates_ref[channel] * relative) * scale_ref[channel]
        env_ref[channel * rows : (channel + 1) * rows, :] = envelope
        kernels.append(envelope * stage_ref[pl.ds(channel, rows, stride=8), :])
    spec_ref[...] = forward(kernels, first_ref, middle_ref, turn_ref)


def spectra_kernel(
    per,
    short_ref,
    recv_ref,
    env_ref,
    first_ref,
    last_ref,
    middle_ref,
    turn_ref,
    raw_ref,
    mixed_ref,
    spec_ref,
    weighted_ref,
    stage_ref,
):
    devices, held, tokens = recv_ref.shape
    step = raw_ref.shape[0] // (devices * tokens // LANES)
    rows = devices * tokens // LANES
    lows = turn_ref.shape[0] // 2
    for device in range(devices):
        for part in range(tokens // LANES):
            at = (device * (tokens // LANES) + part) * step
            raw_ref[at : at + held, :] = recv_ref[
                device, :, part * LANES : (part + 1) * LANES
            ].astype(F32)
    gated, grads = [], []
    for channel in range(per):
        mixed = []
        for index in range(3):
            base = raw_ref[pl.ds(index * per + channel, rows, stride=step), :]
            total = short_ref[(index * per + channel) * 3] * base
            for tap in (1, 2):
                base = later(base)
                total = total + short_ref[(index * per + channel) * 3 + tap] * base
            mixed.append(total)
        cotangent = raw_ref[pl.ds(3 * per + channel, rows, stride=step), :]
        mixed_ref[2 * channel] = mixed[1]
        mixed_ref[2 * channel + 1] = mixed[2]
        gated.append(mixed[1] * mixed[2])
        grads.append(cotangent * mixed[0])
    spectra = forward(gated + grads, first_ref, middle_ref, turn_ref)
    spec_ref[...] = spectra
    products = []
    for channel in range(per):
        at, other = channel * lows, (per + channel) * lows
        gated_real, gated_imag = spectra[at : at + lows, :LANES], spectra[at : at + lows, LANES:]
        grad_real, grad_imag = (
            spectra[other : other + lows, :LANES],
            spectra[other : other + lows, LANES:],
        )
        products.append(
            (
                grad_real * gated_real + grad_imag * gated_imag,
                grad_imag * gated_real - grad_real * gated_imag,
            )
        )
    results = backward(products, last_ref, middle_ref, turn_ref)
    if per < 8:
        stage_ref[...] = jnp.zeros_like(stage_ref)
    for channel in range(per):
        weighted = results[channel] * env_ref[channel * rows : (channel + 1) * rows, :]
        stage_ref[pl.ds(channel, rows, stride=8), :] = weighted
    for row in range(rows):
        weighted_ref[:, row * LANES : (row + 1) * LANES] = stage_ref[row * 8 : (row + 1) * 8, :]


def filter_grad_kernel(
    weighted_ref,
    sine_high_ref,
    sine_low_ref,
    cosine_ref,
    near_ref,
    lane_ref,
    fo_ref,
    out_grad_ref,
    in_grad_ref,
):
    count = lane_ref.shape[0] // 2
    feature_high, feature_low = block_features(near_ref, lane_ref)
    high, low = split(weighted_ref[...])
    both = jnp.concatenate([weighted_ref[...], weighted_ref[...] - high.astype(F32)], 0).astype(BF16)
    first = dot_last(both, sine_high_ref[...])
    out_grad = first[:8] + first[8:] + dot_last(high, sine_low_ref[...])
    grad = dot(fo_ref[...], jnp.concatenate([both.astype(F32), high.astype(F32)], 0).astype(BF16))
    grad_high, grad_low = split(grad * cosine_ref[...])
    second = dot_last(jnp.concatenate([feature_high, feature_low], 0), grad_high)
    in_grad = second[:count] + second[count:] + dot_last(feature_high, grad_low)

    @pl.when(pl.program_id(0) == 0)
    def _():
        out_grad_ref[...] = jnp.zeros_like(out_grad_ref)
        in_grad_ref[...] = jnp.zeros_like(in_grad_ref)

    out_grad_ref[...] += out_grad
    in_grad_ref[...] += in_grad


def proj_grad_kernel(
    per,
    scale,
    short_ref,
    raw_ref,
    mixed_ref,
    spec_ref,
    kernel_spec_ref,
    out_grad_ref,
    last_ref,
    middle_ref,
    turn_ref,
    slab_ref,
    stage_ref,
):
    devices, held, width = slab_ref.shape
    tokens = width - 3 * LANES
    rows = devices * tokens // LANES
    step = raw_ref.shape[0] // rows
    lows = turn_ref.shape[0] // 2
    products = []
    for sign in (1.0, -1.0):
        for channel in range(per):
            at = (channel if sign > 0 else per + channel) * lows
            real, imag = spec_ref[at : at + lows, :LANES], spec_ref[at : at + lows, LANES:]
            at = channel * lows
            kernel_real = kernel_spec_ref[at : at + lows, :LANES]
            kernel_imag = sign * kernel_spec_ref[at : at + lows, LANES:]
            products.append(
                (
                    real * kernel_real - imag * kernel_imag,
                    real * kernel_imag + imag * kernel_real,
                )
            )
    results = backward(products, last_ref, middle_ref, turn_ref)
    sums = [None] * (3 * per)
    for channel in range(per):
        cotangent = raw_ref[pl.ds(3 * per + channel, rows, stride=step), :]
        grad_mixed = (
            cotangent * results[channel],
            results[per + channel] * mixed_ref[2 * channel + 1],
            results[per + channel] * mixed_ref[2 * channel],
        )
        for index in range(3):
            base = raw_ref[pl.ds(index * per + channel, rows, stride=step), :]
            grad = grad_mixed[index]
            total = short_ref[(index * per + channel) * 3] * grad
            taps = [jnp.sum(grad * base, axis=0, keepdims=True)]
            moved = grad
            for tap in (1, 2):
                base = later(base)
                moved = sooner(moved)
                total = total + short_ref[(index * per + channel) * 3 + tap] * moved
                taps.append(jnp.sum(grad * base, axis=0, keepdims=True))
            sums[index * per + channel] = jnp.concatenate(taps, 0)
            stage_ref[pl.ds(index * per + channel, rows, stride=held), :] = total
    for device in range(devices):
        for part in range(tokens // LANES):
            at = (device * (tokens // LANES) + part) * held
            slab_ref[device, :, part * LANES : (part + 1) * LANES] = stage_ref[
                at : at + held, :
            ].astype(BF16)
    row = lax.broadcasted_iota(jnp.int32, (held, LANES), 0)
    lane = lax.broadcasted_iota(jnp.int32, (held, LANES), 1)
    small = jnp.zeros((held, LANES), F32)
    for place in range(3 * per):
        taps = jnp.sum(sums[place], axis=1, keepdims=True) * scale
        for tap in range(3):
            small = jnp.where((row == 4 + place) & (lane == tap), taps[tap : tap + 1, :], small)
    order = out_grad_ref.shape[1]
    out_grad = jnp.concatenate(
        [out_grad_ref[...] * scale, jnp.zeros((8, LANES - order), F32)], 1
    )
    out_grad = jnp.concatenate([out_grad, jnp.zeros((held - 8, LANES), F32)], 0)
    small = jnp.where(row < per, out_grad, small)
    rest = pltpu.roll(small - small.astype(BF16).astype(F32), LANES // 2, 1)
    small = jnp.where(lane < LANES // 2, small, rest).astype(BF16)
    for device in range(devices):
        slab_ref[device, :, tokens : tokens + LANES] = small


def unpack_kernel(per, recv_ref, proj_ref, short_ref, out_ref, in_ref):
    channels, tokens = proj_ref.shape[1:]
    devices = channels // per
    order = out_ref.shape[0]
    for index in range(3):
        rows = [
            recv_ref[device, index * per : (index + 1) * per, :tokens].astype(F32)
            for device in range(devices)
        ]
        proj_ref[index] = jnp.concatenate(rows, 0).astype(BF16)
    small = [recv_ref[device, :, tokens : tokens + LANES].astype(F32) for device in range(devices)]
    small = [part + pltpu.roll(part, LANES // 2, 1) for part in small]
    for index in range(3):
        at = 4 + index * per
        short_ref[index] = jnp.concatenate([part[at : at + per, :3] for part in small], 0)
    out_grad = jnp.concatenate([part[:per, :] for part in small], 0)
    out_ref[...] = out_grad.T[:order, :]
    extra = [
        recv_ref[device, :, tokens + LANES :].astype(F32) for device in range(devices)
    ]
    total = functools.reduce(lambda a, b: a + b, extra)
    total = jnp.concatenate([total[:, :LANES], total[:, LANES:]], 0)
    in_ref[...] = total[:, :order] + total[:, order:]


def call(kernel, out, grid=None, in_specs=None, out_specs=None, scratch=(), flops=0, moved=0):
    vmem = pl.BlockSpec(memory_space=pltpu.VMEM)
    extra = {}
    if grid is not None:
        extra = dict(grid=grid)
    return pl.pallas_call(
        kernel,
        out_shape=out,
        in_specs=in_specs,
        out_specs=out_specs if out_specs is not None else jax.tree.map(lambda _: vmem, out),
        scratch_shapes=scratch,
        compiler_params=pltpu.CompilerParams(vmem_limit_bytes=VMEM_BYTES),
        cost_estimate=pl.CostEstimate(flops=flops, bytes_accessed=moved, transcendentals=0),
        **extra,
    )


def shards(proj, cotangent, short_w, filter_in, filter_out, rates):
    sds = jax.ShapeDtypeStruct
    smem = pl.BlockSpec(memory_space=pltpu.SMEM)
    vmem = pl.BlockSpec(memory_space=pltpu.VMEM)
    channels, tokens = cotangent.shape
    devices = lax.axis_size("seq")
    groups = lax.axis_size("ch")
    length = devices * tokens
    rows = length // LANES
    lows = rows + 8
    features, order = filter_in.shape
    scale = 1.0 / math.sqrt(length)
    per = max(1, channels // devices)
    held = 4 * per
    step = max(8, held)
    start = lax.axis_index("seq") * per % channels

    tables = {name: jnp.asarray(value) for name, value in transform_tables(length).items()}
    first, last = tables["first"], tables["last"]
    middle, turn = tables["middle"], tables["turn"]

    packed = call(
        functools.partial(pack_kernel, per),
        sds((devices, held, tokens), BF16),
        in_specs=[vmem, vmem],
    )(proj, cotangent)
    recv = lax.all_to_all(packed, "seq", split_axis=0, concat_axis=0, tiled=True)

    own_short = lax.dynamic_slice_in_dim(short_w, start, per, 1).reshape(-1)
    own_rates = lax.dynamic_slice_in_dim(rates, start, per, 0)
    own_out = lax.dynamic_slice_in_dim(filter_out, start, per, 1)
    own_scale = 1.0 / jnp.sqrt(
        jnp.expm1(-2.0 * own_rates) / jnp.expm1(-2.0 * own_rates / length)
    )
    near, lane_table = feature_tables(length, features)
    block_rows = min(rows, 64)
    blocks = rows // block_rows
    block = block_rows * LANES
    near = near.reshape(2 * features, blocks, block_rows).transpose(1, 0, 2)
    in_high, in_low = split_outside(filter_in.T)
    out_high, out_low = split_outside(jnp.pad(own_out.T, ((0, 8 - per), (0, 0))))
    at_block = lambda height: pl.BlockSpec((height, block), lambda i: (0, i))
    fixed = lambda shape: pl.BlockSpec(shape, lambda i: (0,) * len(shape))
    near_block = pl.BlockSpec((1, 2 * features, block_rows), lambda i: (i, 0, 0))
    near, lane_table = jnp.asarray(near), jnp.asarray(lane_table)
    sine_high, sine_low, cosine, modulated = call(
        hidden_kernel,
        (
            sds((order, length), BF16),
            sds((order, length), BF16),
            sds((order, length), F32),
            sds((8, length), F32),
        ),
        grid=(blocks,),
        in_specs=[
            near_block,
            fixed((2 * features, LANES)),
            fixed((order, 3 * features)),
            fixed((8, 3 * order)),
        ],
        out_specs=(
            at_block(order),
            at_block(order),
            at_block(order),
            at_block(8),
        ),
        flops=8 * length * order * 3 * features,
        moved=length * order * 8,
    )(
        near,
        lane_table,
        jnp.concatenate([in_high, in_high, in_low], 1),
        jnp.concatenate([out_high, out_high, out_low], 1),
    )
    envelope, kernel_spec = call(
        functools.partial(filter_kernel, per, length),
        (sds((per * rows, LANES), F32), sds((per * lows, 2 * LANES), F32)),
        in_specs=[smem, smem] + [vmem] * 4,
        scratch=[pltpu.VMEM((rows * 8, LANES), F32)],
        flops=200 * length * LANES,
    )(own_rates, own_scale, modulated, first, middle, turn)

    raw, mixed, spec, weighted = call(
        functools.partial(spectra_kernel, per),
        (
            sds((rows * step, LANES), F32),
            sds((2 * per, rows, LANES), F32),
            sds((2 * per * lows, 2 * LANES), F32),
            sds((8, length), F32),
        ),
        in_specs=[smem] + [vmem] * 6,
        scratch=[pltpu.VMEM((rows * 8, LANES), F32)],
        flops=400 * length * LANES,
    )(own_short, recv, envelope, first, last, middle, turn)

    fo_high, fo_low = split_outside(jnp.pad(own_out, ((0, 0), (0, 8 - per))))
    out_grad, in_grad = call(
        filter_grad_kernel,
        (sds((8, order), F32), sds((features, order), F32)),
        grid=(blocks,),
        in_specs=[
            at_block(8),
            at_block(order),
            at_block(order),
            at_block(order),
            near_block,
            fixed((2 * features, LANES)),
            fixed((order, 24)),
        ],
        out_specs=(fixed((8, order)), fixed((features, order))),
        flops=200 * length * LANES,
    )(
        weighted,
        sine_high,
        sine_low,
        cosine,
        near,
        lane_table,
        jnp.concatenate([fo_high, fo_high, fo_low], 1),
    )

    others = [
        lax.ppermute(in_grad, "ch", [(i, (i + by) % groups) for i in range(groups)])
        for by in range(1, groups)
    ]
    slab_rows = max(16, held)
    slab = call(
        functools.partial(proj_grad_kernel, per, scale),
        sds((devices, slab_rows, tokens + 3 * LANES), BF16),
        in_specs=[smem] + [vmem] * 8,
        scratch=[pltpu.VMEM((rows * slab_rows, LANES), F32)],
        flops=400 * length * LANES,
    )(own_short, raw, mixed, spec, kernel_spec, out_grad, last, middle, turn)
    in_high, in_low = split_outside(functools.reduce(lambda a, b: a + b, others, in_grad) * scale)
    halves = jnp.concatenate([in_high, in_low], 1)
    halves = halves.reshape(2, features // 2, 2 * order).transpose(1, 0, 2)
    halves = halves.reshape(1, features // 2, 4 * order)
    halves = jnp.broadcast_to(halves, (devices,) + halves.shape[1:])
    slab = lax.dynamic_update_slice(slab, halves, (0, 0, tokens + LANES))

    back = lax.all_to_all(slab, "seq", split_axis=0, concat_axis=0, tiled=True)
    return call(
        functools.partial(unpack_kernel, per),
        (
            sds((3, channels, tokens), BF16),
            sds((3, channels, 3), F32),
            sds((order, channels), F32),
            sds((features, order), F32),
        ),
        in_specs=[vmem],
    )(back)


def solution(mesh):
    placed = (
        P(None, "ch", "seq"),
        P("ch", "seq"),
        P(None, "ch", None),
        P(),
        P(None, "ch"),
        P("ch"),
    )
    return jax.shard_map(
        shards,
        mesh=mesh,
        in_specs=placed,
        out_specs=(P(None, "ch", "seq"), P(None, "ch", None), P(None, "ch"), P()),
        check_vma=False,
    )
```

```python
import functools
import math

import jax
import jax.numpy as jnp
import ml_dtypes
import numpy as np
from jax import lax
from jax.experimental import pallas as pl
from jax.experimental.pallas import tpu as pltpu
from jax.sharding import PartitionSpec as P

F32 = jnp.float32
BF16 = jnp.bfloat16
LANES = 128
MIB = 1024 * 1024


def split(value):
    high = value.astype(BF16)
    return high, (value - high.astype(F32)).astype(BF16)


def np_split(value):
    high = value.astype(ml_dtypes.bfloat16)
    return high, (value - high.astype(np.float64)).astype(ml_dtypes.bfloat16)


def dot(left, right):
    return jnp.dot(left, right, preferred_element_type=F32)


def dot_first(left, right):
    return lax.dot_general(left, right, (((0,), (0,)), ((), ())), preferred_element_type=F32)


def dot_last(left, right):
    return lax.dot_general(left, right, (((1,), (1,)), ((), ())), preferred_element_type=F32)


@functools.lru_cache(maxsize=None)
def transform_tables(length):
    rows = length // LANES
    points = 2 * length
    lows = rows + 8
    low = np.arange(lows)
    row = np.arange(rows)
    lane = np.arange(LANES)
    angle = 2.0 * np.pi * ((low[:, None] * row[None, :]) % (2 * rows)) / (2 * rows)
    kept = (low <= rows)[:, None]
    first = np.concatenate([np.cos(angle) * kept, -np.sin(angle) * kept], 0)
    weight = np.where((low == 0) | (low == rows), 1.0, 2.0)[:, None] / points
    last = np.concatenate([np.cos(angle) * kept * weight, -np.sin(angle) * kept * weight], 0).T
    turn = 2.0 * np.pi * ((low[:, None] * lane[None, :]) % points) / points
    lane_angle = 2.0 * np.pi * ((lane[:, None] * lane[None, :]) % LANES) / LANES
    cosine, sine = np.cos(lane_angle), np.sin(lane_angle)
    middle = np.block([[cosine, -sine], [sine, cosine]])
    first_high, first_low = np_split(first)
    last_high, last_low = np_split(last)
    middle_high, middle_low = np_split(middle)
    return dict(
        first=np.concatenate([first_high, first_high, first_low], 1),
        last=np.concatenate([last_high, last_high, last_low], 1),
        middle=np.concatenate([middle_high, middle_low], 0),
        turn=np.concatenate([np.cos(turn), np.sin(turn)], 0).astype(np.float32),
    )


@functools.lru_cache(maxsize=None)
def feature_tables(length, feature_count):
    rows = length // LANES
    feature = np.arange(feature_count)
    multiplier = (1 + feature // 2 * 499) % length
    row_angle = 2.0 * np.pi * ((multiplier[:, None] * LANES * np.arange(rows)[None, :]) % length) / length
    lane_angle = 2.0 * np.pi * ((multiplier[:, None] * np.arange(LANES)[None, :]) % length) / length
    even = (feature % 2 == 0)[:, None]
    near = np.where(even, np.cos(row_angle), np.sin(row_angle))
    far = np.where(even, -np.sin(row_angle), np.cos(row_angle))
    return (
        np.concatenate([near, far], 0).astype(np.float32),
        np.concatenate([np.cos(lane_angle), np.sin(lane_angle)], 0).astype(np.float32),
    )


def middle_dot(value, middle_ref):
    high, low = split(value)
    size = 2 * LANES
    table_high, table_low = middle_ref[:size, :], middle_ref[size:, :]
    return dot(high, table_high) + dot(high, table_low) + dot(low, table_high)


def forward(signals, first_ref, middle_ref, turn_ref):
    lows = turn_ref.shape[0] // 2
    high, low = split(jnp.concatenate(signals, 1))
    partial = dot(first_ref[...], jnp.concatenate([high, low, high], 0))
    cosine, sine = turn_ref[:lows, :], turn_ref[lows:, :]
    turned = []
    for index in range(len(signals)):
        real = partial[:lows, index * LANES : (index + 1) * LANES]
        imag = partial[lows:, index * LANES : (index + 1) * LANES]
        turned.append(
            jnp.concatenate([real * cosine + imag * sine, imag * cosine - real * sine], 1)
        )
    return middle_dot(jnp.concatenate(turned, 0), middle_ref)


def backward(spectra, last_ref, middle_ref, turn_ref):
    lows = turn_ref.shape[0] // 2
    swapped = jnp.concatenate([jnp.concatenate([imag, real], 1) for real, imag in spectra], 0)
    partial = middle_dot(swapped, middle_ref)
    cosine, sine = turn_ref[:lows, :], turn_ref[lows:, :]
    turned = []
    for index in range(len(spectra)):
        imag = partial[index * lows : (index + 1) * lows, :LANES]
        real = partial[index * lows : (index + 1) * lows, LANES:]
        turned.append(
            jnp.concatenate([real * cosine - imag * sine, imag * cosine + real * sine], 0)
        )
    high, low = split(jnp.concatenate(turned, 1))
    result = dot(last_ref[...], jnp.concatenate([high, low, high], 0))
    return [result[:, index * LANES : (index + 1) * LANES] for index in range(len(spectra))]


def later(value):
    turned = pltpu.roll(value, 1, 1)
    carried = pltpu.roll(turned, 1, 0)
    row = lax.broadcasted_iota(jnp.int32, value.shape, 0)
    lane = lax.broadcasted_iota(jnp.int32, value.shape, 1)
    carried = jnp.where(row == 0, 0.0, carried)
    return jnp.where(lane == 0, carried, turned)


def sooner(value):
    rows = value.shape[0]
    turned = pltpu.roll(value, LANES - 1, 1)
    carried = pltpu.roll(turned, rows - 1, 0)
    row = lax.broadcasted_iota(jnp.int32, value.shape, 0)
    lane = lax.broadcasted_iota(jnp.int32, value.shape, 1)
    carried = jnp.where(row == rows - 1, 0.0, carried)
    return jnp.where(lane == LANES - 1, carried, turned)


def sine_cosine(half_angle):
    turns = jnp.round(half_angle * (1.0 / math.pi))
    rest = half_angle - turns * 3.140625
    rest = rest - turns * 9.67653589793e-4
    square = rest * rest
    sine = 2.59045638e-06
    for coefficient in (-1.98008819e-04, 8.33289957e-03, -1.66666476e-01, 9.99999977e-01):
        sine = sine * square + coefficient
    cosine = 2.31536124e-05
    for coefficient in (-1.38536905e-03, 4.16635829e-02, -4.99999053e-01, 9.99999953e-01):
        cosine = cosine * square + coefficient
    sine = sine * rest
    twice = sine + sine
    return twice * cosine, 1.0 - twice * sine


def first_channel(per, channels):
    return lax.axis_index("seq") * per % channels


def own_rows(per, out_ref):
    channels = out_ref.shape[0]
    start = first_channel(per, channels)
    return pltpu.roll(out_ref[...], lax.rem(channels - start, channels), 0)[:8, :]


def tap_rows(short_ref):
    return jnp.concatenate([short_ref[index] for index in range(3)], 0)


def own_columns(per, value):
    channels = value.shape[1]
    start = first_channel(per, channels)
    turned = pltpu.roll(value, lax.rem(channels - start, channels), 1)
    return [turned[:, channel : channel + 1] for channel in range(per)]


def small_expm1(value):
    total = 1.0
    for divisor in (7.0, 6.0, 5.0, 4.0, 3.0, 2.0):
        total = 1.0 + total * value * (1.0 / divisor)
    return total * value


def pack_kernel(per, proj_ref, cot_ref, out_ref):
    channels = cot_ref.shape[0]
    whole = [proj_ref[index].astype(F32) for index in range(3)] + [cot_ref[...].astype(F32)]
    for device in range(out_ref.shape[0]):
        start = device * per % channels
        rows = jnp.concatenate([part[start : start + per, :] for part in whole], 0)
        out_ref[device] = rows.astype(BF16)


def block_features(table, lane_ref):
    count = lane_ref.shape[0] // 2
    lane_cos, lane_sin = lane_ref[:count, :], lane_ref[count:, :]
    near, far = table[:count, :], table[count:, :]
    rows = range(table.shape[1])
    blocks = [near[:, row : row + 1] * lane_cos + far[:, row : row + 1] * lane_sin for row in rows]
    return split(jnp.concatenate(blocks, 1))


def in_blocks(blocks, body):
    if blocks == 1:
        body(0)
    else:
        lax.fori_loop(0, blocks, lambda index, carry: (body(index), carry)[1], 0)


def block_copies(index, block, here, there, semaphores, outward):
    columns = pl.ds(pl.multiple_of(index * block, LANES), block)
    pairs = [(near, far.at[:, columns]) for near, far in zip(here, there, strict=True)]
    return [
        pltpu.make_async_copy(*(pair if outward else pair[::-1]), semaphores.at[at])
        for at, pair in enumerate(pairs)
    ]


def filter_kernel(per, length, blocks, *refs):
    given, loaded = refs[:10], refs[10:20]
    env_ref, spec_ref = refs[20:22]
    hidden_refs, buffers = refs[22:25], refs[25:28]
    mod_ref, stage_ref, load_semaphores, out_semaphores = refs[28:]
    loads = [
        pltpu.make_async_copy(source, target, load_semaphores.at[index])
        for index, (source, target) in enumerate(zip(given, loaded, strict=True))
    ]
    for load in loads:
        load.start()
    for load in loads:
        load.wait()
    first_ref, _, middle_ref, turn_ref, near_ref, lane_ref, in_ref, out_ref, rates_ref, _ = loaded
    rows = length // LANES
    block = length // blocks
    block_rows = rows // blocks
    sine_high_ref, sine_low_ref, cosine_ref = buffers
    in_high, in_low = split(in_ref[...] * 0.5)
    in_weights = jnp.concatenate([in_high, in_high, in_low], 0)
    out_high, out_low = split(own_rows(per, out_ref))
    out_weights = jnp.concatenate([out_high, out_high, out_low], 1)

    def hidden_block(index):
        high, low = block_features(near_ref[index], lane_ref)
        half_angle = dot_first(in_weights, jnp.concatenate([high, low, high], 0))
        sine, cosine = sine_cosine(half_angle)
        cosine_ref[...] = cosine
        high, low = split(sine)
        sine_high_ref[...] = high
        sine_low_ref[...] = low
        copies = block_copies(index, block, buffers, hidden_refs, out_semaphores, True)
        for copy in copies:
            copy.start()
        mod_ref[...] = dot(out_weights, jnp.concatenate([high, low, high], 0))
        for row in range(block_rows):
            at = pl.multiple_of((index * block_rows + row) * 8, 8)
            stage_ref[pl.ds(at, 8), :] = mod_ref[:, row * LANES : (row + 1) * LANES]
        if blocks > 1:
            for copy in copies:
                copy.wait()

    in_blocks(blocks, hidden_block)
    rates = own_columns(per, rates_ref[...])
    position = lax.broadcasted_iota(jnp.int32, (rows, LANES), 0) * LANES
    position = position + lax.broadcasted_iota(jnp.int32, (rows, LANES), 1)
    relative = position.astype(F32) * (1.0 / length)
    kernels = []
    for channel in range(per):
        rate = -2.0 * jnp.broadcast_to(rates[channel], (8, LANES))
        inverse = jnp.sqrt(small_expm1(rate * (1.0 / length)) / (jnp.exp(rate) - 1.0))
        envelope = jnp.exp(0.5 * rate[:1, :] * relative) * inverse[:1, :]
        env_ref[channel * rows : (channel + 1) * rows, :] = envelope
        kernels.append(envelope * stage_ref[pl.ds(channel, rows, stride=8), :])
    spec_ref[...] = forward(kernels, first_ref, middle_ref, turn_ref)
    if blocks == 1:
        for copy in block_copies(0, block, buffers, hidden_refs, out_semaphores, True):
            copy.wait()


def signal_kernel(per, blocks, *refs):
    recv_ref, env_ref, first_ref, last_ref, middle_ref, turn_ref = refs[:6]
    near_ref, lane_ref, out_ref, short_ref = refs[6:10]
    hidden_refs = refs[10:13]
    raw_ref, mixed_ref, spec_ref, out_grad_ref, in_grad_ref = refs[13:18]
    buffers = refs[18:21]
    stage_ref, weighted_ref, semaphores = refs[21:]
    devices, held, tokens = recv_ref.shape
    rows = devices * tokens // LANES
    block = rows * LANES // blocks
    block_rows = rows // blocks
    step = raw_ref.shape[0] // rows
    lows = turn_ref.shape[0] // 2
    for copy in block_copies(0, block, buffers, hidden_refs, semaphores, False):
        copy.start()
    taps = own_columns(per, tap_rows(short_ref))
    for device in range(devices):
        for part in range(tokens // LANES):
            at = (device * (tokens // LANES) + part) * step
            raw_ref[at : at + held, :] = recv_ref[
                device, :, part * LANES : (part + 1) * LANES
            ].astype(F32)
    gated, grads = [], []
    for channel in range(per):
        mixed = []
        for index in range(3):
            base = raw_ref[pl.ds(index * per + channel, rows, stride=step), :]
            total = taps[channel][3 * index : 3 * index + 1, :] * base
            for tap in (1, 2):
                base = later(base)
                total = total + taps[channel][3 * index + tap : 3 * index + tap + 1, :] * base
            mixed.append(total)
        cotangent = raw_ref[pl.ds(3 * per + channel, rows, stride=step), :]
        mixed_ref[2 * channel] = mixed[1]
        mixed_ref[2 * channel + 1] = mixed[2]
        gated.append(mixed[1] * mixed[2])
        grads.append(cotangent * mixed[0])
    spectra = forward(gated + grads, first_ref, middle_ref, turn_ref)
    spec_ref[...] = spectra
    products = []
    for channel in range(per):
        at, other = channel * lows, (per + channel) * lows
        gated_real, gated_imag = spectra[at : at + lows, :LANES], spectra[at : at + lows, LANES:]
        grad_real, grad_imag = (
            spectra[other : other + lows, :LANES],
            spectra[other : other + lows, LANES:],
        )
        products.append(
            (
                grad_real * gated_real + grad_imag * gated_imag,
                grad_imag * gated_real - grad_real * gated_imag,
            )
        )
    results = backward(products, last_ref, middle_ref, turn_ref)
    if per < 8:
        stage_ref[...] = jnp.zeros_like(stage_ref)
    for channel in range(per):
        weighted = results[channel] * env_ref[channel * rows : (channel + 1) * rows, :]
        stage_ref[pl.ds(channel, rows, stride=8), :] = weighted
    out_rows = own_rows(per, out_ref)
    out_rounded = out_rows.astype(BF16).astype(F32)
    weights = jnp.concatenate([out_rows, out_rows, out_rows - out_rounded], 0).astype(BF16)
    out_grad_ref[...] = jnp.zeros_like(out_grad_ref)
    in_grad_ref[...] = jnp.zeros_like(in_grad_ref)

    def add_block(index):
        copies = block_copies(index, block, buffers, hidden_refs, semaphores, False)
        if blocks > 1:

            @pl.when(index > 0)
            def _():
                for copy in copies:
                    copy.start()

        for row in range(block_rows):
            at = pl.multiple_of((index * block_rows + row) * 8, 8)
            weighted_ref[:, row * LANES : (row + 1) * LANES] = stage_ref[pl.ds(at, 8), :]
        count = lane_ref.shape[0] // 2
        feature_high, feature_low = block_features(near_ref[index], lane_ref)
        weighted = weighted_ref[...]
        high = weighted.astype(BF16)
        rounded = high.astype(F32)
        both = jnp.concatenate([weighted, weighted - rounded], 0).astype(BF16)
        terms = jnp.concatenate([weighted, weighted - rounded, weighted], 0).astype(BF16)
        grad = dot_first(weights, terms)
        for copy in copies:
            copy.wait()
        sine_high_ref, sine_low_ref, cosine_ref = buffers
        total = dot_last(both, sine_high_ref[...])
        out_grad_ref[...] += total[:8] + total[8:] + dot_last(high, sine_low_ref[...])
        grad_high, grad_low = split(grad * cosine_ref[...])
        total = dot_last(jnp.concatenate([feature_high, feature_low], 0), grad_high)
        in_grad_ref[...] += total[:count] + total[count:] + dot_last(feature_high, grad_low)

    in_blocks(blocks, add_block)


def proj_grad_kernel(
    per,
    scale,
    short_ref,
    raw_ref,
    mixed_ref,
    spec_ref,
    kernel_spec_ref,
    out_grad_ref,
    last_ref,
    middle_ref,
    turn_ref,
    slab_ref,
    stage_ref,
):
    devices, held, width = slab_ref.shape
    tokens = width - LANES
    rows = devices * tokens // LANES
    taps = own_columns(per, tap_rows(short_ref))
    step = raw_ref.shape[0] // rows
    lows = turn_ref.shape[0] // 2
    products = []
    for sign in (1.0, -1.0):
        for channel in range(per):
            at = (channel if sign > 0 else per + channel) * lows
            real, imag = spec_ref[at : at + lows, :LANES], spec_ref[at : at + lows, LANES:]
            at = channel * lows
            kernel_real = kernel_spec_ref[at : at + lows, :LANES]
            kernel_imag = sign * kernel_spec_ref[at : at + lows, LANES:]
            products.append(
                (
                    real * kernel_real - imag * kernel_imag,
                    real * kernel_imag + imag * kernel_real,
                )
            )
    results = backward(products, last_ref, middle_ref, turn_ref)
    sums = [None] * (3 * per)
    for channel in range(per):
        cotangent = raw_ref[pl.ds(3 * per + channel, rows, stride=step), :]
        grad_mixed = (
            cotangent * results[channel],
            results[per + channel] * mixed_ref[2 * channel + 1],
            results[per + channel] * mixed_ref[2 * channel],
        )
        for index in range(3):
            base = raw_ref[pl.ds(index * per + channel, rows, stride=step), :]
            grad = grad_mixed[index]
            total = taps[channel][3 * index : 3 * index + 1, :] * grad
            parts = [jnp.sum(grad * base, axis=0, keepdims=True)]
            moved = grad
            for tap in (1, 2):
                base = later(base)
                moved = sooner(moved)
                total = total + taps[channel][3 * index + tap : 3 * index + tap + 1, :] * moved
                parts.append(jnp.sum(grad * base, axis=0, keepdims=True))
            sums[index * per + channel] = jnp.concatenate(parts, 0)
            stage_ref[pl.ds(index * per + channel, rows, stride=held), :] = total
    for device in range(devices):
        for part in range(tokens // LANES):
            at = (device * (tokens // LANES) + part) * held
            slab_ref[device, :, part * LANES : (part + 1) * LANES] = stage_ref[
                at : at + held, :
            ].astype(BF16)
    row = lax.broadcasted_iota(jnp.int32, (held, LANES), 0)
    lane = lax.broadcasted_iota(jnp.int32, (held, LANES), 1)
    small = jnp.zeros((held, LANES), F32)
    for place in range(3 * per):
        total = jnp.sum(sums[place], axis=1, keepdims=True) * scale
        for tap in range(3):
            small = jnp.where((row == 4 + place) & (lane == tap), total[tap : tap + 1, :], small)
    order = out_grad_ref.shape[1]
    out_grad = jnp.concatenate(
        [out_grad_ref[...] * scale, jnp.zeros((8, LANES - order), F32)], 1
    )
    out_grad = jnp.concatenate([out_grad, jnp.zeros((held - 8, LANES), F32)], 0)
    small = jnp.where(row < per, out_grad, small)
    rest = pltpu.roll(small - small.astype(BF16).astype(F32), LANES // 2, 1)
    small = jnp.where(lane < LANES // 2, small, rest).astype(BF16)
    for device in range(devices):
        slab_ref[device, :, tokens:] = small


def finish_kernel(scale, slab_ref, *refs):
    parts, result_ref = refs[:-1], refs[-1]
    total = parts[0][...]
    for part in parts[1:]:
        total = total + part[...]
    total = total * scale
    rounded = total.astype(BF16).astype(F32)
    halves = jnp.concatenate([total, total - rounded], 1)
    held = slab_ref.shape[1]
    count = halves.shape[0] // 4
    wide = jnp.concatenate([halves[4 * index : 4 * index + 4, :] for index in range(count)], 1)
    wide = jnp.concatenate([jnp.zeros((held - 4, wide.shape[1]), F32), wide], 0)
    keep = lax.broadcasted_iota(jnp.int32, wide.shape, 0) < held - 4
    for device in range(slab_ref.shape[0]):
        main = slab_ref[device, :, : wide.shape[1]].astype(F32)
        result_ref[device, :, : wide.shape[1]] = jnp.where(keep, main, wide).astype(BF16)
        result_ref[device, :, wide.shape[1] :] = slab_ref[device, :, wide.shape[1] :]


def unpack_kernel(per, recv_ref, proj_ref, short_ref, out_ref, in_ref):
    channels, tokens = proj_ref.shape[1:]
    devices = channels // per
    held = recv_ref.shape[1]
    features, order = in_ref.shape
    for index in range(3):
        rows = [
            recv_ref[device, index * per : (index + 1) * per, :tokens].astype(F32)
            for device in range(devices)
        ]
        proj_ref[index] = jnp.concatenate(rows, 0).astype(BF16)
    small = [recv_ref[device, :, tokens:].astype(F32) for device in range(devices)]
    small = [part + pltpu.roll(part, LANES // 2, 1) for part in small]
    for index in range(3):
        at = 4 + index * per
        rows = jnp.concatenate([part[at : at + per, :] for part in small], 0)
        short_ref[index] = rows.T[:3, :]
    out_ref[...] = jnp.concatenate([part[:per, :order] for part in small], 0)
    count = features // 4
    total = recv_ref[0, held - 4 :, : count * LANES].astype(F32)
    for device in range(1, devices):
        total = total + recv_ref[device, held - 4 :, : count * LANES].astype(F32)
    total = jnp.concatenate(
        [total[:, index * LANES : (index + 1) * LANES] for index in range(count)], 0
    )
    in_ref[...] = total[:, :order] + total[:, order:]


def call(kernel, out, limit, in_specs=None, out_specs=None, flops=0, moved=0, **more):
    vmem = pl.BlockSpec(memory_space=pltpu.VMEM)
    return pl.pallas_call(
        kernel,
        out_shape=out,
        in_specs=in_specs,
        out_specs=out_specs if out_specs is not None else jax.tree.map(lambda _: vmem, out),
        compiler_params=pltpu.CompilerParams(vmem_limit_bytes=limit),
        cost_estimate=pl.CostEstimate(flops=flops, bytes_accessed=moved, transcendentals=0),
        **more,
    )


def shards(proj, cotangent, short_w, filter_in, filter_out, rates):
    vmem = pl.BlockSpec(memory_space=pltpu.VMEM)
    hbm = pl.BlockSpec(memory_space=pltpu.HBM)
    channels, tokens = cotangent.shape
    devices = lax.axis_size("seq")
    groups = lax.axis_size("ch")
    length = devices * tokens
    rows = length // LANES
    lows = rows + 8
    features, order = filter_in.shape
    scale = 1.0 / math.sqrt(length)
    per = max(1, channels // devices)
    held = 4 * per
    step = max(8, held)
    small = length * order * 8 <= 8 * MIB
    limit = (24 if small else 56) * MIB
    sds = jax.ShapeDtypeStruct
    made = pltpu.VMEM if small else sds
    put = (lambda x: pltpu.with_memory_space_constraint(x, pltpu.VMEM)) if small else (lambda x: x)
    keep = lambda x: pltpu.with_memory_space_constraint(x, pltpu.HBM)

    packed = call(
        functools.partial(pack_kernel, per),
        made((devices, held, tokens), BF16),
        limit,
        in_specs=[vmem, vmem],
    )(keep(proj), keep(cotangent))
    recv = lax.all_to_all(packed, "seq", split_axis=0, concat_axis=0, tiled=True)

    near, lane_table = feature_tables(length, features)
    blocks = max(1, rows // 64)
    block = length // blocks
    near = near.reshape(2 * features, blocks, rows // blocks).transpose(1, 0, 2)
    tables = transform_tables(length)
    given = [tables[name] for name in ("first", "last", "middle", "turn")] + [near, lane_table]
    given = [jnp.asarray(value) for value in given]
    given += [filter_in, filter_out.T, rates.reshape(1, channels), short_w.transpose(0, 2, 1)]
    hidden = tuple(pltpu.HBM((order, length), kind) for kind in (BF16, BF16, F32))
    buffers = [pltpu.VMEM((order, block), kind) for kind in (BF16, BF16, F32)]
    *loaded, envelope, kernel_spec, sine_high, sine_low, cosine = call(
        functools.partial(filter_kernel, per, length, blocks),
        tuple(made(value.shape, value.dtype) for value in given)
        + (made((per * rows, LANES), F32), made((per * lows, 2 * LANES), F32))
        + hidden,
        limit,
        in_specs=[hbm] * len(given),
        out_specs=(vmem,) * (len(given) + 2) + (hbm,) * 3,
        scratch_shapes=buffers
        + [
            pltpu.VMEM((8, block), F32),
            pltpu.VMEM((rows * 8, LANES), F32),
            pltpu.SemaphoreType.DMA((len(given),)),
            pltpu.SemaphoreType.DMA((3,)),
        ],
        flops=8 * length * order * 3 * features,
        moved=length * order * 8,
    )(*[keep(value) for value in given])
    first, last, middle, turn, near, lane_table, _, out_rows, _, short_taps = map(put, loaded)

    raw, mixed, spec, out_grad, in_grad = call(
        functools.partial(signal_kernel, per, blocks),
        (
            made((rows * step, LANES), F32),
            made((2 * per, rows, LANES), F32),
            made((2 * per * lows, 2 * LANES), F32),
            made((8, order), F32),
            sds((features, order), F32),
        ),
        limit,
        in_specs=[vmem] * 10 + [hbm] * 3,
        scratch_shapes=buffers
        + [
            pltpu.VMEM((rows * 8, LANES), F32),
            pltpu.VMEM((8, block), F32),
            pltpu.SemaphoreType.DMA((3,)),
        ],
        flops=400 * length * LANES,
    )(
        put(recv),
        put(envelope),
        first,
        last,
        middle,
        turn,
        near,
        lane_table,
        out_rows,
        short_taps,
        keep(sine_high),
        keep(sine_low),
        keep(cosine),
    )

    others = [
        lax.ppermute(in_grad, "ch", [(i, (i + by) % groups) for i in range(groups)])
        for by in range(1, groups)
    ]
    slab_rows = max(16, held)
    slab = call(
        functools.partial(proj_grad_kernel, per, scale),
        made((devices, slab_rows, tokens + LANES), BF16),
        limit,
        in_specs=[vmem] + [vmem] * 8,
        scratch_shapes=[pltpu.VMEM((rows * slab_rows, LANES), F32)],
        flops=400 * length * LANES,
    )(short_taps, put(raw), put(mixed), put(spec), put(kernel_spec), put(out_grad), last, middle, turn)
    slab = call(
        functools.partial(finish_kernel, scale),
        sds((devices, slab_rows, tokens + LANES), BF16),
        limit,
        in_specs=[vmem] * (groups + 1),
    )(put(slab), in_grad, *others)

    back = lax.all_to_all(slab, "seq", split_axis=0, concat_axis=0, tiled=True)
    grad_proj, grad_short, grad_out, grad_in = call(
        functools.partial(unpack_kernel, per),
        (
            sds((3, channels, tokens), BF16),
            sds((3, 3, channels), F32),
            sds((channels, order), F32),
            sds((features, order), F32),
        ),
        limit,
        in_specs=[vmem],
    )(back)
    return grad_proj, grad_short.transpose(0, 2, 1), grad_out.T, grad_in


def solution(mesh):
    placed = (
        P(None, "ch", "seq"),
        P("ch", "seq"),
        P(None, "ch", None),
        P(),
        P(None, "ch"),
        P("ch"),
    )
    return jax.shard_map(
        shards,
        mesh=mesh,
        in_specs=placed,
        out_specs=(P(None, "ch", "seq"), P(None, "ch", None), P(None, "ch"), P()),
        check_vma=False,
    )
```

```python
import functools
import math

import jax
import jax.numpy as jnp
import ml_dtypes
import numpy as np
from jax import lax
from jax.experimental import pallas as pl
from jax.experimental.pallas import tpu as pltpu
from jax.sharding import PartitionSpec as P

F32 = jnp.float32
BF16 = jnp.bfloat16
LANES = 128
MIB = 1024 * 1024


def split(value):
    high = value.astype(BF16)
    return high, (value - high.astype(F32)).astype(BF16)


def np_split(value):
    high = value.astype(ml_dtypes.bfloat16)
    return high, (value - high.astype(np.float64)).astype(ml_dtypes.bfloat16)


def dot(left, right):
    return jnp.dot(left, right, preferred_element_type=F32)


def dot_first(left, right):
    return lax.dot_general(left, right, (((0,), (0,)), ((), ())), preferred_element_type=F32)


def dot_last(left, right):
    return lax.dot_general(left, right, (((1,), (1,)), ((), ())), preferred_element_type=F32)


@functools.lru_cache(maxsize=None)
def transform_tables(length):
    rows = length // LANES
    points = 2 * length
    lows = rows + 8
    low = np.arange(lows)
    row = np.arange(rows)
    lane = np.arange(LANES)
    angle = 2.0 * np.pi * ((low[:, None] * row[None, :]) % (2 * rows)) / (2 * rows)
    kept = (low <= rows)[:, None]
    first = np.concatenate([np.cos(angle) * kept, -np.sin(angle) * kept], 0)
    weight = np.where((low == 0) | (low == rows), 1.0, 2.0)[:, None] / points
    last = np.concatenate([np.cos(angle) * kept * weight, -np.sin(angle) * kept * weight], 0).T
    turn = 2.0 * np.pi * ((low[:, None] * lane[None, :]) % points) / points
    lane_angle = 2.0 * np.pi * ((lane[:, None] * lane[None, :]) % LANES) / LANES
    cosine, sine = np.cos(lane_angle), np.sin(lane_angle)
    middle = np.block([[cosine, -sine], [sine, cosine]])
    first_high, first_low = np_split(first)
    last_high, last_low = np_split(last)
    middle_high, middle_low = np_split(middle)
    return dict(
        first=np.concatenate([first_high, first_high, first_low], 1),
        last=np.concatenate([last_high, last_high, last_low], 1),
        middle=np.concatenate([middle_high, middle_low], 0),
        turn=np.concatenate([np.cos(turn), np.sin(turn)], 0).astype(np.float32),
    )


@functools.lru_cache(maxsize=None)
def feature_tables(length, feature_count):
    rows = length // LANES
    feature = np.arange(feature_count)
    multiplier = (1 + feature // 2 * 499) % length
    row_angle = 2.0 * np.pi * ((multiplier[:, None] * LANES * np.arange(rows)[None, :]) % length) / length
    lane_angle = 2.0 * np.pi * ((multiplier[:, None] * np.arange(LANES)[None, :]) % length) / length
    even = (feature % 2 == 0)[:, None]
    near = np.where(even, np.cos(row_angle), np.sin(row_angle))
    far = np.where(even, -np.sin(row_angle), np.cos(row_angle))
    lane = np.concatenate([np.cos(lane_angle), np.sin(lane_angle)], 0)
    lane_high, lane_low = np_split(lane.T)
    grad_lane = np.block([[lane_high, lane_low], [lane_high, np.zeros_like(lane_low)]])
    grad_row = np.concatenate([near, far, near, far], 0).T
    return (
        np.concatenate([near, far], 0).astype(np.float32),
        lane.astype(np.float32),
        grad_lane.astype(ml_dtypes.bfloat16),
        grad_row.astype(np.float32),
    )


def middle_dot(value, middle_ref):
    high, low = split(value)
    size = 2 * LANES
    table_high, table_low = middle_ref[:size, :], middle_ref[size:, :]
    return dot(high, table_high) + dot(high, table_low) + dot(low, table_high)


def forward(signals, first_ref, middle_ref, turn_ref):
    lows = turn_ref.shape[0] // 2
    high, low = split(jnp.concatenate(signals, 1))
    partial = dot(first_ref[...], jnp.concatenate([high, low, high], 0))
    cosine, sine = turn_ref[:lows, :], turn_ref[lows:, :]
    turned = []
    for index in range(len(signals)):
        real = partial[:lows, index * LANES : (index + 1) * LANES]
        imag = partial[lows:, index * LANES : (index + 1) * LANES]
        turned.append(
            jnp.concatenate([real * cosine + imag * sine, imag * cosine - real * sine], 1)
        )
    return middle_dot(jnp.concatenate(turned, 0), middle_ref)


def backward(spectra, last_ref, middle_ref, turn_ref):
    lows = turn_ref.shape[0] // 2
    swapped = jnp.concatenate([jnp.concatenate([imag, real], 1) for real, imag in spectra], 0)
    partial = middle_dot(swapped, middle_ref)
    cosine, sine = turn_ref[:lows, :], turn_ref[lows:, :]
    turned = []
    for index in range(len(spectra)):
        imag = partial[index * lows : (index + 1) * lows, :LANES]
        real = partial[index * lows : (index + 1) * lows, LANES:]
        turned.append(
            jnp.concatenate([real * cosine - imag * sine, imag * cosine + real * sine], 0)
        )
    high, low = split(jnp.concatenate(turned, 1))
    result = dot(last_ref[...], jnp.concatenate([high, low, high], 0))
    return [result[:, index * LANES : (index + 1) * LANES] for index in range(len(spectra))]


def later(value):
    turned = pltpu.roll(value, 1, 1)
    carried = pltpu.roll(turned, 1, 0)
    row = lax.broadcasted_iota(jnp.int32, value.shape, 0)
    lane = lax.broadcasted_iota(jnp.int32, value.shape, 1)
    carried = jnp.where(row == 0, 0.0, carried)
    return jnp.where(lane == 0, carried, turned)


def sooner(value):
    rows = value.shape[0]
    turned = pltpu.roll(value, LANES - 1, 1)
    carried = pltpu.roll(turned, rows - 1, 0)
    row = lax.broadcasted_iota(jnp.int32, value.shape, 0)
    lane = lax.broadcasted_iota(jnp.int32, value.shape, 1)
    carried = jnp.where(row == rows - 1, 0.0, carried)
    return jnp.where(lane == LANES - 1, carried, turned)


def sine_cosine(half_angle):
    turns = jnp.round(half_angle * (1.0 / math.pi))
    rest = half_angle - turns * 3.140625
    rest = rest - turns * 9.67653589793e-4
    square = rest * rest
    sine = 2.59045638e-06
    for coefficient in (-1.98008819e-04, 8.33289957e-03, -1.66666476e-01, 9.99999977e-01):
        sine = sine * square + coefficient
    cosine = 2.31536124e-05
    for coefficient in (-1.38536905e-03, 4.16635829e-02, -4.99999053e-01, 9.99999953e-01):
        cosine = cosine * square + coefficient
    sine = sine * rest
    twice = sine + sine
    return twice * cosine, 1.0 - twice * sine


def first_channel(per, channels):
    return lax.axis_index("seq") * per % channels


def own_rows(per, out_ref):
    channels = out_ref.shape[0]
    start = first_channel(per, channels)
    return pltpu.roll(out_ref[...], lax.rem(channels - start, channels), 0)[:8, :]


def tap_rows(short_ref):
    return jnp.concatenate([short_ref[index] for index in range(3)], 0)


def own_columns(per, value):
    channels = value.shape[1]
    start = first_channel(per, channels)
    turned = pltpu.roll(value, lax.rem(channels - start, channels), 1)
    return [turned[:, channel : channel + 1] for channel in range(per)]


def small_expm1(value):
    total = 1.0
    for divisor in (7.0, 6.0, 5.0, 4.0, 3.0, 2.0):
        total = 1.0 + total * value * (1.0 / divisor)
    return total * value


def pack_kernel(per, proj_ref, cot_ref, out_ref):
    channels = cot_ref.shape[0]
    whole = [proj_ref[index].astype(F32) for index in range(3)] + [cot_ref[...].astype(F32)]
    for device in range(out_ref.shape[0]):
        start = device * per % channels
        rows = jnp.concatenate([part[start : start + per, :] for part in whole], 0)
        out_ref[device] = rows.astype(BF16)


def block_features(table, lane_ref):
    count = lane_ref.shape[0] // 2
    lane_cos, lane_sin = lane_ref[:count, :], lane_ref[count:, :]
    near, far = table[:count, :], table[count:, :]
    rows = range(table.shape[1])
    blocks = [near[:, row : row + 1] * lane_cos + far[:, row : row + 1] * lane_sin for row in rows]
    return split(jnp.concatenate(blocks, 1))


def in_blocks(blocks, body):
    if blocks == 1:
        body(0)
    else:
        lax.fori_loop(0, blocks, lambda index, carry: (body(index), carry)[1], 0)


def block_copies(index, block, here, there, semaphores, outward):
    columns = pl.ds(pl.multiple_of(index * block, LANES), block)
    pairs = [(near, far.at[:, columns]) for near, far in zip(here, there, strict=True)]
    return [
        pltpu.make_async_copy(*(pair if outward else pair[::-1]), semaphores.at[at])
        for at, pair in enumerate(pairs)
    ]


def filter_kernel(per, length, blocks, *refs):
    given, loaded = refs[:12], refs[12:24]
    env_ref, spec_ref = refs[24:26]
    hidden_refs, buffers = refs[26:29], list(refs[29:-4])
    mod_ref, stage_ref, load_semaphores, out_semaphores = refs[-4:]
    loads = [
        pltpu.make_async_copy(source, target, load_semaphores.at[index])
        for index, (source, target) in enumerate(zip(given, loaded, strict=True))
    ]
    for load in loads:
        load.start()
    for load in loads:
        load.wait()
    first_ref, _, middle_ref, turn_ref, near_ref, lane_ref, _, _ = loaded[:8]
    in_ref, out_ref, rates_ref, _ = loaded[8:]
    rows = length // LANES
    block = length // blocks
    block_rows = rows // blocks
    if blocks == 1:
        buffers, hidden_refs = buffers + [hidden_refs[2]], hidden_refs[:2]
    sine_high_ref, sine_low_ref, cosine_ref = buffers
    buffers = buffers[: len(hidden_refs)]
    in_high, in_low = split(in_ref[...] * 0.5)
    in_weights = jnp.concatenate([in_high, in_high, in_low], 0)
    out_high, out_low = split(own_rows(per, out_ref))
    out_weights = jnp.concatenate([out_high, out_high, out_low], 1)

    def hidden_block(index):
        high, low = block_features(near_ref[index], lane_ref)
        half_angle = dot_first(in_weights, jnp.concatenate([high, low, high], 0))
        sine, cosine = sine_cosine(half_angle)
        cosine_ref[...] = cosine
        high, low = split(sine)
        sine_high_ref[...] = high
        sine_low_ref[...] = low
        copies = block_copies(index, block, buffers, hidden_refs, out_semaphores, True)
        for copy in copies:
            copy.start()
        mod_ref[...] = dot(out_weights, jnp.concatenate([high, low, high], 0))
        for row in range(block_rows):
            at = pl.multiple_of((index * block_rows + row) * 8, 8)
            stage_ref[pl.ds(at, 8), :] = mod_ref[:, row * LANES : (row + 1) * LANES]
        if blocks > 1:
            for copy in copies:
                copy.wait()

    in_blocks(blocks, hidden_block)
    rates = own_columns(per, rates_ref[...])
    position = lax.broadcasted_iota(jnp.int32, (rows, LANES), 0) * LANES
    position = position + lax.broadcasted_iota(jnp.int32, (rows, LANES), 1)
    relative = position.astype(F32) * (1.0 / length)
    kernels = []
    for channel in range(per):
        rate = -2.0 * jnp.broadcast_to(rates[channel], (8, LANES))
        inverse = jnp.sqrt(small_expm1(rate * (1.0 / length)) / (jnp.exp(rate) - 1.0))
        envelope = jnp.exp(0.5 * rate[:1, :] * relative) * inverse[:1, :]
        env_ref[channel * rows : (channel + 1) * rows, :] = envelope
        kernels.append(envelope * stage_ref[pl.ds(channel, rows, stride=8), :])
    spec_ref[...] = forward(kernels, first_ref, middle_ref, turn_ref)
    if blocks == 1:
        for copy in block_copies(0, block, buffers, hidden_refs, out_semaphores, True):
            copy.wait()


def signal_kernel(per, blocks, *refs):
    recv_ref, env_ref, first_ref, last_ref, middle_ref, turn_ref = refs[:6]
    lane_ref, row_ref, out_ref, short_ref, cosine_ref = refs[6:11]
    sines = refs[11:13]
    raw_ref, mixed_ref, spec_ref, weighted_ref, in_grad_ref = refs[13:18]
    stage_ref, semaphores = refs[-2:]
    devices, held, tokens = recv_ref.shape
    rows = devices * tokens // LANES
    block = rows * LANES // blocks
    block_rows = rows // blocks
    step = raw_ref.shape[0] // rows
    lows = turn_ref.shape[0] // 2
    ahead = []
    if blocks == 1:
        ahead = [
            pltpu.make_async_copy(source, target, semaphores.at[at])
            for at, source, target in zip((0, 1), sines, refs[18:20], strict=True)
        ]
        for copy in ahead:
            copy.start()
    taps = own_columns(per, tap_rows(short_ref))
    for device in range(devices):
        for part in range(tokens // LANES):
            at = (device * (tokens // LANES) + part) * step
            raw_ref[at : at + held, :] = recv_ref[
                device, :, part * LANES : (part + 1) * LANES
            ].astype(F32)
    gated, grads = [], []
    for channel in range(per):
        mixed = []
        for index in range(3):
            base = raw_ref[pl.ds(index * per + channel, rows, stride=step), :]
            total = taps[channel][3 * index : 3 * index + 1, :] * base
            for tap in (1, 2):
                base = later(base)
                total = total + taps[channel][3 * index + tap : 3 * index + tap + 1, :] * base
            mixed.append(total)
        cotangent = raw_ref[pl.ds(3 * per + channel, rows, stride=step), :]
        mixed_ref[2 * channel] = mixed[1]
        mixed_ref[2 * channel + 1] = mixed[2]
        gated.append(mixed[1] * mixed[2])
        grads.append(cotangent * mixed[0])
    spectra = forward(gated + grads, first_ref, middle_ref, turn_ref)
    spec_ref[...] = spectra
    products = []
    for channel in range(per):
        at, other = channel * lows, (per + channel) * lows
        gated_real, gated_imag = spectra[at : at + lows, :LANES], spectra[at : at + lows, LANES:]
        grad_real, grad_imag = (
            spectra[other : other + lows, :LANES],
            spectra[other : other + lows, LANES:],
        )
        products.append(
            (
                grad_real * gated_real + grad_imag * gated_imag,
                grad_imag * gated_real - grad_real * gated_imag,
            )
        )
    results = backward(products, last_ref, middle_ref, turn_ref)
    if per < 8:
        stage_ref[...] = jnp.zeros_like(stage_ref)
    for channel in range(per):
        weighted = results[channel] * env_ref[channel * rows : (channel + 1) * rows, :]
        stage_ref[pl.ds(channel, rows, stride=8), :] = weighted
    out_rows = own_rows(per, out_ref)
    out_rounded = out_rows.astype(BF16).astype(F32)
    weights = jnp.concatenate([out_rows, out_rows, out_rows - out_rounded], 0).astype(BF16)
    order, features = out_ref.shape[1], lane_ref.shape[1] // 4
    in_grad_ref[...] = jnp.zeros_like(in_grad_ref)

    def add_block(index):
        cosine_here = cosine_ref
        if blocks > 1:
            cosine_here = refs[-3]
            (copy,) = block_copies(index, block, [cosine_here], [cosine_ref], semaphores, False)
            copy.start()
            copy.wait()
        parts = []
        for row in range(block_rows):
            at = pl.multiple_of((index * block_rows + row) * 8, 8)
            parts.append(stage_ref[pl.ds(at, 8), :])
        weighted = jnp.concatenate(parts, 1)
        weighted_ref[:, pl.ds(pl.multiple_of(index * block, LANES), block)] = weighted
        rounded = weighted.astype(BF16).astype(F32)
        terms = jnp.concatenate([weighted, weighted - rounded, weighted], 0).astype(BF16)
        grad = dot_first(weights, terms)
        high, low = split(grad * cosine_here[...])
        parts = []
        for row in range(block_rows):
            lanes = slice(row * LANES, (row + 1) * LANES)
            parts.append(jnp.concatenate([high[:, lanes], low[:, lanes]], 1))
        parts = dot(jnp.concatenate(parts, 0), lane_ref[...])
        total = jnp.zeros((order, LANES), F32)
        factors = row_ref[pl.ds(pl.multiple_of(index * block_rows, 8), block_rows), :]
        for row in range(block_rows):
            total = total + parts[row * order : (row + 1) * order, :] * factors[row : row + 1, :]
        total = total + pltpu.roll(total, 2 * features, 1)
        total = total + pltpu.roll(total, features, 1)
        in_grad_ref[...] += total.T[:features, :]

    in_blocks(blocks, add_block)
    for copy in ahead:
        copy.wait()


def proj_grad_kernel(
    per,
    blocks,
    scale,
    short_ref,
    raw_ref,
    mixed_ref,
    spec_ref,
    kernel_spec_ref,
    weighted_ref,
    last_ref,
    middle_ref,
    turn_ref,
    high_ref,
    low_ref,
    slab_ref,
    stage_ref,
    high_buffer=None,
    low_buffer=None,
    semaphores=None,
):
    order, block = high_ref.shape[0], high_ref.shape[1] // blocks
    devices, held, width = slab_ref.shape
    tokens = width - LANES
    rows = devices * tokens // LANES
    taps = own_columns(per, tap_rows(short_ref))
    step = raw_ref.shape[0] // rows
    lows = turn_ref.shape[0] // 2
    products = []
    for sign in (1.0, -1.0):
        for channel in range(per):
            at = (channel if sign > 0 else per + channel) * lows
            real, imag = spec_ref[at : at + lows, :LANES], spec_ref[at : at + lows, LANES:]
            at = channel * lows
            kernel_real = kernel_spec_ref[at : at + lows, :LANES]
            kernel_imag = sign * kernel_spec_ref[at : at + lows, LANES:]
            products.append(
                (
                    real * kernel_real - imag * kernel_imag,
                    real * kernel_imag + imag * kernel_real,
                )
            )
    results = backward(products, last_ref, middle_ref, turn_ref)
    sums = [None] * (3 * per)
    for channel in range(per):
        cotangent = raw_ref[pl.ds(3 * per + channel, rows, stride=step), :]
        grad_mixed = (
            cotangent * results[channel],
            results[per + channel] * mixed_ref[2 * channel + 1],
            results[per + channel] * mixed_ref[2 * channel],
        )
        for index in range(3):
            base = raw_ref[pl.ds(index * per + channel, rows, stride=step), :]
            grad = grad_mixed[index]
            total = taps[channel][3 * index : 3 * index + 1, :] * grad
            parts = [jnp.sum(grad * base, axis=0, keepdims=True)]
            moved = grad
            for tap in (1, 2):
                base = later(base)
                moved = sooner(moved)
                total = total + taps[channel][3 * index + tap : 3 * index + tap + 1, :] * moved
                parts.append(jnp.sum(grad * base, axis=0, keepdims=True))
            sums[index * per + channel] = jnp.concatenate(parts, 0)
            stage_ref[pl.ds(index * per + channel, rows, stride=held), :] = total
    for device in range(devices):
        for part in range(tokens // LANES):
            at = (device * (tokens // LANES) + part) * held
            slab_ref[device, :, part * LANES : (part + 1) * LANES] = stage_ref[
                at : at + held, :
            ].astype(BF16)
    row = lax.broadcasted_iota(jnp.int32, (held, LANES), 0)
    lane = lax.broadcasted_iota(jnp.int32, (held, LANES), 1)
    small = jnp.zeros((held, LANES), F32)
    for place in range(3 * per):
        total = jnp.sum(sums[place], axis=1, keepdims=True) * scale
        for tap in range(3):
            small = jnp.where((row == 4 + place) & (lane == tap), total[tap : tap + 1, :], small)
    out_grad = jnp.zeros((order, 2 * LANES), F32)
    for index in range(blocks):
        high_here, low_here = high_ref, low_ref
        if blocks > 1:
            high_here, low_here = high_buffer, low_buffer
            copies = block_copies(
                index, block, [high_here, low_here], [high_ref, low_ref], semaphores, False
            )
            for copy in copies:
                copy.start()
            for copy in copies:
                copy.wait()
        weighted = weighted_ref[:, index * block : (index + 1) * block]
        rounded = weighted.astype(BF16).astype(F32)
        both = jnp.concatenate([weighted, weighted - rounded], 0).astype(BF16)
        total = dot_last(high_here[...], both)
        total = total[:, :8] + total[:, 8:] + dot_last(low_here[...], both)[:, :8]
        out_grad = out_grad + jnp.concatenate([total, jnp.zeros((order, 2 * LANES - 8), F32)], 1)
    out_grad = jnp.concatenate([out_grad[:, :LANES], jnp.zeros((LANES - order, LANES), F32)], 0)
    out_grad = out_grad.T[:held, :] * scale
    small = jnp.where(row < per, out_grad, small)
    rest = pltpu.roll(small - small.astype(BF16).astype(F32), LANES // 2, 1)
    small = jnp.where(lane < LANES // 2, small, rest).astype(BF16)
    for device in range(devices):
        slab_ref[device, :, tokens:] = small


def finish_kernel(scale, slab_ref, *refs):
    parts, result_ref = refs[:-1], refs[-1]
    total = parts[0][...]
    for part in parts[1:]:
        total = total + part[...]
    total = total * scale
    rounded = total.astype(BF16).astype(F32)
    halves = jnp.concatenate([total, total - rounded], 1)
    held = slab_ref.shape[1]
    count = halves.shape[0] // 4
    wide = jnp.concatenate([halves[4 * index : 4 * index + 4, :] for index in range(count)], 1)
    wide = jnp.concatenate([jnp.zeros((held - 4, wide.shape[1]), F32), wide], 0)
    keep = lax.broadcasted_iota(jnp.int32, wide.shape, 0) < held - 4
    for device in range(slab_ref.shape[0]):
        main = slab_ref[device, :, : wide.shape[1]].astype(F32)
        result_ref[device, :, : wide.shape[1]] = jnp.where(keep, main, wide).astype(BF16)
        result_ref[device, :, wide.shape[1] :] = slab_ref[device, :, wide.shape[1] :]


def unpack_kernel(per, recv_ref, proj_ref, short_ref, out_ref, in_ref):
    channels, tokens = proj_ref.shape[1:]
    devices = channels // per
    held = recv_ref.shape[1]
    features, order = in_ref.shape
    for index in range(3):
        rows = [
            recv_ref[device, index * per : (index + 1) * per, :tokens].astype(F32)
            for device in range(devices)
        ]
        proj_ref[index] = jnp.concatenate(rows, 0).astype(BF16)
    small = [recv_ref[device, :, tokens:].astype(F32) for device in range(devices)]
    small = [part + pltpu.roll(part, LANES // 2, 1) for part in small]
    for index in range(3):
        at = 4 + index * per
        rows = jnp.concatenate([part[at : at + per, :] for part in small], 0)
        short_ref[index] = rows.T[:3, :]
    out_ref[...] = jnp.concatenate([part[:per, :order] for part in small], 0)
    count = features // 4
    total = recv_ref[0, held - 4 :, : count * LANES].astype(F32)
    for device in range(1, devices):
        total = total + recv_ref[device, held - 4 :, : count * LANES].astype(F32)
    total = jnp.concatenate(
        [total[:, index * LANES : (index + 1) * LANES] for index in range(count)], 0
    )
    in_ref[...] = total[:, :order] + total[:, order:]


def call(kernel, out, limit, in_specs=None, out_specs=None, flops=0, moved=0, **more):
    vmem = pl.BlockSpec(memory_space=pltpu.VMEM)
    return pl.pallas_call(
        kernel,
        out_shape=out,
        in_specs=in_specs,
        out_specs=out_specs if out_specs is not None else jax.tree.map(lambda _: vmem, out),
        compiler_params=pltpu.CompilerParams(vmem_limit_bytes=limit),
        cost_estimate=pl.CostEstimate(flops=flops, bytes_accessed=moved, transcendentals=0),
        **more,
    )


def shards(proj, cotangent, short_w, filter_in, filter_out, rates):
    vmem = pl.BlockSpec(memory_space=pltpu.VMEM)
    hbm = pl.BlockSpec(memory_space=pltpu.HBM)
    channels, tokens = cotangent.shape
    devices = lax.axis_size("seq")
    groups = lax.axis_size("ch")
    length = devices * tokens
    rows = length // LANES
    lows = rows + 8
    features, order = filter_in.shape
    scale = 1.0 / math.sqrt(length)
    per = max(1, channels // devices)
    held = 4 * per
    step = max(8, held)
    slab_rows = max(16, held)
    blocks = max(1, rows // 64)
    block = length // blocks
    small = blocks == 1
    limit = (24 if small else 56) * MIB
    sds = jax.ShapeDtypeStruct
    made = pltpu.VMEM if small else sds
    put = (lambda x: pltpu.with_memory_space_constraint(x, pltpu.VMEM)) if small else (lambda x: x)
    keep = lambda x: pltpu.with_memory_space_constraint(x, pltpu.HBM)

    packed = call(
        functools.partial(pack_kernel, per),
        sds((devices, held, tokens), BF16),
        limit,
        in_specs=[vmem] * 2,
    )(keep(proj), keep(cotangent))
    recv = lax.all_to_all(packed, "seq", split_axis=0, concat_axis=0, tiled=True)

    near, *lane_tables = feature_tables(length, features)
    near = near.reshape(2 * features, blocks, rows // blocks).transpose(1, 0, 2)
    tables = transform_tables(length)
    given = [tables[name] for name in ("first", "last", "middle", "turn")]
    given += [near, *lane_tables]
    given = [jnp.asarray(value) for value in given]
    given += [filter_in, filter_out.T, rates.reshape(1, channels), short_w.transpose(0, 2, 1)]
    hidden = tuple(pltpu.HBM((order, length), BF16) for _ in range(2))
    hidden += ((made if small else pltpu.HBM)((order, length), F32),)
    buffers = [pltpu.VMEM((order, block), kind) for kind in (BF16, BF16, F32)]
    *loaded, envelope, kernel_spec, sine_high, sine_low, cosine = call(
        functools.partial(filter_kernel, per, length, blocks),
        tuple(made(value.shape, value.dtype) for value in given)
        + (made((per * rows, LANES), F32), made((per * lows, 2 * LANES), F32))
        + hidden,
        limit,
        in_specs=[hbm] * len(given),
        out_specs=(vmem,) * (len(given) + 2) + (hbm, hbm, vmem if small else hbm),
        scratch_shapes=(buffers[:2] if small else buffers)
        + [
            pltpu.VMEM((8, block), F32),
            pltpu.VMEM((rows * 8, LANES), F32),
            pltpu.SemaphoreType.DMA((len(given),)),
            pltpu.SemaphoreType.DMA((3,)),
        ],
        flops=8 * length * order * 3 * features,
        moved=length * order * 8,
    )(*[keep(value) for value in given])
    first, last, middle, turn, _, _, grad_lane, grad_row = map(put, loaded[:8])
    _, out_rows, _, short_taps = map(put, loaded[8:])

    raw, mixed, spec, weighted, in_grad, *sines = call(
        functools.partial(signal_kernel, per, blocks),
        (
            made((rows * step, LANES), F32),
            made((2 * per, rows, LANES), F32),
            made((2 * per * lows, 2 * LANES), F32),
            made((8, length), F32),
            sds((features, order), F32),
        )
        + ((made((order, length), BF16),) * 2 if small else ()),
        limit,
        in_specs=[vmem] * 10 + [vmem if small else hbm] + [hbm] * 2,
        scratch_shapes=([] if small else buffers[2:])
        + [pltpu.VMEM((rows * 8, LANES), F32), pltpu.SemaphoreType.DMA((2,))],
        flops=400 * length * LANES,
    )(
        put(recv),
        put(envelope),
        first,
        last,
        middle,
        turn,
        grad_lane,
        grad_row,
        out_rows,
        short_taps,
        put(cosine) if small else keep(cosine),
        keep(sine_high),
        keep(sine_low),
    )
    if not small:
        sines = [sine_high, sine_low]

    others = [
        lax.ppermute(in_grad, "ch", [(i, (i + by) % groups) for i in range(groups)])
        for by in range(1, groups)
    ]
    slab = call(
        functools.partial(proj_grad_kernel, per, blocks, scale),
        made((devices, slab_rows, tokens + LANES), BF16),
        limit,
        in_specs=[vmem] * 9 + [vmem if small else hbm] * 2,
        scratch_shapes=[pltpu.VMEM((rows * slab_rows, LANES), F32)]
        + ([] if small else [*buffers[:2], pltpu.SemaphoreType.DMA((2,))]),
        flops=400 * length * LANES,
    )(
        short_taps,
        put(raw),
        put(mixed),
        put(spec),
        put(kernel_spec),
        put(weighted),
        last,
        middle,
        turn,
        *[put(value) if small else keep(value) for value in sines],
    )
    slab = call(
        functools.partial(finish_kernel, scale),
        sds((devices, slab_rows, tokens + LANES), BF16),
        limit,
        in_specs=[vmem] * (groups + 1),
    )(put(slab), in_grad, *others)

    back = lax.all_to_all(slab, "seq", split_axis=0, concat_axis=0, tiled=True)
    grad_proj, grad_short, grad_out, grad_in = call(
        functools.partial(unpack_kernel, per),
        (
            sds((3, channels, tokens), BF16),
            sds((3, 3, channels), F32),
            sds((channels, order), F32),
            sds((features, order), F32),
        ),
        limit,
        in_specs=[vmem],
    )(back)
    return grad_proj, grad_short.transpose(0, 2, 1), grad_out.T, grad_in


def solution(mesh):
    placed = (
        P(None, "ch", "seq"),
        P("ch", "seq"),
        P(None, "ch", None),
        P(),
        P(None, "ch"),
        P("ch"),
    )
    return jax.shard_map(
        shards,
        mesh=mesh,
        in_specs=placed,
        out_specs=(P(None, "ch", "seq"), P(None, "ch", None), P(None, "ch"), P()),
        check_vma=False,
    )
```

```python
import functools
import math

import jax
import jax.numpy as jnp
import ml_dtypes
import numpy as np
from jax import lax
from jax.experimental import pallas as pl
from jax.experimental.pallas import tpu as pltpu
from jax.sharding import PartitionSpec as P

F32 = jnp.float32
BF16 = jnp.bfloat16
LANES = 128
MIB = 1024 * 1024


def split(value):
    high = value.astype(BF16)
    return high, (value - high.astype(F32)).astype(BF16)


def np_split(value):
    high = value.astype(ml_dtypes.bfloat16)
    return high, (value - high.astype(np.float64)).astype(ml_dtypes.bfloat16)


def dot(left, right):
    return jnp.dot(left, right, preferred_element_type=F32)


def dot_first(left, right):
    return lax.dot_general(left, right, (((0,), (0,)), ((), ())), preferred_element_type=F32)


def dot_last(left, right):
    return lax.dot_general(left, right, (((1,), (1,)), ((), ())), preferred_element_type=F32)


@functools.lru_cache(maxsize=None)
def transform_tables(length):
    rows = length // LANES
    points = 2 * length
    lows = rows + 8
    low = np.arange(lows)
    row = np.arange(rows)
    lane = np.arange(LANES)
    angle = 2.0 * np.pi * ((low[:, None] * row[None, :]) % (2 * rows)) / (2 * rows)
    kept = (low <= rows)[:, None]
    first = np.concatenate([np.cos(angle) * kept, -np.sin(angle) * kept], 0)
    weight = np.where((low == 0) | (low == rows), 1.0, 2.0)[:, None] / points
    last = np.concatenate([np.cos(angle) * kept * weight, -np.sin(angle) * kept * weight], 0).T
    turn = 2.0 * np.pi * ((low[:, None] * lane[None, :]) % points) / points
    lane_angle = 2.0 * np.pi * ((lane[:, None] * lane[None, :]) % LANES) / LANES
    cosine, sine = np.cos(lane_angle), np.sin(lane_angle)
    middle = np.block([[cosine, -sine], [sine, cosine]])
    first_high, first_low = np_split(first)
    last_high, last_low = np_split(last)
    middle_high, middle_low = np_split(middle)
    return dict(
        first=np.concatenate([first_high, first_high, first_low], 1),
        last=np.concatenate([last_high, last_high, last_low], 1),
        middle=np.concatenate([middle_high, middle_low], 0),
        turn=np.concatenate([np.cos(turn), np.sin(turn)], 0).astype(np.float32),
    )


@functools.lru_cache(maxsize=None)
def feature_tables(length, feature_count):
    rows = length // LANES
    feature = np.arange(feature_count)
    multiplier = (1 + feature // 2 * 499) % length
    row_angle = 2.0 * np.pi * ((multiplier[:, None] * LANES * np.arange(rows)[None, :]) % length) / length
    lane_angle = 2.0 * np.pi * ((multiplier[:, None] * np.arange(LANES)[None, :]) % length) / length
    even = (feature % 2 == 0)[:, None]
    near = np.where(even, np.cos(row_angle), np.sin(row_angle))
    far = np.where(even, -np.sin(row_angle), np.cos(row_angle))
    lane = np.concatenate([np.cos(lane_angle), np.sin(lane_angle)], 0)
    lane_high, lane_low = np_split(lane.T)
    grad_lane = np.block([[lane_high, lane_low], [lane_high, np.zeros_like(lane_low)]])
    grad_row = np.concatenate([near, far, near, far], 0).T
    return (
        np.concatenate([near, far], 0).astype(np.float32),
        lane.astype(np.float32),
        grad_lane.astype(ml_dtypes.bfloat16),
        grad_row.astype(np.float32),
    )


def middle_dot(value, middle_ref):
    high, low = split(value)
    size = 2 * LANES
    table_high, table_low = middle_ref[:size, :], middle_ref[size:, :]
    return dot(high, table_high) + dot(high, table_low) + dot(low, table_high)


def forward(signals, first_ref, middle_ref, turn_ref):
    lows = turn_ref.shape[0] // 2
    high, low = split(jnp.concatenate(signals, 1))
    partial = dot(first_ref[...], jnp.concatenate([high, low, high], 0))
    cosine, sine = turn_ref[:lows, :], turn_ref[lows:, :]
    turned = []
    for index in range(len(signals)):
        real = partial[:lows, index * LANES : (index + 1) * LANES]
        imag = partial[lows:, index * LANES : (index + 1) * LANES]
        turned.append(
            jnp.concatenate([real * cosine + imag * sine, imag * cosine - real * sine], 1)
        )
    return middle_dot(jnp.concatenate(turned, 0), middle_ref)


def backward(spectra, last_ref, middle_ref, turn_ref):
    lows = turn_ref.shape[0] // 2
    swapped = jnp.concatenate([jnp.concatenate([imag, real], 1) for real, imag in spectra], 0)
    partial = middle_dot(swapped, middle_ref)
    cosine, sine = turn_ref[:lows, :], turn_ref[lows:, :]
    turned = []
    for index in range(len(spectra)):
        imag = partial[index * lows : (index + 1) * lows, :LANES]
        real = partial[index * lows : (index + 1) * lows, LANES:]
        turned.append(
            jnp.concatenate([real * cosine - imag * sine, imag * cosine + real * sine], 0)
        )
    high, low = split(jnp.concatenate(turned, 1))
    result = dot(last_ref[...], jnp.concatenate([high, low, high], 0))
    return [result[:, index * LANES : (index + 1) * LANES] for index in range(len(spectra))]


def later(value):
    turned = pltpu.roll(value, 1, 1)
    carried = pltpu.roll(turned, 1, 0)
    row = lax.broadcasted_iota(jnp.int32, value.shape, 0)
    lane = lax.broadcasted_iota(jnp.int32, value.shape, 1)
    carried = jnp.where(row == 0, 0.0, carried)
    return jnp.where(lane == 0, carried, turned)


def sooner(value):
    rows = value.shape[0]
    turned = pltpu.roll(value, LANES - 1, 1)
    carried = pltpu.roll(turned, rows - 1, 0)
    row = lax.broadcasted_iota(jnp.int32, value.shape, 0)
    lane = lax.broadcasted_iota(jnp.int32, value.shape, 1)
    carried = jnp.where(row == rows - 1, 0.0, carried)
    return jnp.where(lane == LANES - 1, carried, turned)


def sine_cosine(half_angle):
    turns = jnp.round(half_angle * (1.0 / math.pi))
    rest = half_angle - turns * 3.140625
    rest = rest - turns * 9.67653589793e-4
    square = rest * rest
    sine = 2.59045638e-06
    for coefficient in (-1.98008819e-04, 8.33289957e-03, -1.66666476e-01, 9.99999977e-01):
        sine = sine * square + coefficient
    cosine = 2.31536124e-05
    for coefficient in (-1.38536905e-03, 4.16635829e-02, -4.99999053e-01, 9.99999953e-01):
        cosine = cosine * square + coefficient
    sine = sine * rest
    twice = sine + sine
    return twice * cosine, 1.0 - twice * sine


def first_channel(per, channels):
    return lax.axis_index("seq") * per % channels


def own_rows(per, out_ref):
    channels = out_ref.shape[0]
    start = first_channel(per, channels)
    return pltpu.roll(out_ref[...], lax.rem(channels - start, channels), 0)[:8, :]


def tap_rows(short_ref):
    return jnp.concatenate([short_ref[index] for index in range(3)], 0)


def own_columns(per, value):
    channels = value.shape[1]
    start = first_channel(per, channels)
    turned = pltpu.roll(value, lax.rem(channels - start, channels), 1)
    return [turned[:, channel : channel + 1] for channel in range(per)]


def small_expm1(value):
    total = 1.0
    for divisor in (7.0, 6.0, 5.0, 4.0, 3.0, 2.0):
        total = 1.0 + total * value * (1.0 / divisor)
    return total * value


def pack_kernel(per, proj_ref, cot_ref, out_ref):
    channels = cot_ref.shape[0]
    whole = [proj_ref[index].astype(F32) for index in range(3)] + [cot_ref[...].astype(F32)]
    for device in range(out_ref.shape[0]):
        start = device * per % channels
        rows = jnp.concatenate([part[start : start + per, :] for part in whole], 0)
        out_ref[device] = rows.astype(BF16)


def block_features(table, lane_ref):
    count = lane_ref.shape[0] // 2
    lane_cos, lane_sin = lane_ref[:count, :], lane_ref[count:, :]
    near, far = table[:count, :], table[count:, :]
    rows = range(table.shape[1])
    blocks = [near[:, row : row + 1] * lane_cos + far[:, row : row + 1] * lane_sin for row in rows]
    return split(jnp.concatenate(blocks, 1))


def in_blocks(blocks, body):
    if blocks == 1:
        body(0)
    else:
        lax.fori_loop(0, blocks, lambda index, carry: (body(index), carry)[1], 0)


def block_copies(index, block, here, there, semaphores, outward):
    columns = pl.ds(pl.multiple_of(index * block, LANES), block)
    pairs = [(near, far.at[:, columns]) for near, far in zip(here, there, strict=True)]
    return [
        pltpu.make_async_copy(*(pair if outward else pair[::-1]), semaphores.at[at])
        for at, pair in enumerate(pairs)
    ]


def filter_kernel(per, length, blocks, *refs):
    given, loaded = refs[:12], refs[12:24]
    env_ref, spec_ref = refs[24:26]
    hidden_refs, buffers = refs[26:29], list(refs[29:-4])
    mod_ref, stage_ref, load_semaphores, out_semaphores = refs[-4:]
    loads = [
        pltpu.make_async_copy(source, target, load_semaphores.at[index])
        for index, (source, target) in enumerate(zip(given, loaded, strict=True))
    ]
    for load in loads:
        load.start()
    for load in loads:
        load.wait()
    first_ref, _, middle_ref, turn_ref, near_ref, lane_ref, _, _ = loaded[:8]
    in_ref, out_ref, rates_ref, _ = loaded[8:]
    rows = length // LANES
    block = length // blocks
    block_rows = rows // blocks
    if blocks == 1:
        buffers, hidden_refs = buffers + [hidden_refs[2]], hidden_refs[:2]
    sine_high_ref, sine_low_ref, cosine_ref = buffers
    buffers = buffers[: len(hidden_refs)]
    in_high, in_low = split(in_ref[...] * 0.5)
    in_weights = jnp.concatenate([in_high, in_high, in_low], 0)
    out_high, out_low = split(own_rows(per, out_ref))
    out_weights = jnp.concatenate([out_high, out_high, out_low], 1)

    def hidden_block(index):
        high, low = block_features(near_ref[index], lane_ref)
        half_angle = dot_first(in_weights, jnp.concatenate([high, low, high], 0))
        sine, cosine = sine_cosine(half_angle)
        cosine_ref[...] = cosine
        high, low = split(sine)
        sine_high_ref[...] = high
        sine_low_ref[...] = low
        copies = block_copies(index, block, buffers, hidden_refs, out_semaphores, True)
        for copy in copies:
            copy.start()
        mod_ref[...] = dot(out_weights, jnp.concatenate([high, low, high], 0))
        for row in range(block_rows):
            at = pl.multiple_of((index * block_rows + row) * 8, 8)
            stage_ref[pl.ds(at, 8), :] = mod_ref[:, row * LANES : (row + 1) * LANES]
        if blocks > 1:
            for copy in copies:
                copy.wait()

    in_blocks(blocks, hidden_block)
    rates = own_columns(per, rates_ref[...])
    position = lax.broadcasted_iota(jnp.int32, (rows, LANES), 0) * LANES
    position = position + lax.broadcasted_iota(jnp.int32, (rows, LANES), 1)
    relative = position.astype(F32) * (1.0 / length)
    kernels = []
    for channel in range(per):
        rate = -2.0 * jnp.broadcast_to(rates[channel], (8, LANES))
        inverse = jnp.sqrt(small_expm1(rate * (1.0 / length)) / (jnp.exp(rate) - 1.0))
        envelope = jnp.exp(0.5 * rate[:1, :] * relative) * inverse[:1, :]
        env_ref[channel * rows : (channel + 1) * rows, :] = envelope
        kernels.append(envelope * stage_ref[pl.ds(channel, rows, stride=8), :])
    spec_ref[...] = forward(kernels, first_ref, middle_ref, turn_ref)
    if blocks == 1:
        for copy in block_copies(0, block, buffers, hidden_refs, out_semaphores, True):
            copy.wait()


def signal_kernel(per, blocks, *refs):
    recv_ref, env_ref, first_ref, last_ref, middle_ref, turn_ref = refs[:6]
    lane_ref, row_ref, out_ref, short_ref, cosine_ref = refs[6:11]
    sines = refs[11:13]
    raw_ref, mixed_ref, spec_ref, weighted_ref, in_grad_ref = refs[13:18]
    stage_ref, semaphores = refs[-2:]
    devices, held, tokens = recv_ref.shape
    rows = devices * tokens // LANES
    block = rows * LANES // blocks
    block_rows = rows // blocks
    step = raw_ref.shape[0] // rows
    lows = turn_ref.shape[0] // 2
    ahead = []
    if blocks == 1:
        ahead = [
            pltpu.make_async_copy(source, target, semaphores.at[at])
            for at, source, target in zip((0, 1), sines, refs[18:20], strict=True)
        ]
        for copy in ahead:
            copy.start()
    taps = own_columns(per, tap_rows(short_ref))
    for device in range(devices):
        for part in range(tokens // LANES):
            at = (device * (tokens // LANES) + part) * step
            raw_ref[at : at + held, :] = recv_ref[
                device, :, part * LANES : (part + 1) * LANES
            ].astype(F32)
    gated, grads = [], []
    for channel in range(per):
        mixed = []
        for index in range(3):
            base = raw_ref[pl.ds(index * per + channel, rows, stride=step), :]
            total = taps[channel][3 * index : 3 * index + 1, :] * base
            for tap in (1, 2):
                base = later(base)
                total = total + taps[channel][3 * index + tap : 3 * index + tap + 1, :] * base
            mixed.append(total)
        cotangent = raw_ref[pl.ds(3 * per + channel, rows, stride=step), :]
        mixed_ref[2 * channel] = mixed[1]
        mixed_ref[2 * channel + 1] = mixed[2]
        gated.append(mixed[1] * mixed[2])
        grads.append(cotangent * mixed[0])
    spectra = forward(gated + grads, first_ref, middle_ref, turn_ref)
    spec_ref[...] = spectra
    products = []
    for channel in range(per):
        at, other = channel * lows, (per + channel) * lows
        gated_real, gated_imag = spectra[at : at + lows, :LANES], spectra[at : at + lows, LANES:]
        grad_real, grad_imag = (
            spectra[other : other + lows, :LANES],
            spectra[other : other + lows, LANES:],
        )
        products.append(
            (
                grad_real * gated_real + grad_imag * gated_imag,
                grad_imag * gated_real - grad_real * gated_imag,
            )
        )
    results = backward(products, last_ref, middle_ref, turn_ref)
    if per < 8:
        stage_ref[...] = jnp.zeros_like(stage_ref)
    for channel in range(per):
        weighted = results[channel] * env_ref[channel * rows : (channel + 1) * rows, :]
        stage_ref[pl.ds(channel, rows, stride=8), :] = weighted
    out_rows = own_rows(per, out_ref)
    out_rounded = out_rows.astype(BF16).astype(F32)
    weights = jnp.concatenate([out_rows, out_rows, out_rows - out_rounded], 0).astype(BF16)
    order, features = out_ref.shape[1], lane_ref.shape[1] // 4
    in_grad_ref[...] = jnp.zeros_like(in_grad_ref)

    def add_block(index):
        cosine_here = cosine_ref
        if blocks > 1:
            cosine_here = refs[-3]
            (copy,) = block_copies(index, block, [cosine_here], [cosine_ref], semaphores, False)
            copy.start()
            copy.wait()
        parts = []
        for row in range(block_rows):
            at = pl.multiple_of((index * block_rows + row) * 8, 8)
            parts.append(stage_ref[pl.ds(at, 8), :])
        weighted = jnp.concatenate(parts, 1)
        weighted_ref[:, pl.ds(pl.multiple_of(index * block, LANES), block)] = weighted
        rounded = weighted.astype(BF16).astype(F32)
        terms = jnp.concatenate([weighted, weighted - rounded, weighted], 0).astype(BF16)
        grad = dot_first(weights, terms)
        high, low = split(grad * cosine_here[...])
        parts = []
        for row in range(block_rows):
            lanes = slice(row * LANES, (row + 1) * LANES)
            parts.append(jnp.concatenate([high[:, lanes], low[:, lanes]], 1))
        parts = dot(jnp.concatenate(parts, 0), lane_ref[...])
        total = jnp.zeros((order, LANES), F32)
        factors = row_ref[pl.ds(pl.multiple_of(index * block_rows, 8), block_rows), :]
        for row in range(block_rows):
            total = total + parts[row * order : (row + 1) * order, :] * factors[row : row + 1, :]
        total = total + pltpu.roll(total, 2 * features, 1)
        total = total + pltpu.roll(total, features, 1)
        total = total.T
        half = features // 2
        in_grad_ref[...] += jnp.concatenate([total[:half, :], total[half:features, :]], 1)

    in_blocks(blocks, add_block)
    for copy in ahead:
        copy.wait()


def proj_grad_kernel(
    per,
    blocks,
    scale,
    short_ref,
    raw_ref,
    mixed_ref,
    spec_ref,
    kernel_spec_ref,
    weighted_ref,
    last_ref,
    middle_ref,
    turn_ref,
    high_ref,
    low_ref,
    slab_ref,
    stage_ref,
    high_buffer=None,
    low_buffer=None,
    semaphores=None,
):
    order, block = high_ref.shape[0], high_ref.shape[1] // blocks
    devices, held, width = slab_ref.shape
    tokens = width - LANES
    rows = devices * tokens // LANES
    taps = own_columns(per, tap_rows(short_ref))
    step = raw_ref.shape[0] // rows
    lows = turn_ref.shape[0] // 2
    products = []
    for sign in (1.0, -1.0):
        for channel in range(per):
            at = (channel if sign > 0 else per + channel) * lows
            real, imag = spec_ref[at : at + lows, :LANES], spec_ref[at : at + lows, LANES:]
            at = channel * lows
            kernel_real = kernel_spec_ref[at : at + lows, :LANES]
            kernel_imag = sign * kernel_spec_ref[at : at + lows, LANES:]
            products.append(
                (
                    real * kernel_real - imag * kernel_imag,
                    real * kernel_imag + imag * kernel_real,
                )
            )
    results = backward(products, last_ref, middle_ref, turn_ref)
    sums = [None] * (3 * per)
    for channel in range(per):
        cotangent = raw_ref[pl.ds(3 * per + channel, rows, stride=step), :]
        grad_mixed = (
            cotangent * results[channel],
            results[per + channel] * mixed_ref[2 * channel + 1],
            results[per + channel] * mixed_ref[2 * channel],
        )
        for index in range(3):
            base = raw_ref[pl.ds(index * per + channel, rows, stride=step), :]
            grad = grad_mixed[index]
            total = taps[channel][3 * index : 3 * index + 1, :] * grad
            parts = [jnp.sum(grad * base, axis=0, keepdims=True)]
            moved = grad
            for tap in (1, 2):
                base = later(base)
                moved = sooner(moved)
                total = total + taps[channel][3 * index + tap : 3 * index + tap + 1, :] * moved
                parts.append(jnp.sum(grad * base, axis=0, keepdims=True))
            sums[index * per + channel] = jnp.concatenate(parts, 0)
            stage_ref[pl.ds(index * per + channel, rows, stride=held), :] = total
    for device in range(devices):
        for part in range(tokens // LANES):
            at = (device * (tokens // LANES) + part) * held
            slab_ref[device, :, part * LANES : (part + 1) * LANES] = stage_ref[
                at : at + held, :
            ].astype(BF16)
    row = lax.broadcasted_iota(jnp.int32, (held, LANES), 0)
    lane = lax.broadcasted_iota(jnp.int32, (held, LANES), 1)
    small = jnp.zeros((held, LANES), F32)
    for place in range(3 * per):
        total = jnp.sum(sums[place], axis=1, keepdims=True) * scale
        for tap in range(3):
            small = jnp.where((row == 4 + place) & (lane == tap), total[tap : tap + 1, :], small)
    out_grad = jnp.zeros((order, 2 * LANES), F32)
    for index in range(blocks):
        high_here, low_here = high_ref, low_ref
        if blocks > 1:
            high_here, low_here = high_buffer, low_buffer
            copies = block_copies(
                index, block, [high_here, low_here], [high_ref, low_ref], semaphores, False
            )
            for copy in copies:
                copy.start()
            for copy in copies:
                copy.wait()
        weighted = weighted_ref[:, index * block : (index + 1) * block]
        rounded = weighted.astype(BF16).astype(F32)
        both = jnp.concatenate([weighted, weighted - rounded], 0).astype(BF16)
        total = dot_last(high_here[...], both)
        total = total[:, :8] + total[:, 8:] + dot_last(low_here[...], both)[:, :8]
        out_grad = out_grad + jnp.concatenate([total, jnp.zeros((order, 2 * LANES - 8), F32)], 1)
    out_grad = jnp.concatenate([out_grad[:, :LANES], jnp.zeros((LANES - order, LANES), F32)], 0)
    out_grad = out_grad.T[:held, :] * scale
    small = jnp.where(row < per, out_grad, small)
    rest = pltpu.roll(small - small.astype(BF16).astype(F32), LANES // 2, 1)
    small = jnp.where(lane < LANES // 2, small, rest).astype(BF16)
    for device in range(devices):
        slab_ref[device, :, tokens:] = small


def finish_kernel(scale, slab_ref, *refs):
    parts, result_ref = refs[:-1], refs[-1]
    total = parts[0][...]
    for part in parts[1:]:
        total = total + part[...]
    total = total * scale
    rounded = total.astype(BF16).astype(F32)
    halves = jnp.concatenate([total, total - rounded], 0)
    held = slab_ref.shape[1]
    count = halves.shape[0] // 4
    wide = jnp.concatenate([halves[4 * index : 4 * index + 4, :] for index in range(count)], 1)
    wide = jnp.concatenate([jnp.zeros((held - 4, wide.shape[1]), F32), wide], 0)
    keep = lax.broadcasted_iota(jnp.int32, wide.shape, 0) < held - 4
    for device in range(slab_ref.shape[0]):
        main = slab_ref[device, :, : wide.shape[1]].astype(F32)
        result_ref[device, :, : wide.shape[1]] = jnp.where(keep, main, wide).astype(BF16)
        result_ref[device, :, wide.shape[1] :] = slab_ref[device, :, wide.shape[1] :]


def unpack_kernel(per, recv_ref, proj_ref, short_ref, out_ref, in_ref):
    channels, tokens = proj_ref.shape[1:]
    devices = channels // per
    held = recv_ref.shape[1]
    features, order = in_ref.shape
    for index in range(3):
        rows = [
            recv_ref[device, index * per : (index + 1) * per, :tokens].astype(F32)
            for device in range(devices)
        ]
        proj_ref[index] = jnp.concatenate(rows, 0).astype(BF16)
    small = [recv_ref[device, :, tokens:].astype(F32) for device in range(devices)]
    small = [part + pltpu.roll(part, LANES // 2, 1) for part in small]
    for index in range(3):
        at = 4 + index * per
        rows = jnp.concatenate([part[at : at + per, :] for part in small], 0)
        short_ref[index] = rows.T[:3, :]
    out_ref[...] = jnp.concatenate([part[:per, :order] for part in small], 0)
    count = features // 4
    total = recv_ref[0, held - 4 :, : count * LANES].astype(F32)
    for device in range(1, devices):
        total = total + recv_ref[device, held - 4 :, : count * LANES].astype(F32)
    total = jnp.concatenate(
        [total[:, index * LANES : (index + 1) * LANES] for index in range(count)], 0
    )
    half = features // 2
    total = total[:half, :] + total[half:, :]
    in_ref[:half, :] = total[:, :order]
    in_ref[half:, :] = total[:, order:]


def call(kernel, out, limit, in_specs=None, out_specs=None, flops=0, moved=0, **more):
    vmem = pl.BlockSpec(memory_space=pltpu.VMEM)
    return pl.pallas_call(
        kernel,
        out_shape=out,
        in_specs=in_specs,
        out_specs=out_specs if out_specs is not None else jax.tree.map(lambda _: vmem, out),
        compiler_params=pltpu.CompilerParams(vmem_limit_bytes=limit),
        cost_estimate=pl.CostEstimate(flops=flops, bytes_accessed=moved, transcendentals=0),
        **more,
    )


def shards(proj, cotangent, short_w, filter_in, filter_out, rates):
    vmem = pl.BlockSpec(memory_space=pltpu.VMEM)
    hbm = pl.BlockSpec(memory_space=pltpu.HBM)
    channels, tokens = cotangent.shape
    devices = lax.axis_size("seq")
    groups = lax.axis_size("ch")
    length = devices * tokens
    rows = length // LANES
    lows = rows + 8
    features, order = filter_in.shape
    scale = 1.0 / math.sqrt(length)
    per = max(1, channels // devices)
    held = 4 * per
    step = max(8, held)
    slab_rows = max(16, held)
    blocks = max(1, rows // 64)
    block = length // blocks
    small = blocks == 1
    limit = (24 if small else 56) * MIB
    sds = jax.ShapeDtypeStruct
    made = pltpu.VMEM if small else sds
    put = (lambda x: pltpu.with_memory_space_constraint(x, pltpu.VMEM)) if small else (lambda x: x)
    keep = lambda x: pltpu.with_memory_space_constraint(x, pltpu.HBM)

    packed = call(
        functools.partial(pack_kernel, per),
        sds((devices, held, tokens), BF16),
        limit,
        in_specs=[vmem] * 2,
    )(keep(proj), keep(cotangent))
    recv = lax.all_to_all(packed, "seq", split_axis=0, concat_axis=0, tiled=True)

    near, *lane_tables = feature_tables(length, features)
    near = near.reshape(2 * features, blocks, rows // blocks).transpose(1, 0, 2)
    tables = transform_tables(length)
    given = [tables[name] for name in ("first", "last", "middle", "turn")]
    given += [near, *lane_tables]
    given = [jnp.asarray(value) for value in given]
    given += [filter_in, filter_out.T, rates.reshape(1, channels), short_w.transpose(0, 2, 1)]
    hidden = tuple(pltpu.HBM((order, length), BF16) for _ in range(2))
    hidden += ((made if small else pltpu.HBM)((order, length), F32),)
    buffers = [pltpu.VMEM((order, block), kind) for kind in (BF16, BF16, F32)]
    *loaded, envelope, kernel_spec, sine_high, sine_low, cosine = call(
        functools.partial(filter_kernel, per, length, blocks),
        tuple(made(value.shape, value.dtype) for value in given)
        + (made((per * rows, LANES), F32), made((per * lows, 2 * LANES), F32))
        + hidden,
        limit,
        in_specs=[hbm] * len(given),
        out_specs=(vmem,) * (len(given) + 2) + (hbm, hbm, vmem if small else hbm),
        scratch_shapes=(buffers[:2] if small else buffers)
        + [
            pltpu.VMEM((8, block), F32),
            pltpu.VMEM((rows * 8, LANES), F32),
            pltpu.SemaphoreType.DMA((len(given),)),
            pltpu.SemaphoreType.DMA((3,)),
        ],
        flops=8 * length * order * 3 * features,
        moved=length * order * 8,
    )(*[keep(value) for value in given])
    first, last, middle, turn, _, _, grad_lane, grad_row = map(put, loaded[:8])
    _, out_rows, _, short_taps = map(put, loaded[8:])

    raw, mixed, spec, weighted, in_grad, *sines = call(
        functools.partial(signal_kernel, per, blocks),
        (
            made((rows * step, LANES), F32),
            made((2 * per, rows, LANES), F32),
            made((2 * per * lows, 2 * LANES), F32),
            made((8, length), F32),
            sds((features // 2, 2 * order), F32),
        )
        + ((made((order, length), BF16),) * 2 if small else ()),
        limit,
        in_specs=[vmem] * 10 + [vmem if small else hbm] + [hbm] * 2,
        scratch_shapes=([] if small else buffers[2:])
        + [pltpu.VMEM((rows * 8, LANES), F32), pltpu.SemaphoreType.DMA((2,))],
        flops=400 * length * LANES,
    )(
        put(recv),
        put(envelope),
        first,
        last,
        middle,
        turn,
        grad_lane,
        grad_row,
        out_rows,
        short_taps,
        put(cosine) if small else keep(cosine),
        keep(sine_high),
        keep(sine_low),
    )
    if not small:
        sines = [sine_high, sine_low]

    others = [
        lax.ppermute(in_grad, "ch", [(i, i ^ by) for i in range(groups)])
        for by in (2,1,3)
    ]
    slab = call(
        functools.partial(proj_grad_kernel, per, blocks, scale),
        made((devices, slab_rows, tokens + LANES), BF16),
        limit,
        in_specs=[vmem] * 9 + [vmem if small else hbm] * 2,
        scratch_shapes=[pltpu.VMEM((rows * slab_rows, LANES), F32)]
        + ([] if small else [*buffers[:2], pltpu.SemaphoreType.DMA((2,))]),
        flops=400 * length * LANES,
    )(
        short_taps,
        put(raw),
        put(mixed),
        put(spec),
        put(kernel_spec),
        put(weighted),
        last,
        middle,
        turn,
        *[put(value) if small else keep(value) for value in sines],
    )
    slab = call(
        functools.partial(finish_kernel, scale),
        sds((devices, slab_rows, tokens + LANES), BF16),
        limit,
        in_specs=[vmem] * (groups + 1),
    )(put(slab), in_grad, *others)

    back = lax.all_to_all(slab, "seq", split_axis=0, concat_axis=0, tiled=True)
    grad_proj, grad_short, grad_out, grad_in = call(
        functools.partial(unpack_kernel, per),
        (
            sds((3, channels, tokens), BF16),
            sds((3, 3, channels), F32),
            sds((channels, order), F32),
            sds((features, order), F32),
        ),
        limit,
        in_specs=[vmem],
    )(back)
    return grad_proj, grad_short.transpose(0, 2, 1), grad_out.T, grad_in


def solution(mesh):
    placed = (
        P(None, "ch", "seq"),
        P("ch", "seq"),
        P(None, "ch", None),
        P(),
        P(None, "ch"),
        P("ch"),
    )
    return jax.shard_map(
        shards,
        mesh=mesh,
        in_specs=placed,
        out_specs=(P(None, "ch", "seq"), P(None, "ch", None), P(None, "ch"), P()),
        check_vma=False,
    )
```

```python
import functools
import math

import jax
import jax.numpy as jnp
import ml_dtypes
import numpy as np
from jax import lax
from jax.experimental import pallas as pl
from jax.experimental.pallas import tpu as pltpu
from jax.sharding import PartitionSpec as P

F32 = jnp.float32
BF16 = jnp.bfloat16
LANES = 128
MIB = 1024 * 1024


def split(value):
    high = value.astype(BF16)
    return high, (value - high.astype(F32)).astype(BF16)


def np_split(value):
    high = value.astype(ml_dtypes.bfloat16)
    return high, (value - high.astype(np.float64)).astype(ml_dtypes.bfloat16)


def dot(left, right):
    return jnp.dot(left, right, preferred_element_type=F32)


def dot_first(left, right):
    return lax.dot_general(left, right, (((0,), (0,)), ((), ())), preferred_element_type=F32)


def dot_last(left, right):
    return lax.dot_general(left, right, (((1,), (1,)), ((), ())), preferred_element_type=F32)


@functools.lru_cache(maxsize=None)
def transform_tables(length):
    rows = length // LANES
    points = 2 * length
    lows = rows + 8
    low = np.arange(lows)
    row = np.arange(rows)
    lane = np.arange(LANES)
    angle = 2.0 * np.pi * ((low[:, None] * row[None, :]) % (2 * rows)) / (2 * rows)
    kept = (low <= rows)[:, None]
    first = np.concatenate([np.cos(angle) * kept, -np.sin(angle) * kept], 0)
    weight = np.where((low == 0) | (low == rows), 1.0, 2.0)[:, None] / points
    last = np.concatenate([np.cos(angle) * kept * weight, -np.sin(angle) * kept * weight], 0).T
    turn = 2.0 * np.pi * ((low[:, None] * lane[None, :]) % points) / points
    lane_angle = 2.0 * np.pi * ((lane[:, None] * lane[None, :]) % LANES) / LANES
    cosine, sine = np.cos(lane_angle), np.sin(lane_angle)
    middle = np.block([[cosine, -sine], [sine, cosine]])
    first_high, first_low = np_split(first)
    last_high, last_low = np_split(last)
    middle_high, middle_low = np_split(middle)
    return dict(
        first=np.concatenate([first_high, first_high, first_low], 1),
        last=np.concatenate([last_high, last_high, last_low], 1),
        middle=np.concatenate([middle_high, middle_low], 0),
        turn=np.concatenate([np.cos(turn), np.sin(turn)], 0).astype(np.float32),
    )


@functools.lru_cache(maxsize=None)
def feature_tables(length, feature_count):
    rows = length // LANES
    feature = np.arange(feature_count)
    multiplier = (1 + feature // 2 * 499) % length
    row_angle = 2.0 * np.pi * ((multiplier[:, None] * LANES * np.arange(rows)[None, :]) % length) / length
    lane_angle = 2.0 * np.pi * ((multiplier[:, None] * np.arange(LANES)[None, :]) % length) / length
    even = (feature % 2 == 0)[:, None]
    near = np.where(even, np.cos(row_angle), np.sin(row_angle))
    far = np.where(even, -np.sin(row_angle), np.cos(row_angle))
    lane = np.concatenate([np.cos(lane_angle), np.sin(lane_angle)], 0)
    lane_high, lane_low = np_split(lane.T)
    grad_lane = np.block([[lane_high, lane_low], [lane_high, np.zeros_like(lane_low)]])
    grad_row = np.concatenate([near, far, near, far], 0).T
    return (
        np.concatenate([near, far], 0).astype(np.float32),
        lane.astype(np.float32),
        grad_lane.astype(ml_dtypes.bfloat16),
        grad_row.astype(np.float32),
    )


def middle_dot(value, middle_ref):
    high, low = split(value)
    size = 2 * LANES
    table_high, table_low = middle_ref[:size, :], middle_ref[size:, :]
    return dot(high, table_high) + dot(high, table_low) + dot(low, table_high)


def forward(signals, first_ref, middle_ref, turn_ref):
    lows = turn_ref.shape[0] // 2
    high, low = split(jnp.concatenate(signals, 1))
    partial = dot(first_ref[...], jnp.concatenate([high, low, high], 0))
    cosine, sine = turn_ref[:lows, :], turn_ref[lows:, :]
    turned = []
    for index in range(len(signals)):
        real = partial[:lows, index * LANES : (index + 1) * LANES]
        imag = partial[lows:, index * LANES : (index + 1) * LANES]
        turned.append(
            jnp.concatenate([real * cosine + imag * sine, imag * cosine - real * sine], 1)
        )
    return middle_dot(jnp.concatenate(turned, 0), middle_ref)


def backward(spectra, last_ref, middle_ref, turn_ref):
    lows = turn_ref.shape[0] // 2
    swapped = jnp.concatenate([jnp.concatenate([imag, real], 1) for real, imag in spectra], 0)
    partial = middle_dot(swapped, middle_ref)
    cosine, sine = turn_ref[:lows, :], turn_ref[lows:, :]
    turned = []
    for index in range(len(spectra)):
        imag = partial[index * lows : (index + 1) * lows, :LANES]
        real = partial[index * lows : (index + 1) * lows, LANES:]
        turned.append(
            jnp.concatenate([real * cosine - imag * sine, imag * cosine + real * sine], 0)
        )
    high, low = split(jnp.concatenate(turned, 1))
    result = dot(last_ref[...], jnp.concatenate([high, low, high], 0))
    return [result[:, index * LANES : (index + 1) * LANES] for index in range(len(spectra))]


def later(value):
    turned = pltpu.roll(value, 1, 1)
    carried = pltpu.roll(turned, 1, 0)
    row = lax.broadcasted_iota(jnp.int32, value.shape, 0)
    lane = lax.broadcasted_iota(jnp.int32, value.shape, 1)
    carried = jnp.where(row == 0, 0.0, carried)
    return jnp.where(lane == 0, carried, turned)


def sooner(value):
    rows = value.shape[0]
    turned = pltpu.roll(value, LANES - 1, 1)
    carried = pltpu.roll(turned, rows - 1, 0)
    row = lax.broadcasted_iota(jnp.int32, value.shape, 0)
    lane = lax.broadcasted_iota(jnp.int32, value.shape, 1)
    carried = jnp.where(row == rows - 1, 0.0, carried)
    return jnp.where(lane == LANES - 1, carried, turned)


def sine_cosine(half_angle):
    turns = jnp.round(half_angle * (1.0 / math.pi))
    rest = half_angle - turns * 3.140625
    rest = rest - turns * 9.67653589793e-4
    square = rest * rest
    sine = 2.59045638e-06
    for coefficient in (-1.98008819e-04, 8.33289957e-03, -1.66666476e-01, 9.99999977e-01):
        sine = sine * square + coefficient
    cosine = 2.31536124e-05
    for coefficient in (-1.38536905e-03, 4.16635829e-02, -4.99999053e-01, 9.99999953e-01):
        cosine = cosine * square + coefficient
    sine = sine * rest
    twice = sine + sine
    return twice * cosine, 1.0 - twice * sine


def first_channel(per, channels):
    return lax.axis_index("seq") * per % channels


def own_rows(per, out_ref):
    channels = out_ref.shape[0]
    start = first_channel(per, channels)
    return pltpu.roll(out_ref[...], lax.rem(channels - start, channels), 0)[:8, :]


def tap_rows(short_ref):
    return jnp.concatenate([short_ref[index] for index in range(3)], 0)


def own_columns(per, value):
    channels = value.shape[1]
    start = first_channel(per, channels)
    turned = pltpu.roll(value, lax.rem(channels - start, channels), 1)
    return [turned[:, channel : channel + 1] for channel in range(per)]


def small_expm1(value):
    total = 1.0
    for divisor in (7.0, 6.0, 5.0, 4.0, 3.0, 2.0):
        total = 1.0 + total * value * (1.0 / divisor)
    return total * value


def pack_kernel(per, proj_ref, cot_ref, out_ref):
    channels = cot_ref.shape[0]
    whole = [proj_ref[index].astype(F32) for index in range(3)] + [cot_ref[...].astype(F32)]
    for device in range(out_ref.shape[0]):
        start = device * per % channels
        rows = jnp.concatenate([part[start : start + per, :] for part in whole], 0)
        out_ref[device] = rows.astype(BF16)


def block_features(table, lane_ref):
    count = lane_ref.shape[0] // 2
    lane_cos, lane_sin = lane_ref[:count, :], lane_ref[count:, :]
    near, far = table[:count, :], table[count:, :]
    rows = range(table.shape[1])
    blocks = [near[:, row : row + 1] * lane_cos + far[:, row : row + 1] * lane_sin for row in rows]
    return split(jnp.concatenate(blocks, 1))


def in_blocks(blocks, body):
    if blocks == 1:
        body(0)
    else:
        lax.fori_loop(0, blocks, lambda index, carry: (body(index), carry)[1], 0)


def block_copies(index, block, here, there, semaphores, outward):
    columns = pl.ds(pl.multiple_of(index * block, LANES), block)
    pairs = [(near, far.at[:, columns]) for near, far in zip(here, there, strict=True)]
    return [
        pltpu.make_async_copy(*(pair if outward else pair[::-1]), semaphores.at[at])
        for at, pair in enumerate(pairs)
    ]


def filter_kernel(per, length, blocks, *refs):
    given, loaded = refs[:12], refs[12:24]
    env_ref, spec_ref = refs[24:26]
    hidden_refs, buffers = refs[26:29], list(refs[29:-4])
    mod_ref, stage_ref, load_semaphores, out_semaphores = refs[-4:]
    loads = [
        pltpu.make_async_copy(source, target, load_semaphores.at[index])
        for index, (source, target) in enumerate(zip(given, loaded, strict=True))
    ]
    for load in loads:
        load.start()
    for load in loads:
        load.wait()
    first_ref, _, middle_ref, turn_ref, near_ref, lane_ref, _, _ = loaded[:8]
    in_ref, out_ref, rates_ref, _ = loaded[8:]
    rows = length // LANES
    block = length // blocks
    block_rows = rows // blocks
    if blocks == 1:
        buffers, hidden_refs = buffers + [hidden_refs[2]], hidden_refs[:2]
    sine_high_ref, sine_low_ref, cosine_ref = buffers
    buffers = buffers[: len(hidden_refs)]
    in_high, in_low = split(in_ref[...] * 0.5)
    in_weights = jnp.concatenate([in_high, in_high, in_low], 0)
    out_high, out_low = split(own_rows(per, out_ref))
    out_weights = jnp.concatenate([out_high, out_high, out_low], 1)

    def hidden_block(index):
        high, low = block_features(near_ref[index], lane_ref)
        half_angle = dot_first(in_weights, jnp.concatenate([high, low, high], 0))
        sine, cosine = sine_cosine(half_angle)
        cosine_ref[...] = cosine
        high, low = split(sine)
        sine_high_ref[...] = high
        sine_low_ref[...] = low
        copies = block_copies(index, block, buffers, hidden_refs, out_semaphores, True)
        for copy in copies:
            copy.start()
        mod_ref[...] = dot(out_weights, jnp.concatenate([high, low, high], 0))
        for row in range(block_rows):
            at = pl.multiple_of((index * block_rows + row) * 8, 8)
            stage_ref[pl.ds(at, 8), :] = mod_ref[:, row * LANES : (row + 1) * LANES]
        if blocks > 1:
            for copy in copies:
                copy.wait()

    in_blocks(blocks, hidden_block)
    rates = own_columns(per, rates_ref[...])
    position = lax.broadcasted_iota(jnp.int32, (rows, LANES), 0) * LANES
    position = position + lax.broadcasted_iota(jnp.int32, (rows, LANES), 1)
    relative = position.astype(F32) * (1.0 / length)
    kernels = []
    for channel in range(per):
        rate = -2.0 * jnp.broadcast_to(rates[channel], (8, LANES))
        inverse = jnp.sqrt(small_expm1(rate * (1.0 / length)) / (jnp.exp(rate) - 1.0))
        envelope = jnp.exp(0.5 * rate[:1, :] * relative) * inverse[:1, :]
        env_ref[channel * rows : (channel + 1) * rows, :] = envelope
        kernels.append(envelope * stage_ref[pl.ds(channel, rows, stride=8), :])
    spec_ref[...] = forward(kernels, first_ref, middle_ref, turn_ref)
    if blocks == 1:
        for copy in block_copies(0, block, buffers, hidden_refs, out_semaphores, True):
            copy.wait()


def signal_kernel(per, blocks, *refs):
    recv_ref, env_ref, first_ref, last_ref, middle_ref, turn_ref = refs[:6]
    lane_ref, row_ref, out_ref, short_ref, cosine_ref = refs[6:11]
    sines = refs[11:13]
    raw_ref, mixed_ref, spec_ref, weighted_ref, in_grad_ref = refs[13:18]
    stage_ref, semaphores = refs[-2:]
    devices, held, tokens = recv_ref.shape
    rows = devices * tokens // LANES
    block = rows * LANES // blocks
    block_rows = rows // blocks
    step = raw_ref.shape[0] // rows
    lows = turn_ref.shape[0] // 2
    ahead = []
    if blocks == 1:
        ahead = [
            pltpu.make_async_copy(source, target, semaphores.at[at])
            for at, source, target in zip((0, 1), sines, refs[18:20], strict=True)
        ]
        for copy in ahead:
            copy.start()
    taps = own_columns(per, tap_rows(short_ref))
    for device in range(devices):
        for part in range(tokens // LANES):
            at = (device * (tokens // LANES) + part) * step
            raw_ref[at : at + held, :] = recv_ref[
                device, :, part * LANES : (part + 1) * LANES
            ].astype(F32)
    gated, grads = [], []
    for channel in range(per):
        mixed = []
        for index in range(3):
            base = raw_ref[pl.ds(index * per + channel, rows, stride=step), :]
            total = taps[channel][3 * index : 3 * index + 1, :] * base
            for tap in (1, 2):
                base = later(base)
                total = total + taps[channel][3 * index + tap : 3 * index + tap + 1, :] * base
            mixed.append(total)
        cotangent = raw_ref[pl.ds(3 * per + channel, rows, stride=step), :]
        mixed_ref[2 * channel] = mixed[1]
        mixed_ref[2 * channel + 1] = mixed[2]
        gated.append(mixed[1] * mixed[2])
        grads.append(cotangent * mixed[0])
    spectra = forward(gated + grads, first_ref, middle_ref, turn_ref)
    spec_ref[...] = spectra
    products = []
    for channel in range(per):
        at, other = channel * lows, (per + channel) * lows
        gated_real, gated_imag = spectra[at : at + lows, :LANES], spectra[at : at + lows, LANES:]
        grad_real, grad_imag = (
            spectra[other : other + lows, :LANES],
            spectra[other : other + lows, LANES:],
        )
        products.append(
            (
                grad_real * gated_real + grad_imag * gated_imag,
                grad_imag * gated_real - grad_real * gated_imag,
            )
        )
    results = backward(products, last_ref, middle_ref, turn_ref)
    if per < 8:
        stage_ref[...] = jnp.zeros_like(stage_ref)
    for channel in range(per):
        weighted = results[channel] * env_ref[channel * rows : (channel + 1) * rows, :]
        stage_ref[pl.ds(channel, rows, stride=8), :] = weighted
    out_rows = own_rows(per, out_ref)
    out_rounded = out_rows.astype(BF16).astype(F32)
    weights = jnp.concatenate([out_rows, out_rows, out_rows - out_rounded], 0).astype(BF16)
    order, features = out_ref.shape[1], lane_ref.shape[1] // 4
    in_grad_ref[...] = jnp.zeros_like(in_grad_ref)

    def add_block(index):
        cosine_here = cosine_ref
        if blocks > 1:
            cosine_here = refs[-3]
            (copy,) = block_copies(index, block, [cosine_here], [cosine_ref], semaphores, False)
            copy.start()
            copy.wait()
        parts = []
        for row in range(block_rows):
            at = pl.multiple_of((index * block_rows + row) * 8, 8)
            parts.append(stage_ref[pl.ds(at, 8), :])
        weighted = jnp.concatenate(parts, 1)
        weighted_ref[:, pl.ds(pl.multiple_of(index * block, LANES), block)] = weighted
        rounded = weighted.astype(BF16).astype(F32)
        terms = jnp.concatenate([weighted, weighted - rounded, weighted], 0).astype(BF16)
        grad = dot_first(weights, terms)
        high, low = split(grad * cosine_here[...])
        parts = []
        for row in range(block_rows):
            lanes = slice(row * LANES, (row + 1) * LANES)
            parts.append(jnp.concatenate([high[:, lanes], low[:, lanes]], 1))
        parts = dot(jnp.concatenate(parts, 0), lane_ref[...])
        total = jnp.zeros((order, LANES), F32)
        factors = row_ref[pl.ds(pl.multiple_of(index * block_rows, 8), block_rows), :]
        for row in range(block_rows):
            total = total + parts[row * order : (row + 1) * order, :] * factors[row : row + 1, :]
        total = total + pltpu.roll(total, 2 * features, 1)
        total = total + pltpu.roll(total, features, 1)
        total = total.T
        half = features // 2
        in_grad_ref[...] += jnp.concatenate([total[:half, :], total[half:features, :]], 1)

    in_blocks(blocks, add_block)
    for copy in ahead:
        copy.wait()


def proj_grad_kernel(
    per,
    blocks,
    scale,
    short_ref,
    raw_ref,
    mixed_ref,
    spec_ref,
    kernel_spec_ref,
    weighted_ref,
    last_ref,
    middle_ref,
    turn_ref,
    high_ref,
    low_ref,
    slab_ref,
    stage_ref,
    high_buffer=None,
    low_buffer=None,
    semaphores=None,
):
    order, block = high_ref.shape[0], high_ref.shape[1] // blocks
    devices = slab_ref.shape[0]
    rows = weighted_ref.shape[1] // LANES
    tokens = rows // devices * LANES
    held = stage_ref.shape[0] // rows
    taps = own_columns(per, tap_rows(short_ref))
    step = raw_ref.shape[0] // rows
    lows = turn_ref.shape[0] // 2
    products = []
    for sign in (1.0, -1.0):
        for channel in range(per):
            at = (channel if sign > 0 else per + channel) * lows
            real, imag = spec_ref[at : at + lows, :LANES], spec_ref[at : at + lows, LANES:]
            at = channel * lows
            kernel_real = kernel_spec_ref[at : at + lows, :LANES]
            kernel_imag = sign * kernel_spec_ref[at : at + lows, LANES:]
            products.append(
                (
                    real * kernel_real - imag * kernel_imag,
                    real * kernel_imag + imag * kernel_real,
                )
            )
    results = backward(products, last_ref, middle_ref, turn_ref)
    sums = [None] * (3 * per)
    for channel in range(per):
        cotangent = raw_ref[pl.ds(3 * per + channel, rows, stride=step), :]
        grad_mixed = (
            cotangent * results[channel],
            results[per + channel] * mixed_ref[2 * channel + 1],
            results[per + channel] * mixed_ref[2 * channel],
        )
        for index in range(3):
            base = raw_ref[pl.ds(index * per + channel, rows, stride=step), :]
            grad = grad_mixed[index]
            total = taps[channel][3 * index : 3 * index + 1, :] * grad
            parts = [jnp.sum(grad * base, axis=0, keepdims=True)]
            moved = grad
            for tap in (1, 2):
                base = later(base)
                moved = sooner(moved)
                total = total + taps[channel][3 * index + tap : 3 * index + tap + 1, :] * moved
                parts.append(jnp.sum(grad * base, axis=0, keepdims=True))
            sums[index * per + channel] = jnp.concatenate(parts, 0)
            stage_ref[pl.ds(index * per + channel, rows, stride=held), :] = total
    parts = tokens // LANES
    for device in range(devices):
        blocks_here = []
        for part in range(parts):
            at = (device * parts + part) * held
            blocks_here.append(stage_ref[at : at + held, :])
        for part in range(parts):
            lanes = slice(part * LANES, (part + 1) * LANES)
            slab_ref[device, :, lanes] = blocks_here[part][:8, :].astype(BF16)
        if held > 8:
            for part in range(parts // 2):
                lanes = slice(tokens + part * LANES, tokens + (part + 1) * LANES)
                pair = [blocks_here[part][8:12, :], blocks_here[part + parts // 2][8:12, :]]
                slab_ref[device, :, lanes] = jnp.concatenate(pair, 0).astype(BF16)
    row = lax.broadcasted_iota(jnp.int32, (8, LANES), 0)
    lane = lax.broadcasted_iota(jnp.int32, (8, LANES), 1)
    small = jnp.zeros((8, LANES), F32)
    for place in range(3 * per):
        index, channel = place // per, place % per
        total = jnp.sum(sums[place], axis=1, keepdims=True) * scale
        for tap in range(3):
            at = (row == per + channel) & (lane == 3 * index + tap)
            small = jnp.where(at, total[tap : tap + 1, :], small)
    out_grad = jnp.zeros((order, 2 * LANES), F32)
    for index in range(blocks):
        high_here, low_here = high_ref, low_ref
        if blocks > 1:
            high_here, low_here = high_buffer, low_buffer
            copies = block_copies(
                index, block, [high_here, low_here], [high_ref, low_ref], semaphores, False
            )
            for copy in copies:
                copy.start()
            for copy in copies:
                copy.wait()
        weighted = weighted_ref[:, index * block : (index + 1) * block]
        rounded = weighted.astype(BF16).astype(F32)
        both = jnp.concatenate([weighted, weighted - rounded], 0).astype(BF16)
        total = dot_last(high_here[...], both)
        total = total[:, :8] + total[:, 8:] + dot_last(low_here[...], both)[:, :8]
        out_grad = out_grad + jnp.concatenate([total, jnp.zeros((order, 2 * LANES - 8), F32)], 1)
    out_grad = jnp.concatenate([out_grad[:, :LANES], jnp.zeros((LANES - order, LANES), F32)], 0)
    out_grad = out_grad.T[:8, :] * scale
    small = jnp.where(row < per, out_grad, small)
    rest = pltpu.roll(small - small.astype(BF16).astype(F32), LANES // 2, 1)
    small = jnp.where(lane < LANES // 2, small, rest).astype(BF16)
    for device in range(devices):
        slab_ref[device, :, slab_ref.shape[2] - LANES :] = small


def finish_kernel(scale, slab_ref, *refs):
    parts, result_ref = [ref[...] for ref in refs[:-1]], refs[-1]
    while len(parts) > 1:
        parts = [parts[at] + parts[at + 1] for at in range(0, len(parts), 2)]
    total = parts[0] * scale
    halves = jnp.concatenate([total, total - total.astype(BF16).astype(F32)], 0)
    count = halves.shape[0] // 8
    wide = jnp.concatenate([halves[8 * index : 8 * index + 8, :] for index in range(count)], 1)
    wide = wide.astype(BF16)
    start, end = slab_ref.shape[2] - (count + 1) * LANES, slab_ref.shape[2] - LANES
    for device in range(slab_ref.shape[0]):
        result_ref[device, :, :start] = slab_ref[device, :, :start]
        result_ref[device, :, start:end] = wide
        result_ref[device, :, end:] = slab_ref[device, :, end:]


def unpack_kernel(per, recv_ref, proj_ref, short_ref, out_ref):
    channels, tokens = proj_ref.shape[1:]
    devices = channels // per
    order = out_ref.shape[1]
    slabs = [recv_ref[device].astype(F32) for device in range(devices)]
    for index in range(3):
        rows = []
        for slab in slabs:
            if index * per < 8:
                rows.append(slab[index * per : (index + 1) * per, :tokens])
            else:
                lanes = slice(tokens, tokens + tokens // 2)
                rows.append(jnp.concatenate([slab[:per, lanes], slab[per : 2 * per, lanes]], 1))
        proj_ref[index] = jnp.concatenate(rows, 0).astype(BF16)
    small = [slab[:, slab.shape[1] - LANES :] for slab in slabs]
    small = [part + pltpu.roll(part, LANES // 2, 1) for part in small]
    out_ref[...] = jnp.concatenate([part[:per, :order] for part in small], 0)
    rows = jnp.concatenate([part[per : 2 * per, :] for part in small], 0).T
    for index in range(3):
        short_ref[index] = rows[3 * index : 3 * index + 3, :]


def in_sum_kernel(sources, recv_ref, sum_ref):
    count = sum_ref.shape[0] // 4
    start = recv_ref.shape[2] - (count + 1) * LANES
    total = recv_ref[0, :, start : start + count * LANES].astype(F32)
    for source in range(1, sources):
        total = total + recv_ref[source, :, start : start + count * LANES].astype(F32)
    total = [total[:, index * LANES : (index + 1) * LANES] for index in range(count)]
    sum_ref[...] = jnp.concatenate(total[: count // 2], 0) + jnp.concatenate(total[count // 2 :], 0)


def in_grad_kernel(own_ref, other_ref, in_ref):
    half, order = in_ref.shape[0] // 2, in_ref.shape[1]
    total = own_ref[...] + other_ref[...]
    in_ref[:half, :] = total[:, :order]
    in_ref[half:, :] = total[:, order:]


def call(kernel, out, limit, in_specs=None, out_specs=None, flops=0, moved=0, **more):
    vmem = pl.BlockSpec(memory_space=pltpu.VMEM)
    return pl.pallas_call(
        kernel,
        out_shape=out,
        in_specs=in_specs,
        out_specs=out_specs if out_specs is not None else jax.tree.map(lambda _: vmem, out),
        compiler_params=pltpu.CompilerParams(vmem_limit_bytes=limit),
        cost_estimate=pl.CostEstimate(flops=flops, bytes_accessed=moved, transcendentals=0),
        **more,
    )


def shards(proj, cotangent, short_w, filter_in, filter_out, rates):
    vmem = pl.BlockSpec(memory_space=pltpu.VMEM)
    hbm = pl.BlockSpec(memory_space=pltpu.HBM)
    channels, tokens = cotangent.shape
    devices = lax.axis_size("seq")
    groups = lax.axis_size("ch")
    length = devices * tokens
    rows = length // LANES
    lows = rows + 8
    features, order = filter_in.shape
    scale = 1.0 / math.sqrt(length)
    per = max(1, channels // devices)
    held = 4 * per
    step = max(8, held)
    width = tokens if 3 * per <= 8 else tokens + tokens // 2
    blocks = max(1, rows // 64)
    block = length // blocks
    small = blocks == 1
    limit = (24 if small else 56) * MIB
    sds = jax.ShapeDtypeStruct
    made = pltpu.VMEM if small else sds
    put = (lambda x: pltpu.with_memory_space_constraint(x, pltpu.VMEM)) if small else (lambda x: x)
    keep = lambda x: pltpu.with_memory_space_constraint(x, pltpu.HBM)

    packed = call(
        functools.partial(pack_kernel, per),
        sds((devices, held, tokens), BF16),
        limit,
        in_specs=[vmem] * 2,
    )(keep(proj), keep(cotangent))
    recv = lax.all_to_all(packed, "seq", split_axis=0, concat_axis=0, tiled=True)

    near, *lane_tables = feature_tables(length, features)
    near = near.reshape(2 * features, blocks, rows // blocks).transpose(1, 0, 2)
    tables = transform_tables(length)
    given = [tables[name] for name in ("first", "last", "middle", "turn")]
    given += [near, *lane_tables]
    given = [jnp.asarray(value) for value in given]
    given += [filter_in, filter_out.T, rates.reshape(1, channels), short_w.transpose(0, 2, 1)]
    hidden = tuple(pltpu.HBM((order, length), BF16) for _ in range(2))
    hidden += ((made if small else pltpu.HBM)((order, length), F32),)
    buffers = [pltpu.VMEM((order, block), kind) for kind in (BF16, BF16, F32)]
    *loaded, envelope, kernel_spec, sine_high, sine_low, cosine = call(
        functools.partial(filter_kernel, per, length, blocks),
        tuple(made(value.shape, value.dtype) for value in given)
        + (made((per * rows, LANES), F32), made((per * lows, 2 * LANES), F32))
        + hidden,
        limit,
        in_specs=[hbm] * len(given),
        out_specs=(vmem,) * (len(given) + 2) + (hbm, hbm, vmem if small else hbm),
        scratch_shapes=(buffers[:2] if small else buffers)
        + [
            pltpu.VMEM((8, block), F32),
            pltpu.VMEM((rows * 8, LANES), F32),
            pltpu.SemaphoreType.DMA((len(given),)),
            pltpu.SemaphoreType.DMA((3,)),
        ],
        flops=8 * length * order * 3 * features,
        moved=length * order * 8,
    )(*[keep(value) for value in given])
    first, last, middle, turn, _, _, grad_lane, grad_row = map(put, loaded[:8])
    _, out_rows, _, short_taps = map(put, loaded[8:])

    raw, mixed, spec, weighted, in_grad, *sines = call(
        functools.partial(signal_kernel, per, blocks),
        (
            made((rows * step, LANES), F32),
            made((2 * per, rows, LANES), F32),
            made((2 * per * lows, 2 * LANES), F32),
            made((8, length), F32),
            sds((features // 2, 2 * order), F32),
        )
        + ((made((order, length), BF16),) * 2 if small else ()),
        limit,
        in_specs=[vmem] * 10 + [vmem if small else hbm] + [hbm] * 2,
        scratch_shapes=([] if small else buffers[2:])
        + [pltpu.VMEM((rows * 8, LANES), F32), pltpu.SemaphoreType.DMA((2,))],
        flops=400 * length * LANES,
    )(
        put(recv),
        put(envelope),
        first,
        last,
        middle,
        turn,
        grad_lane,
        grad_row,
        out_rows,
        short_taps,
        put(cosine) if small else keep(cosine),
        keep(sine_high),
        keep(sine_low),
    )
    if not small:
        sines = [sine_high, sine_low]

    def exchange(value, by):
        return lax.ppermute(value, "ch", [(i, i ^ by) for i in range(groups)])

    steps = [1 << step for step in range(1, groups.bit_length() - 1)][::-1]
    for by in steps[:-1]:
        in_grad = in_grad + exchange(in_grad, by)
    others = [exchange(in_grad, by) for by in steps[-1:]]
    shape = (devices, 8, width + features // 8 * LANES + LANES)
    slab = call(
        functools.partial(proj_grad_kernel, per, blocks, scale),
        made(shape, BF16),
        limit,
        in_specs=[vmem] * 9 + [vmem if small else hbm] * 2,
        scratch_shapes=[pltpu.VMEM((rows * max(8, held), LANES), F32)]
        + ([] if small else [*buffers[:2], pltpu.SemaphoreType.DMA((2,))]),
        flops=400 * length * LANES,
    )(
        short_taps,
        put(raw),
        put(mixed),
        put(spec),
        put(kernel_spec),
        put(weighted),
        last,
        middle,
        turn,
        *[put(value) if small else keep(value) for value in sines],
    )
    slab = call(
        functools.partial(finish_kernel, scale),
        sds(shape, BF16),
        limit,
        in_specs=[vmem] * (2 + len(others)),
    )(put(slab), in_grad, *others)

    back = lax.all_to_all(slab, "seq", split_axis=0, concat_axis=0, tiled=True)
    in_sum = call(
        functools.partial(in_sum_kernel, channels // per),
        made((features // 2, 2 * order), F32),
        limit,
        in_specs=[vmem],
    )(back)
    in_other = exchange(in_sum, 1)
    grad_proj, grad_short, grad_out = call(
        functools.partial(unpack_kernel, per),
        (
            sds((3, channels, tokens), BF16),
            sds((3, 3, channels), F32),
            sds((channels, order), F32),
        ),
        limit,
        in_specs=[vmem],
    )(back)
    grad_in = call(
        in_grad_kernel,
        sds((features, order), F32),
        limit,
        in_specs=[vmem] * 2,
    )(put(in_sum), in_other)
    return grad_proj, grad_short.transpose(0, 2, 1), grad_out.T, grad_in


def solution(mesh):
    placed = (
        P(None, "ch", "seq"),
        P("ch", "seq"),
        P(None, "ch", None),
        P(),
        P(None, "ch"),
        P("ch"),
    )
    return jax.shard_map(
        shards,
        mesh=mesh,
        in_specs=placed,
        out_specs=(P(None, "ch", "seq"), P(None, "ch", None), P(None, "ch"), P()),
        check_vma=False,
    )
```

```python
import functools
import math

import jax
import jax.numpy as jnp
import ml_dtypes
import numpy as np
from jax import lax
from jax.experimental import pallas as pl
from jax.experimental.pallas import tpu as pltpu
from jax.sharding import PartitionSpec as P

F32 = jnp.float32
BF16 = jnp.bfloat16
LANES = 128
MIB = 1024 * 1024


def split(value):
    high = value.astype(BF16)
    return high, (value - high.astype(F32)).astype(BF16)


def np_split(value):
    high = value.astype(ml_dtypes.bfloat16)
    return high, (value - high.astype(np.float64)).astype(ml_dtypes.bfloat16)


def dot(left, right):
    return jnp.dot(left, right, preferred_element_type=F32)


def dot_first(left, right):
    return lax.dot_general(left, right, (((0,), (0,)), ((), ())), preferred_element_type=F32)


def dot_last(left, right):
    return lax.dot_general(left, right, (((1,), (1,)), ((), ())), preferred_element_type=F32)


@functools.lru_cache(maxsize=None)
def transform_tables(length):
    rows = length // LANES
    points = 2 * length
    lows = rows + 8
    low = np.arange(lows)
    row = np.arange(rows)
    lane = np.arange(LANES)
    angle = 2.0 * np.pi * ((low[:, None] * row[None, :]) % (2 * rows)) / (2 * rows)
    kept = (low <= rows)[:, None]
    first = np.concatenate([np.cos(angle) * kept, -np.sin(angle) * kept], 0)
    weight = np.where((low == 0) | (low == rows), 1.0, 2.0)[:, None] / points
    last = np.concatenate([np.cos(angle) * kept * weight, -np.sin(angle) * kept * weight], 0).T
    turn = 2.0 * np.pi * ((low[:, None] * lane[None, :]) % points) / points
    lane_angle = 2.0 * np.pi * ((lane[:, None] * lane[None, :]) % LANES) / LANES
    cosine, sine = np.cos(lane_angle), np.sin(lane_angle)
    middle = np.block([[cosine, -sine], [sine, cosine]])
    first_high, first_low = np_split(first)
    last_high, last_low = np_split(last)
    middle_high, middle_low = np_split(middle)
    return dict(
        first=np.concatenate([first_high, first_high, first_low], 1),
        last=np.concatenate([last_high, last_high, last_low], 1),
        middle=np.concatenate([middle_high, middle_low], 0),
        turn=np.concatenate([np.cos(turn), np.sin(turn)], 0).astype(np.float32),
    )


@functools.lru_cache(maxsize=None)
def feature_tables(length, feature_count):
    rows = length // LANES
    feature = np.arange(feature_count)
    multiplier = (1 + feature // 2 * 499) % length
    row_angle = 2.0 * np.pi * ((multiplier[:, None] * LANES * np.arange(rows)[None, :]) % length) / length
    lane_angle = 2.0 * np.pi * ((multiplier[:, None] * np.arange(LANES)[None, :]) % length) / length
    even = (feature % 2 == 0)[:, None]
    near = np.where(even, np.cos(row_angle), np.sin(row_angle))
    far = np.where(even, -np.sin(row_angle), np.cos(row_angle))
    lane = np.concatenate([np.cos(lane_angle), np.sin(lane_angle)], 0)
    lane_high, lane_low = np_split(lane.T)
    grad_lane = np.block([[lane_high, lane_low], [lane_high, np.zeros_like(lane_low)]])
    grad_row = np.concatenate([near, far, near, far], 0).T
    return (
        np.concatenate([near, far], 0).astype(np.float32),
        lane.astype(np.float32),
        grad_lane.astype(ml_dtypes.bfloat16),
        grad_row.astype(np.float32),
    )


def middle_dot(value, middle_ref):
    high, low = split(value)
    size = 2 * LANES
    table_high, table_low = middle_ref[:size, :], middle_ref[size:, :]
    return dot(high, table_high) + dot(high, table_low) + dot(low, table_high)


def forward(signals, first_ref, middle_ref, turn_ref):
    lows = turn_ref.shape[0] // 2
    high, low = split(jnp.concatenate(signals, 1))
    partial = dot(first_ref[...], jnp.concatenate([high, low, high], 0))
    cosine, sine = turn_ref[:lows, :], turn_ref[lows:, :]
    turned = []
    for index in range(len(signals)):
        real = partial[:lows, index * LANES : (index + 1) * LANES]
        imag = partial[lows:, index * LANES : (index + 1) * LANES]
        turned.append(
            jnp.concatenate([real * cosine + imag * sine, imag * cosine - real * sine], 1)
        )
    return middle_dot(jnp.concatenate(turned, 0), middle_ref)


def backward(spectra, last_ref, middle_ref, turn_ref):
    lows = turn_ref.shape[0] // 2
    swapped = jnp.concatenate([jnp.concatenate([imag, real], 1) for real, imag in spectra], 0)
    partial = middle_dot(swapped, middle_ref)
    cosine, sine = turn_ref[:lows, :], turn_ref[lows:, :]
    turned = []
    for index in range(len(spectra)):
        imag = partial[index * lows : (index + 1) * lows, :LANES]
        real = partial[index * lows : (index + 1) * lows, LANES:]
        turned.append(
            jnp.concatenate([real * cosine - imag * sine, imag * cosine + real * sine], 0)
        )
    high, low = split(jnp.concatenate(turned, 1))
    result = dot(last_ref[...], jnp.concatenate([high, low, high], 0))
    return [result[:, index * LANES : (index + 1) * LANES] for index in range(len(spectra))]


def later(value):
    turned = pltpu.roll(value, 1, 1)
    carried = pltpu.roll(turned, 1, 0)
    row = lax.broadcasted_iota(jnp.int32, value.shape, 0)
    lane = lax.broadcasted_iota(jnp.int32, value.shape, 1)
    carried = jnp.where(row == 0, 0.0, carried)
    return jnp.where(lane == 0, carried, turned)


def sooner(value):
    rows = value.shape[0]
    turned = pltpu.roll(value, LANES - 1, 1)
    carried = pltpu.roll(turned, rows - 1, 0)
    row = lax.broadcasted_iota(jnp.int32, value.shape, 0)
    lane = lax.broadcasted_iota(jnp.int32, value.shape, 1)
    carried = jnp.where(row == rows - 1, 0.0, carried)
    return jnp.where(lane == LANES - 1, carried, turned)


def sine_cosine(half_angle):
    turns = jnp.round(half_angle * (1.0 / math.pi))
    rest = half_angle - turns * 3.140625
    rest = rest - turns * 9.67653589793e-4
    square = rest * rest
    sine = 2.59045638e-06
    for coefficient in (-1.98008819e-04, 8.33289957e-03, -1.66666476e-01, 9.99999977e-01):
        sine = sine * square + coefficient
    cosine = 2.31536124e-05
    for coefficient in (-1.38536905e-03, 4.16635829e-02, -4.99999053e-01, 9.99999953e-01):
        cosine = cosine * square + coefficient
    sine = sine * rest
    twice = sine + sine
    return twice * cosine, 1.0 - twice * sine


def first_channel(per, channels):
    return lax.axis_index("seq") * per % channels


def own_rows(per, out_ref):
    channels = out_ref.shape[0]
    start = first_channel(per, channels)
    return pltpu.roll(out_ref[...], lax.rem(channels - start, channels), 0)[:8, :]


def tap_rows(short_ref):
    return jnp.concatenate([short_ref[index] for index in range(3)], 0)


def own_columns(per, value):
    channels = value.shape[1]
    start = first_channel(per, channels)
    turned = pltpu.roll(value, lax.rem(channels - start, channels), 1)
    return [turned[:, channel : channel + 1] for channel in range(per)]


def small_expm1(value):
    total = 1.0
    for divisor in (7.0, 6.0, 5.0, 4.0, 3.0, 2.0):
        total = 1.0 + total * value * (1.0 / divisor)
    return total * value


def pack_kernel(per, proj_ref, cot_ref, out_ref):
    channels = cot_ref.shape[0]
    whole = [proj_ref[index].astype(F32) for index in range(3)] + [cot_ref[...].astype(F32)]
    for device in range(out_ref.shape[0]):
        start = device * per % channels
        rows = jnp.concatenate([part[start : start + per, :] for part in whole], 0)
        out_ref[device] = rows.astype(BF16)


def block_features(table, lane_ref):
    count = lane_ref.shape[0] // 2
    lane_cos, lane_sin = lane_ref[:count, :], lane_ref[count:, :]
    near, far = table[:count, :], table[count:, :]
    rows = range(table.shape[1])
    blocks = [near[:, row : row + 1] * lane_cos + far[:, row : row + 1] * lane_sin for row in rows]
    return split(jnp.concatenate(blocks, 1))


def in_blocks(blocks, body):
    if blocks == 1:
        body(0)
    else:
        lax.fori_loop(0, blocks, lambda index, carry: (body(index), carry)[1], 0)


def block_copies(index, block, here, there, semaphores, outward):
    columns = pl.ds(pl.multiple_of(index * block, LANES), block)
    pairs = [(near, far.at[:, columns]) for near, far in zip(here, there, strict=True)]
    return [
        pltpu.make_async_copy(*(pair if outward else pair[::-1]), semaphores.at[at])
        for at, pair in enumerate(pairs)
    ]


def filter_kernel(per, length, blocks, *refs):
    given, loaded = refs[:12], refs[12:24]
    env_ref, spec_ref = refs[24:26]
    hidden_refs, buffers = refs[26:29], list(refs[29:-4])
    mod_ref, stage_ref, load_semaphores, out_semaphores = refs[-4:]
    loads = [
        pltpu.make_async_copy(source, target, load_semaphores.at[index])
        for index, (source, target) in enumerate(zip(given, loaded, strict=True))
    ]
    for load in loads:
        load.start()
    for load in loads:
        load.wait()
    first_ref, _, middle_ref, turn_ref, near_ref, lane_ref, _, _ = loaded[:8]
    in_ref, out_ref, rates_ref, _ = loaded[8:]
    rows = length // LANES
    block = length // blocks
    block_rows = rows // blocks
    if blocks == 1:
        buffers, hidden_refs = buffers + [hidden_refs[2]], hidden_refs[:2]
    sine_high_ref, sine_low_ref, cosine_ref = buffers
    buffers = buffers[: len(hidden_refs)]
    in_high, in_low = split(in_ref[...] * 0.5)
    in_weights = jnp.concatenate([in_high, in_high, in_low], 0)
    out_high, out_low = split(own_rows(per, out_ref))
    out_weights = jnp.concatenate([out_high, out_high, out_low], 1)

    def hidden_block(index):
        high, low = block_features(near_ref[index], lane_ref)
        half_angle = dot_first(in_weights, jnp.concatenate([high, low, high], 0))
        sine, cosine = sine_cosine(half_angle)
        cosine_ref[...] = cosine
        high, low = split(sine)
        sine_high_ref[...] = high
        sine_low_ref[...] = low
        copies = block_copies(index, block, buffers, hidden_refs, out_semaphores, True)
        for copy in copies:
            copy.start()
        mod_ref[...] = dot(out_weights, jnp.concatenate([high, low, high], 0))
        for row in range(block_rows):
            at = pl.multiple_of((index * block_rows + row) * 8, 8)
            stage_ref[pl.ds(at, 8), :] = mod_ref[:, row * LANES : (row + 1) * LANES]
        if blocks > 1:
            for copy in copies:
                copy.wait()

    in_blocks(blocks, hidden_block)
    rates = own_columns(per, rates_ref[...])
    position = lax.broadcasted_iota(jnp.int32, (rows, LANES), 0) * LANES
    position = position + lax.broadcasted_iota(jnp.int32, (rows, LANES), 1)
    relative = position.astype(F32) * (1.0 / length)
    kernels = []
    for channel in range(per):
        rate = -2.0 * jnp.broadcast_to(rates[channel], (8, LANES))
        inverse = jnp.sqrt(small_expm1(rate * (1.0 / length)) / (jnp.exp(rate) - 1.0))
        envelope = jnp.exp(0.5 * rate[:1, :] * relative) * inverse[:1, :]
        env_ref[channel * rows : (channel + 1) * rows, :] = envelope
        kernels.append(envelope * stage_ref[pl.ds(channel, rows, stride=8), :])
    spec_ref[...] = forward(kernels, first_ref, middle_ref, turn_ref)
    if blocks == 1:
        for copy in block_copies(0, block, buffers, hidden_refs, out_semaphores, True):
            copy.wait()


def signal_kernel(per, blocks, *refs):
    recv_ref, env_ref, first_ref, last_ref, middle_ref, turn_ref = refs[:6]
    lane_ref, row_ref, out_ref, short_ref, cosine_ref = refs[6:11]
    sines = refs[11:13]
    raw_ref, mixed_ref, spec_ref, weighted_ref, in_grad_ref = refs[13:18]
    stage_ref, semaphores = refs[-2:]
    devices, held, tokens = recv_ref.shape
    rows = devices * tokens // LANES
    block = rows * LANES // blocks
    block_rows = rows // blocks
    step = raw_ref.shape[0] // rows
    lows = turn_ref.shape[0] // 2
    ahead = []
    if blocks == 1:
        ahead = [
            pltpu.make_async_copy(source, target, semaphores.at[at])
            for at, source, target in zip((0, 1), sines, refs[18:20], strict=True)
        ]
        for copy in ahead:
            copy.start()
    taps = own_columns(per, tap_rows(short_ref))
    for device in range(devices):
        for part in range(tokens // LANES):
            at = (device * (tokens // LANES) + part) * step
            raw_ref[at : at + held, :] = recv_ref[
                device, :, part * LANES : (part + 1) * LANES
            ].astype(F32)
    gated, grads = [], []
    for channel in range(per):
        mixed = []
        for index in range(3):
            base = raw_ref[pl.ds(index * per + channel, rows, stride=step), :]
            total = taps[channel][3 * index : 3 * index + 1, :] * base
            for tap in (1, 2):
                base = later(base)
                total = total + taps[channel][3 * index + tap : 3 * index + tap + 1, :] * base
            mixed.append(total)
        cotangent = raw_ref[pl.ds(3 * per + channel, rows, stride=step), :]
        mixed_ref[2 * channel] = mixed[1]
        mixed_ref[2 * channel + 1] = mixed[2]
        gated.append(mixed[1] * mixed[2])
        grads.append(cotangent * mixed[0])
    spectra = forward(gated + grads, first_ref, middle_ref, turn_ref)
    spec_ref[...] = spectra
    products = []
    for channel in range(per):
        at, other = channel * lows, (per + channel) * lows
        gated_real, gated_imag = spectra[at : at + lows, :LANES], spectra[at : at + lows, LANES:]
        grad_real, grad_imag = (
            spectra[other : other + lows, :LANES],
            spectra[other : other + lows, LANES:],
        )
        products.append(
            (
                grad_real * gated_real + grad_imag * gated_imag,
                grad_imag * gated_real - grad_real * gated_imag,
            )
        )
    results = backward(products, last_ref, middle_ref, turn_ref)
    if per < 8:
        stage_ref[...] = jnp.zeros_like(stage_ref)
    for channel in range(per):
        weighted = results[channel] * env_ref[channel * rows : (channel + 1) * rows, :]
        stage_ref[pl.ds(channel, rows, stride=8), :] = weighted
    out_rows = own_rows(per, out_ref)
    out_rounded = out_rows.astype(BF16).astype(F32)
    weights = jnp.concatenate([out_rows, out_rows, out_rows - out_rounded], 0).astype(BF16)
    order, features = out_ref.shape[1], lane_ref.shape[1] // 4
    if blocks > 1:
        in_grad_ref[...] = jnp.zeros_like(in_grad_ref)

    def add_block(index):
        cosine_here = cosine_ref
        if blocks > 1:
            cosine_here = refs[-3]
            (copy,) = block_copies(index, block, [cosine_here], [cosine_ref], semaphores, False)
            copy.start()
            copy.wait()
        parts = []
        for row in range(block_rows):
            at = pl.multiple_of((index * block_rows + row) * 8, 8)
            parts.append(stage_ref[pl.ds(at, 8), :])
        weighted = jnp.concatenate(parts, 1)
        weighted_ref[:, pl.ds(pl.multiple_of(index * block, LANES), block)] = weighted
        rounded = weighted.astype(BF16).astype(F32)
        terms = jnp.concatenate([weighted, weighted - rounded, weighted], 0).astype(BF16)
        grad = dot_first(weights, terms)
        high, low = split(grad * cosine_here[...])
        parts = []
        for row in range(block_rows):
            lanes = slice(row * LANES, (row + 1) * LANES)
            parts.append(jnp.concatenate([high[:, lanes], low[:, lanes]], 1))
        parts = dot(jnp.concatenate(parts, 0), lane_ref[...])
        factors = row_ref[pl.ds(pl.multiple_of(index * block_rows, 8), block_rows), :]
        totals = []
        height = order // 2
        for start in range(0, order, height):
            total = jnp.zeros((height, LANES), F32)
            for row in range(block_rows):
                at = row * order + start
                total = total + parts[at : at + height, :] * factors[row : row + 1, :]
            totals.append(total)
        total = jnp.concatenate(totals, 0)
        total = total + pltpu.roll(total, 2 * features, 1)
        total = total + pltpu.roll(total, features, 1)
        total = total.T
        half = features // 2
        total = jnp.concatenate([total[:half, :], total[half:features, :]], 1)
        if blocks > 1:
            total = total + in_grad_ref[...]
        in_grad_ref[...] = total

    in_blocks(blocks, add_block)
    for copy in ahead:
        copy.wait()


def proj_grad_kernel(
    per,
    blocks,
    scale,
    short_ref,
    raw_ref,
    mixed_ref,
    spec_ref,
    kernel_spec_ref,
    weighted_ref,
    last_ref,
    middle_ref,
    turn_ref,
    high_ref,
    low_ref,
    slab_ref,
    stage_ref,
    high_buffer=None,
    low_buffer=None,
    semaphores=None,
):
    order, block = high_ref.shape[0], high_ref.shape[1] // blocks
    devices = slab_ref.shape[0]
    rows = weighted_ref.shape[1] // LANES
    tokens = rows // devices * LANES
    held = stage_ref.shape[0] // rows
    taps = own_columns(per, tap_rows(short_ref))
    step = raw_ref.shape[0] // rows
    lows = turn_ref.shape[0] // 2
    products = []
    for sign in (1.0, -1.0):
        for channel in range(per):
            at = (channel if sign > 0 else per + channel) * lows
            real, imag = spec_ref[at : at + lows, :LANES], spec_ref[at : at + lows, LANES:]
            at = channel * lows
            kernel_real = kernel_spec_ref[at : at + lows, :LANES]
            kernel_imag = sign * kernel_spec_ref[at : at + lows, LANES:]
            products.append(
                (
                    real * kernel_real - imag * kernel_imag,
                    real * kernel_imag + imag * kernel_real,
                )
            )
    results = backward(products, last_ref, middle_ref, turn_ref)
    sums = [None] * (3 * per)
    for channel in range(per):
        cotangent = raw_ref[pl.ds(3 * per + channel, rows, stride=step), :]
        grad_mixed = (
            cotangent * results[channel],
            results[per + channel] * mixed_ref[2 * channel + 1],
            results[per + channel] * mixed_ref[2 * channel],
        )
        for index in range(3):
            base = raw_ref[pl.ds(index * per + channel, rows, stride=step), :]
            grad = grad_mixed[index]
            total = taps[channel][3 * index : 3 * index + 1, :] * grad
            parts = [jnp.sum(grad * base, axis=0, keepdims=True)]
            moved = grad
            for tap in (1, 2):
                base = later(base)
                moved = sooner(moved)
                total = total + taps[channel][3 * index + tap : 3 * index + tap + 1, :] * moved
                parts.append(jnp.sum(grad * base, axis=0, keepdims=True))
            sums[index * per + channel] = jnp.concatenate(parts, 0)
            stage_ref[pl.ds(index * per + channel, rows, stride=held), :] = total
    parts = tokens // LANES
    for device in range(devices):
        blocks_here = []
        for part in range(parts):
            at = (device * parts + part) * held
            blocks_here.append(stage_ref[at : at + held, :])
        for part in range(parts):
            lanes = slice(part * LANES, (part + 1) * LANES)
            slab_ref[device, :, lanes] = blocks_here[part][:8, :].astype(BF16)
        if held > 8:
            for part in range(parts // 2):
                lanes = slice(tokens + part * LANES, tokens + (part + 1) * LANES)
                pair = [blocks_here[part][8:12, :], blocks_here[part + parts // 2][8:12, :]]
                slab_ref[device, :, lanes] = jnp.concatenate(pair, 0).astype(BF16)
    row = lax.broadcasted_iota(jnp.int32, (8, LANES), 0)
    lane = lax.broadcasted_iota(jnp.int32, (8, LANES), 1)
    small = jnp.zeros((8, LANES), F32)
    for place in range(3 * per):
        index, channel = place // per, place % per
        total = jnp.sum(sums[place], axis=1, keepdims=True) * scale
        for tap in range(3):
            at = (row == per + channel) & (lane == 3 * index + tap)
            small = jnp.where(at, total[tap : tap + 1, :], small)
    out_grad = jnp.zeros((order, 2 * LANES), F32)
    for index in range(blocks):
        high_here, low_here = high_ref, low_ref
        if blocks > 1:
            high_here, low_here = high_buffer, low_buffer
            copies = block_copies(
                index, block, [high_here, low_here], [high_ref, low_ref], semaphores, False
            )
            for copy in copies:
                copy.start()
            for copy in copies:
                copy.wait()
        weighted = weighted_ref[:, index * block : (index + 1) * block]
        rounded = weighted.astype(BF16).astype(F32)
        both = jnp.concatenate([weighted, weighted - rounded], 0).astype(BF16)
        total = dot_last(high_here[...], both)
        total = total[:, :8] + total[:, 8:] + dot_last(low_here[...], both)[:, :8]
        out_grad = out_grad + jnp.concatenate([total, jnp.zeros((order, 2 * LANES - 8), F32)], 1)
    out_grad = jnp.concatenate([out_grad[:, :LANES], jnp.zeros((LANES - order, LANES), F32)], 0)
    out_grad = out_grad.T[:8, :] * scale
    small = jnp.where(row < per, out_grad, small)
    rest = pltpu.roll(small - small.astype(BF16).astype(F32), LANES // 2, 1)
    small = jnp.where(lane < LANES // 2, small, rest).astype(BF16)
    for device in range(devices):
        slab_ref[device, :, slab_ref.shape[2] - LANES :] = small


def finish_kernel(scale, slab_ref, *refs):
    parts, result_ref = [ref[...] for ref in refs[:-1]], refs[-1]
    while len(parts) > 1:
        parts = [parts[at] + parts[at + 1] for at in range(0, len(parts), 2)]
    total = parts[0] * scale
    halves = jnp.concatenate([total, total - total.astype(BF16).astype(F32)], 0)
    count = halves.shape[0] // 8
    wide = jnp.concatenate([halves[8 * index : 8 * index + 8, :] for index in range(count)], 1)
    wide = wide.astype(BF16)
    start, end = slab_ref.shape[2] - (count + 1) * LANES, slab_ref.shape[2] - LANES
    for device in range(slab_ref.shape[0]):
        result_ref[device, :, :start] = slab_ref[device, :, :start]
        result_ref[device, :, start:end] = wide
        result_ref[device, :, end:] = slab_ref[device, :, end:]


def unpack_kernel(per, recv_ref, proj_ref, short_ref, out_ref):
    channels, tokens = proj_ref.shape[1:]
    devices = channels // per
    order = out_ref.shape[1]
    slabs = [recv_ref[device].astype(F32) for device in range(devices)]
    for index in range(3):
        rows = []
        for slab in slabs:
            if index * per < 8:
                rows.append(slab[index * per : (index + 1) * per, :tokens])
            else:
                lanes = slice(tokens, tokens + tokens // 2)
                rows.append(jnp.concatenate([slab[:per, lanes], slab[per : 2 * per, lanes]], 1))
        proj_ref[index] = jnp.concatenate(rows, 0).astype(BF16)
    small = [slab[:, slab.shape[1] - LANES :] for slab in slabs]
    small = [part + pltpu.roll(part, LANES // 2, 1) for part in small]
    out_ref[...] = jnp.concatenate([part[:per, :order] for part in small], 0)
    rows = jnp.concatenate([part[per : 2 * per, :] for part in small], 0).T
    for index in range(3):
        short_ref[index] = rows[3 * index : 3 * index + 3, :]


def in_sum_kernel(sources, recv_ref, sum_ref):
    count = sum_ref.shape[0] // 4
    start = recv_ref.shape[2] - (count + 1) * LANES
    total = recv_ref[0, :, start : start + count * LANES].astype(F32)
    for source in range(1, sources):
        total = total + recv_ref[source, :, start : start + count * LANES].astype(F32)
    total = [total[:, index * LANES : (index + 1) * LANES] for index in range(count)]
    sum_ref[...] = jnp.concatenate(total[: count // 2], 0) + jnp.concatenate(total[count // 2 :], 0)


def in_grad_kernel(own_ref, other_ref, in_ref):
    half, order = in_ref.shape[0] // 2, in_ref.shape[1]
    total = own_ref[...] + other_ref[...]
    in_ref[:half, :] = total[:, :order]
    in_ref[half:, :] = total[:, order:]


def call(kernel, out, limit, in_specs=None, out_specs=None, flops=0, moved=0, **more):
    vmem = pl.BlockSpec(memory_space=pltpu.VMEM)
    return pl.pallas_call(
        kernel,
        out_shape=out,
        in_specs=in_specs,
        out_specs=out_specs if out_specs is not None else jax.tree.map(lambda _: vmem, out),
        compiler_params=pltpu.CompilerParams(vmem_limit_bytes=limit),
        cost_estimate=pl.CostEstimate(flops=flops, bytes_accessed=moved, transcendentals=0),
        **more,
    )


def shards(proj, cotangent, short_w, filter_in, filter_out, rates):
    vmem = pl.BlockSpec(memory_space=pltpu.VMEM)
    hbm = pl.BlockSpec(memory_space=pltpu.HBM)
    channels, tokens = cotangent.shape
    devices = lax.axis_size("seq")
    groups = lax.axis_size("ch")
    length = devices * tokens
    rows = length // LANES
    lows = rows + 8
    features, order = filter_in.shape
    scale = 1.0 / math.sqrt(length)
    per = max(1, channels // devices)
    held = 4 * per
    step = max(8, held)
    width = tokens if 3 * per <= 8 else tokens + tokens // 2
    blocks = max(1, rows // 64)
    block = length // blocks
    small = blocks == 1
    limit = (24 if small else 56) * MIB
    sds = jax.ShapeDtypeStruct
    made = pltpu.VMEM if small else sds
    put = (lambda x: pltpu.with_memory_space_constraint(x, pltpu.VMEM)) if small else (lambda x: x)
    keep = lambda x: pltpu.with_memory_space_constraint(x, pltpu.HBM)

    packed = call(
        functools.partial(pack_kernel, per),
        sds((devices, held, tokens), BF16),
        limit,
        in_specs=[vmem] * 2,
    )(keep(proj), keep(cotangent))
    recv = lax.all_to_all(packed, "seq", split_axis=0, concat_axis=0, tiled=True)

    near, *lane_tables = feature_tables(length, features)
    near = near.reshape(2 * features, blocks, rows // blocks).transpose(1, 0, 2)
    tables = transform_tables(length)
    given = [tables[name] for name in ("first", "last", "middle", "turn")]
    given += [near, *lane_tables]
    given = [jnp.asarray(value) for value in given]
    given += [filter_in, filter_out.T, rates.reshape(1, channels), short_w.transpose(0, 2, 1)]
    hidden = tuple(pltpu.HBM((order, length), BF16) for _ in range(2))
    hidden += ((made if small else pltpu.HBM)((order, length), F32),)
    buffers = [pltpu.VMEM((order, block), kind) for kind in (BF16, BF16, F32)]
    *loaded, envelope, kernel_spec, sine_high, sine_low, cosine = call(
        functools.partial(filter_kernel, per, length, blocks),
        tuple(made(value.shape, value.dtype) for value in given)
        + (made((per * rows, LANES), F32), made((per * lows, 2 * LANES), F32))
        + hidden,
        limit,
        in_specs=[hbm] * len(given),
        out_specs=(vmem,) * (len(given) + 2) + (hbm, hbm, vmem if small else hbm),
        scratch_shapes=(buffers[:2] if small else buffers)
        + [
            pltpu.VMEM((8, block), F32),
            pltpu.VMEM((rows * 8, LANES), F32),
            pltpu.SemaphoreType.DMA((len(given),)),
            pltpu.SemaphoreType.DMA((3,)),
        ],
        flops=8 * length * order * 3 * features,
        moved=length * order * 8,
    )(*[keep(value) for value in given])
    first, last, middle, turn, _, _, grad_lane, grad_row = map(put, loaded[:8])
    _, out_rows, _, short_taps = map(put, loaded[8:])

    raw, mixed, spec, weighted, in_grad, *sines = call(
        functools.partial(signal_kernel, per, blocks),
        (
            made((rows * step, LANES), F32),
            made((2 * per, rows, LANES), F32),
            made((2 * per * lows, 2 * LANES), F32),
            made((8, length), F32),
            sds((features // 2, 2 * order), F32),
        )
        + ((made((order, length), BF16),) * 2 if small else ()),
        limit,
        in_specs=[vmem] * 10 + [vmem if small else hbm] + [hbm] * 2,
        scratch_shapes=([] if small else buffers[2:])
        + [pltpu.VMEM((rows * 8, LANES), F32), pltpu.SemaphoreType.DMA((2,))],
        flops=400 * length * LANES,
    )(
        put(recv),
        put(envelope),
        first,
        last,
        middle,
        turn,
        grad_lane,
        grad_row,
        out_rows,
        short_taps,
        put(cosine) if small else keep(cosine),
        keep(sine_high),
        keep(sine_low),
    )
    if not small:
        sines = [sine_high, sine_low]

    def exchange(value, by):
        return lax.ppermute(value, "ch", [(i, i ^ by) for i in range(groups)])

    steps = [1 << step for step in range(1, groups.bit_length() - 1)][::-1]
    for by in steps[:-1]:
        in_grad = in_grad + exchange(in_grad, by)
    others = [exchange(in_grad, by) for by in steps[-1:]]
    shape = (devices, 8, width + features // 8 * LANES + LANES)
    slab = call(
        functools.partial(proj_grad_kernel, per, blocks, scale),
        made(shape, BF16),
        limit,
        in_specs=[vmem] * 9 + [vmem if small else hbm] * 2,
        scratch_shapes=[pltpu.VMEM((rows * max(8, held), LANES), F32)]
        + ([] if small else [*buffers[:2], pltpu.SemaphoreType.DMA((2,))]),
        flops=400 * length * LANES,
    )(
        short_taps,
        put(raw),
        put(mixed),
        put(spec),
        put(kernel_spec),
        put(weighted),
        last,
        middle,
        turn,
        *[put(value) if small else keep(value) for value in sines],
    )
    slab = call(
        functools.partial(finish_kernel, scale),
        sds(shape, BF16),
        limit,
        in_specs=[vmem] * (2 + len(others)),
    )(put(slab), in_grad, *others)

    back = lax.all_to_all(slab, "seq", split_axis=0, concat_axis=0, tiled=True)
    in_sum = call(
        functools.partial(in_sum_kernel, channels // per),
        made((features // 2, 2 * order), F32),
        limit,
        in_specs=[vmem],
    )(back)
    in_other = exchange(in_sum, 1)
    grad_proj, grad_short, grad_out = call(
        functools.partial(unpack_kernel, per),
        (
            sds((3, channels, tokens), BF16),
            sds((3, 3, channels), F32),
            sds((channels, order), F32),
        ),
        limit,
        in_specs=[vmem],
    )(back)
    grad_in = call(
        in_grad_kernel,
        sds((features, order), F32),
        limit,
        in_specs=[vmem] * 2,
    )(put(in_sum), in_other)
    return grad_proj, grad_short.transpose(0, 2, 1), grad_out.T, grad_in


def solution(mesh):
    placed = (
        P(None, "ch", "seq"),
        P("ch", "seq"),
        P(None, "ch", None),
        P(),
        P(None, "ch"),
        P("ch"),
    )
    return jax.shard_map(
        shards,
        mesh=mesh,
        in_specs=placed,
        out_specs=(P(None, "ch", "seq"), P(None, "ch", None), P(None, "ch"), P()),
        check_vma=False,
    )
```

```python
import functools
import math

import jax
import jax.numpy as jnp
import ml_dtypes
import numpy as np
from jax import lax
from jax.experimental import pallas as pl
from jax.experimental.pallas import tpu as pltpu
from jax.sharding import PartitionSpec as P

F32 = jnp.float32
BF16 = jnp.bfloat16
LANES = 128
MIB = 1024 * 1024


def split(value):
    high = value.astype(BF16)
    return high, (value - high.astype(F32)).astype(BF16)


def np_split(value):
    high = value.astype(ml_dtypes.bfloat16)
    return high, (value - high.astype(np.float64)).astype(ml_dtypes.bfloat16)


def dot(left, right):
    return jnp.dot(left, right, preferred_element_type=F32)


def dot_first(left, right):
    return lax.dot_general(left, right, (((0,), (0,)), ((), ())), preferred_element_type=F32)


def dot_last(left, right):
    return lax.dot_general(left, right, (((1,), (1,)), ((), ())), preferred_element_type=F32)


@functools.lru_cache(maxsize=None)
def transform_tables(length):
    rows = length // LANES
    points = 2 * length
    lows = rows + 8
    low = np.arange(lows)
    row = np.arange(rows)
    lane = np.arange(LANES)
    angle = 2.0 * np.pi * ((low[:, None] * row[None, :]) % (2 * rows)) / (2 * rows)
    kept = (low <= rows)[:, None]
    first = np.concatenate([np.cos(angle) * kept, -np.sin(angle) * kept], 0)
    weight = np.where((low == 0) | (low == rows), 1.0, 2.0)[:, None] / points
    last = np.concatenate([np.cos(angle) * kept * weight, -np.sin(angle) * kept * weight], 0).T
    turn = 2.0 * np.pi * ((low[:, None] * lane[None, :]) % points) / points
    lane_angle = 2.0 * np.pi * ((lane[:, None] * lane[None, :]) % LANES) / LANES
    cosine, sine = np.cos(lane_angle), np.sin(lane_angle)
    middle = np.block([[cosine, -sine], [sine, cosine]])
    first_high, first_low = np_split(first)
    last_high, last_low = np_split(last)
    middle_high, middle_low = np_split(middle)
    return dict(
        first=np.concatenate([first_high, first_high, first_low], 1),
        last=np.concatenate([last_high, last_high, last_low], 1),
        middle=np.concatenate([middle_high, middle_low], 0),
        turn=np.concatenate([np.cos(turn), np.sin(turn)], 0).astype(np.float32),
    )


@functools.lru_cache(maxsize=None)
def feature_tables(length, feature_count):
    rows = length // LANES
    feature = np.arange(feature_count)
    multiplier = (1 + feature // 2 * 499) % length
    row_angle = 2.0 * np.pi * ((multiplier[:, None] * LANES * np.arange(rows)[None, :]) % length) / length
    lane_angle = 2.0 * np.pi * ((multiplier[:, None] * np.arange(LANES)[None, :]) % length) / length
    even = (feature % 2 == 0)[:, None]
    near = np.where(even, np.cos(row_angle), np.sin(row_angle))
    far = np.where(even, -np.sin(row_angle), np.cos(row_angle))
    lane = np.concatenate([np.cos(lane_angle), np.sin(lane_angle)], 0)
    lane_high, lane_low = np_split(lane.T)
    grad_lane = np.block([[lane_high, lane_low], [lane_high, np.zeros_like(lane_low)]])
    grad_row = np.concatenate([near, far, near, far], 0).T
    return (
        np.concatenate([near, far], 0).astype(np.float32),
        lane.astype(np.float32),
        grad_lane.astype(ml_dtypes.bfloat16),
        grad_row.astype(np.float32),
    )


def middle_dot(value, middle_ref):
    high, low = split(value)
    size = 2 * LANES
    table_high, table_low = middle_ref[:size, :], middle_ref[size:, :]
    left = jnp.concatenate([high, high, low], 1)
    return dot(left, jnp.concatenate([table_high, table_low, table_high], 0))


def forward(signals, first_ref, middle_ref, turn_ref):
    lows = turn_ref.shape[0] // 2
    high, low = split(jnp.concatenate(signals, 1))
    partial = dot(first_ref[...], jnp.concatenate([high, low, high], 0))
    cosine, sine = turn_ref[:lows, :], turn_ref[lows:, :]
    turned = []
    for index in range(len(signals)):
        real = partial[:lows, index * LANES : (index + 1) * LANES]
        imag = partial[lows:, index * LANES : (index + 1) * LANES]
        turned.append(
            jnp.concatenate([real * cosine + imag * sine, imag * cosine - real * sine], 1)
        )
    return middle_dot(jnp.concatenate(turned, 0), middle_ref)


def backward(spectra, last_ref, middle_ref, turn_ref):
    lows = turn_ref.shape[0] // 2
    swapped = jnp.concatenate([jnp.concatenate([imag, real], 1) for real, imag in spectra], 0)
    partial = middle_dot(swapped, middle_ref)
    cosine, sine = turn_ref[:lows, :], turn_ref[lows:, :]
    turned = []
    for index in range(len(spectra)):
        imag = partial[index * lows : (index + 1) * lows, :LANES]
        real = partial[index * lows : (index + 1) * lows, LANES:]
        turned.append(
            jnp.concatenate([real * cosine - imag * sine, imag * cosine + real * sine], 0)
        )
    high, low = split(jnp.concatenate(turned, 1))
    result = dot(last_ref[...], jnp.concatenate([high, low, high], 0))
    return [result[:, index * LANES : (index + 1) * LANES] for index in range(len(spectra))]


def later(value):
    turned = pltpu.roll(value, 1, 1)
    carried = pltpu.roll(turned, 1, 0)
    row = lax.broadcasted_iota(jnp.int32, value.shape, 0)
    lane = lax.broadcasted_iota(jnp.int32, value.shape, 1)
    carried = jnp.where(row == 0, 0.0, carried)
    return jnp.where(lane == 0, carried, turned)


def sooner(value):
    rows = value.shape[0]
    turned = pltpu.roll(value, LANES - 1, 1)
    carried = pltpu.roll(turned, rows - 1, 0)
    row = lax.broadcasted_iota(jnp.int32, value.shape, 0)
    lane = lax.broadcasted_iota(jnp.int32, value.shape, 1)
    carried = jnp.where(row == rows - 1, 0.0, carried)
    return jnp.where(lane == LANES - 1, carried, turned)


def sine_cosine(half_angle):
    turns = jnp.round(half_angle * (1.0 / math.pi))
    rest = half_angle - turns * 3.140625
    rest = rest - turns * 9.67653589793e-4
    square = rest * rest
    sine = 2.59045638e-06
    for coefficient in (-1.98008819e-04, 8.33289957e-03, -1.66666476e-01, 9.99999977e-01):
        sine = sine * square + coefficient
    cosine = 2.31536124e-05
    for coefficient in (-1.38536905e-03, 4.16635829e-02, -4.99999053e-01, 9.99999953e-01):
        cosine = cosine * square + coefficient
    sine = sine * rest
    twice = sine + sine
    return twice * cosine, 1.0 - twice * sine


def first_channel(per, channels):
    return lax.axis_index("seq") * per % channels


def own_rows(per, out_ref):
    channels = out_ref.shape[0]
    start = first_channel(per, channels)
    return pltpu.roll(out_ref[...], lax.rem(channels - start, channels), 0)[:8, :]


def tap_rows(short_ref):
    return jnp.concatenate([short_ref[index] for index in range(3)], 0)


def own_columns(per, value):
    channels = value.shape[1]
    start = first_channel(per, channels)
    turned = pltpu.roll(value, lax.rem(channels - start, channels), 1)
    return [turned[:, channel : channel + 1] for channel in range(per)]


def small_expm1(value):
    total = 1.0
    for divisor in (7.0, 6.0, 5.0, 4.0, 3.0, 2.0):
        total = 1.0 + total * value * (1.0 / divisor)
    return total * value


def pack_kernel(per, proj_ref, cot_ref, out_ref):
    channels = cot_ref.shape[0]
    whole = [proj_ref[index].astype(F32) for index in range(3)] + [cot_ref[...].astype(F32)]
    for device in range(out_ref.shape[0]):
        start = device * per % channels
        rows = jnp.concatenate([part[start : start + per, :] for part in whole], 0)
        out_ref[device] = rows.astype(BF16)


def block_features(table, lane_ref):
    count = lane_ref.shape[0] // 2
    lane_cos, lane_sin = lane_ref[:count, :], lane_ref[count:, :]
    near, far = table[:count, :], table[count:, :]
    rows = range(table.shape[1])
    blocks = [near[:, row : row + 1] * lane_cos + far[:, row : row + 1] * lane_sin for row in rows]
    return split(jnp.concatenate(blocks, 1))


def in_blocks(blocks, body):
    if blocks == 1:
        body(0)
    else:
        lax.fori_loop(0, blocks, lambda index, carry: (body(index), carry)[1], 0)


def block_copies(index, block, here, there, semaphores, outward):
    columns = pl.ds(pl.multiple_of(index * block, LANES), block)
    pairs = [(near, far.at[:, columns]) for near, far in zip(here, there, strict=True)]
    return [
        pltpu.make_async_copy(*(pair if outward else pair[::-1]), semaphores.at[at])
        for at, pair in enumerate(pairs)
    ]


def filter_kernel(per, length, blocks, *refs):
    given, loaded = refs[:12], refs[12:24]
    env_ref, spec_ref = refs[24:26]
    hidden_refs, buffers = refs[26:29], list(refs[29:-4])
    mod_ref, stage_ref, load_semaphores, out_semaphores = refs[-4:]
    loads = [
        pltpu.make_async_copy(source, target, load_semaphores.at[index])
        for index, (source, target) in enumerate(zip(given, loaded, strict=True))
    ]
    for load in loads:
        load.start()
    for load in loads:
        load.wait()
    first_ref, _, middle_ref, turn_ref, near_ref, lane_ref, _, _ = loaded[:8]
    in_ref, out_ref, rates_ref, _ = loaded[8:]
    rows = length // LANES
    block = length // blocks
    block_rows = rows // blocks
    if blocks == 1:
        buffers, hidden_refs = buffers + [hidden_refs[2]], hidden_refs[:2]
    sine_high_ref, sine_low_ref, cosine_ref = buffers
    buffers = buffers[: len(hidden_refs)]
    in_high, in_low = split(in_ref[...] * 0.5)
    in_weights = jnp.concatenate([in_high, in_high, in_low], 0)
    out_high, out_low = split(own_rows(per, out_ref))
    out_weights = jnp.concatenate([out_high, out_high, out_low], 1)

    def hidden_block(index):
        high, low = block_features(near_ref[index], lane_ref)
        half_angle = dot_first(in_weights, jnp.concatenate([high, low, high], 0))
        sine, cosine = sine_cosine(half_angle)
        cosine_ref[...] = cosine
        high, low = split(sine)
        sine_high_ref[...] = high
        sine_low_ref[...] = low
        copies = block_copies(index, block, buffers, hidden_refs, out_semaphores, True)
        for copy in copies:
            copy.start()
        mod_ref[...] = dot(out_weights, jnp.concatenate([high, low, high], 0))
        for row in range(block_rows):
            at = pl.multiple_of((index * block_rows + row) * 8, 8)
            stage_ref[pl.ds(at, 8), :] = mod_ref[:, row * LANES : (row + 1) * LANES]
        if blocks > 1:
            for copy in copies:
                copy.wait()

    in_blocks(blocks, hidden_block)
    rates = own_columns(per, rates_ref[...])
    position = lax.broadcasted_iota(jnp.int32, (rows, LANES), 0) * LANES
    position = position + lax.broadcasted_iota(jnp.int32, (rows, LANES), 1)
    relative = position.astype(F32) * (1.0 / length)
    kernels = []
    for channel in range(per):
        rate = -2.0 * jnp.broadcast_to(rates[channel], (8, LANES))
        inverse = jnp.sqrt(small_expm1(rate * (1.0 / length)) / (jnp.exp(rate) - 1.0))
        envelope = jnp.exp(0.5 * rate[:1, :] * relative) * inverse[:1, :]
        env_ref[channel * rows : (channel + 1) * rows, :] = envelope
        kernels.append(envelope * stage_ref[pl.ds(channel, rows, stride=8), :])
    spec_ref[...] = forward(kernels, first_ref, middle_ref, turn_ref)
    if blocks == 1:
        for copy in block_copies(0, block, buffers, hidden_refs, out_semaphores, True):
            copy.wait()


def signal_kernel(per, blocks, *refs):
    recv_ref, env_ref, first_ref, last_ref, middle_ref, turn_ref = refs[:6]
    lane_ref, row_ref, out_ref, short_ref, cosine_ref = refs[6:11]
    sines = refs[11:13]
    raw_ref, mixed_ref, spec_ref, weighted_ref, in_grad_ref = refs[13:18]
    stage_ref, semaphores = refs[-2:]
    devices, held, tokens = recv_ref.shape
    rows = devices * tokens // LANES
    block = rows * LANES // blocks
    block_rows = rows // blocks
    step = raw_ref.shape[0] // rows
    lows = turn_ref.shape[0] // 2
    ahead = []
    if blocks == 1:
        ahead = [
            pltpu.make_async_copy(source, target, semaphores.at[at])
            for at, source, target in zip((0, 1), sines, refs[18:20], strict=True)
        ]
        for copy in ahead:
            copy.start()
    taps = own_columns(per, tap_rows(short_ref))
    for device in range(devices):
        for part in range(tokens // LANES):
            at = (device * (tokens // LANES) + part) * step
            raw_ref[at : at + held, :] = recv_ref[
                device, :, part * LANES : (part + 1) * LANES
            ].astype(F32)
    gated, grads = [], []
    for channel in range(per):
        mixed = []
        for index in range(3):
            base = raw_ref[pl.ds(index * per + channel, rows, stride=step), :]
            total = taps[channel][3 * index : 3 * index + 1, :] * base
            for tap in (1, 2):
                base = later(base)
                total = total + taps[channel][3 * index + tap : 3 * index + tap + 1, :] * base
            mixed.append(total)
        cotangent = raw_ref[pl.ds(3 * per + channel, rows, stride=step), :]
        mixed_ref[2 * channel] = mixed[1]
        mixed_ref[2 * channel + 1] = mixed[2]
        gated.append(mixed[1] * mixed[2])
        grads.append(cotangent * mixed[0])
    spectra = forward(gated + grads, first_ref, middle_ref, turn_ref)
    spec_ref[...] = spectra
    products = []
    for channel in range(per):
        at, other = channel * lows, (per + channel) * lows
        gated_real, gated_imag = spectra[at : at + lows, :LANES], spectra[at : at + lows, LANES:]
        grad_real, grad_imag = (
            spectra[other : other + lows, :LANES],
            spectra[other : other + lows, LANES:],
        )
        products.append(
            (
                grad_real * gated_real + grad_imag * gated_imag,
                grad_imag * gated_real - grad_real * gated_imag,
            )
        )
    results = backward(products, last_ref, middle_ref, turn_ref)
    if per < 8:
        stage_ref[...] = jnp.zeros_like(stage_ref)
    for channel in range(per):
        weighted = results[channel] * env_ref[channel * rows : (channel + 1) * rows, :]
        stage_ref[pl.ds(channel, rows, stride=8), :] = weighted
    out_columns = own_rows(per, out_ref).T
    order, features = out_ref.shape[1], lane_ref.shape[1] // 4
    in_grad_ref[...] = jnp.zeros_like(in_grad_ref)

    def add_block(index):
        cosine_here = cosine_ref
        if blocks > 1:
            cosine_here = refs[-3]
            (copy,) = block_copies(index, block, [cosine_here], [cosine_ref], semaphores, False)
            copy.start()
            copy.wait()
        parts = []
        for row in range(block_rows):
            at = pl.multiple_of((index * block_rows + row) * 8, 8)
            parts.append(stage_ref[pl.ds(at, 8), :])
        weighted = jnp.concatenate(parts, 1)
        weighted_ref[:, pl.ds(pl.multiple_of(index * block, LANES), block)] = weighted
        spread = [
            jnp.broadcast_to(out_columns[:, channel : channel + 1], (order, LANES))
            for channel in range(per)
        ]
        scales = row_ref[pl.ds(pl.multiple_of(index * block_rows, 8), block_rows), :]
        total = jnp.zeros((order, LANES), F32)
        for start in range(0, block_rows, 8):
            parts = []
            for row in range(start, start + 8):
                lanes = slice(row * LANES, (row + 1) * LANES)
                grad = spread[0] * weighted[:1, lanes]
                for channel in range(1, per):
                    grad = grad + spread[channel] * weighted[channel : channel + 1, lanes]
                parts.append(jnp.concatenate(split(grad * cosine_here[:, lanes]), 1))
            parts = dot(jnp.concatenate(parts, 0), lane_ref[...])
            for row in range(8):
                scale = scales[start + row : start + row + 1, :]
                total = total + parts[row * order : (row + 1) * order, :] * scale
        total = total + pltpu.roll(total, 2 * features, 1)
        total = total + pltpu.roll(total, features, 1)
        total = total.T
        half = features // 2
        in_grad_ref[...] += jnp.concatenate([total[:half, :], total[half:features, :]], 1)

    in_blocks(blocks, add_block)
    for copy in ahead:
        copy.wait()


def proj_grad_kernel(
    per,
    blocks,
    scale,
    short_ref,
    raw_ref,
    mixed_ref,
    spec_ref,
    kernel_spec_ref,
    weighted_ref,
    last_ref,
    middle_ref,
    turn_ref,
    high_ref,
    low_ref,
    slab_ref,
    stage_ref,
    high_buffer=None,
    low_buffer=None,
    semaphores=None,
):
    order, block = high_ref.shape[0], high_ref.shape[1] // blocks
    devices = slab_ref.shape[0]
    rows = weighted_ref.shape[1] // LANES
    tokens = rows // devices * LANES
    held = stage_ref.shape[0] // rows
    taps = own_columns(per, tap_rows(short_ref))
    step = raw_ref.shape[0] // rows
    lows = turn_ref.shape[0] // 2
    products = []
    for sign in (1.0, -1.0):
        for channel in range(per):
            at = (channel if sign > 0 else per + channel) * lows
            real, imag = spec_ref[at : at + lows, :LANES], spec_ref[at : at + lows, LANES:]
            at = channel * lows
            kernel_real = kernel_spec_ref[at : at + lows, :LANES]
            kernel_imag = sign * kernel_spec_ref[at : at + lows, LANES:]
            products.append(
                (
                    real * kernel_real - imag * kernel_imag,
                    real * kernel_imag + imag * kernel_real,
                )
            )
    results = backward(products, last_ref, middle_ref, turn_ref)
    sums = [None] * (3 * per)
    for channel in range(per):
        cotangent = raw_ref[pl.ds(3 * per + channel, rows, stride=step), :]
        grad_mixed = (
            cotangent * results[channel],
            results[per + channel] * mixed_ref[2 * channel + 1],
            results[per + channel] * mixed_ref[2 * channel],
        )
        for index in range(3):
            base = raw_ref[pl.ds(index * per + channel, rows, stride=step), :]
            grad = grad_mixed[index]
            total = taps[channel][3 * index : 3 * index + 1, :] * grad
            parts = [jnp.sum(grad * base, axis=0, keepdims=True)]
            moved = grad
            for tap in (1, 2):
                base = later(base)
                moved = sooner(moved)
                total = total + taps[channel][3 * index + tap : 3 * index + tap + 1, :] * moved
                parts.append(jnp.sum(grad * base, axis=0, keepdims=True))
            sums[index * per + channel] = jnp.concatenate(parts, 0)
            stage_ref[pl.ds(index * per + channel, rows, stride=held), :] = total
    parts = tokens // LANES
    for device in range(devices):
        blocks_here = []
        for part in range(parts):
            at = (device * parts + part) * held
            blocks_here.append(stage_ref[at : at + held, :])
        for part in range(parts):
            lanes = slice(part * LANES, (part + 1) * LANES)
            slab_ref[device, :, lanes] = blocks_here[part][:8, :].astype(BF16)
        if held > 8:
            for part in range(parts // 2):
                lanes = slice(tokens + part * LANES, tokens + (part + 1) * LANES)
                pair = [blocks_here[part][8:12, :], blocks_here[part + parts // 2][8:12, :]]
                slab_ref[device, :, lanes] = jnp.concatenate(pair, 0).astype(BF16)
    row = lax.broadcasted_iota(jnp.int32, (8, LANES), 0)
    lane = lax.broadcasted_iota(jnp.int32, (8, LANES), 1)
    small = jnp.zeros((8, LANES), F32)
    for place in range(3 * per):
        index, channel = place // per, place % per
        total = jnp.sum(sums[place], axis=1, keepdims=True) * scale
        for tap in range(3):
            at = (row == per + channel) & (lane == 3 * index + tap)
            small = jnp.where(at, total[tap : tap + 1, :], small)
    out_grad = jnp.zeros((order, 2 * LANES), F32)
    for index in range(blocks):
        high_here, low_here = high_ref, low_ref
        if blocks > 1:
            high_here, low_here = high_buffer, low_buffer
            copies = block_copies(
                index, block, [high_here, low_here], [high_ref, low_ref], semaphores, False
            )
            for copy in copies:
                copy.start()
            for copy in copies:
                copy.wait()
        weighted = weighted_ref[:, index * block : (index + 1) * block]
        rounded = weighted.astype(BF16).astype(F32)
        both = jnp.concatenate([weighted, weighted - rounded], 0).astype(BF16)
        total = dot_last(high_here[...], both)
        total = total[:, :8] + total[:, 8:] + dot_last(low_here[...], both)[:, :8]
        out_grad = out_grad + jnp.concatenate([total, jnp.zeros((order, 2 * LANES - 8), F32)], 1)
    out_grad = jnp.concatenate([out_grad[:, :LANES], jnp.zeros((LANES - order, LANES), F32)], 0)
    out_grad = out_grad.T[:8, :] * scale
    small = jnp.where(row < per, out_grad, small)
    rest = pltpu.roll(small - small.astype(BF16).astype(F32), LANES // 2, 1)
    small = jnp.where(lane < LANES // 2, small, rest).astype(BF16)
    for device in range(devices):
        slab_ref[device, :, slab_ref.shape[2] - LANES :] = small


def finish_kernel(scale, slab_ref, *refs):
    parts, result_ref = [ref[...] for ref in refs[:-1]], refs[-1]
    while len(parts) > 1:
        parts = [parts[at] + parts[at + 1] for at in range(0, len(parts), 2)]
    total = parts[0] * scale
    halves = jnp.concatenate([total, total - total.astype(BF16).astype(F32)], 0)
    count = halves.shape[0] // 8
    wide = jnp.concatenate([halves[8 * index : 8 * index + 8, :] for index in range(count)], 1)
    wide = wide.astype(BF16)
    start, end = slab_ref.shape[2] - (count + 1) * LANES, slab_ref.shape[2] - LANES
    for device in range(slab_ref.shape[0]):
        result_ref[device, :, start:end] = wide


def unpack_kernel(per, recv_ref, proj_ref, short_ref, out_ref):
    channels, tokens = proj_ref.shape[1:]
    devices = channels // per
    order = out_ref.shape[1]
    slabs = [recv_ref[device].astype(F32) for device in range(devices)]
    for index in range(3):
        rows = []
        for slab in slabs:
            if index * per < 8:
                rows.append(slab[index * per : (index + 1) * per, :tokens])
            else:
                lanes = slice(tokens, tokens + tokens // 2)
                rows.append(jnp.concatenate([slab[:per, lanes], slab[per : 2 * per, lanes]], 1))
        proj_ref[index] = jnp.concatenate(rows, 0).astype(BF16)
    small = [slab[:, slab.shape[1] - LANES :] for slab in slabs]
    small = [part + pltpu.roll(part, LANES // 2, 1) for part in small]
    out_ref[...] = jnp.concatenate([part[:per, :order] for part in small], 0)
    rows = jnp.concatenate([part[per : 2 * per, :] for part in small], 0).T
    for index in range(3):
        short_ref[index] = rows[3 * index : 3 * index + 3, :]


def in_sum_kernel(sources, recv_ref, sum_ref):
    count = sum_ref.shape[0] // 4
    start = recv_ref.shape[2] - (count + 1) * LANES
    total = recv_ref[0, :, start : start + count * LANES].astype(F32)
    for source in range(1, sources):
        total = total + recv_ref[source, :, start : start + count * LANES].astype(F32)
    total = [total[:, index * LANES : (index + 1) * LANES] for index in range(count)]
    sum_ref[...] = jnp.concatenate(total[: count // 2], 0) + jnp.concatenate(total[count // 2 :], 0)


def in_grad_kernel(own_ref, other_ref, in_ref):
    half, order = in_ref.shape[0] // 2, in_ref.shape[1]
    total = own_ref[...] + other_ref[...]
    in_ref[:half, :] = total[:, :order]
    in_ref[half:, :] = total[:, order:]


def call(kernel, out, limit, in_specs=None, out_specs=None, flops=0, moved=0, **more):
    vmem = pl.BlockSpec(memory_space=pltpu.VMEM)
    return pl.pallas_call(
        kernel,
        out_shape=out,
        in_specs=in_specs,
        out_specs=out_specs if out_specs is not None else jax.tree.map(lambda _: vmem, out),
        compiler_params=pltpu.CompilerParams(vmem_limit_bytes=limit),
        cost_estimate=pl.CostEstimate(flops=flops, bytes_accessed=moved, transcendentals=0),
        **more,
    )


def shards(proj, cotangent, short_w, filter_in, filter_out, rates):
    vmem = pl.BlockSpec(memory_space=pltpu.VMEM)
    hbm = pl.BlockSpec(memory_space=pltpu.HBM)
    channels, tokens = cotangent.shape
    devices = lax.axis_size("seq")
    groups = lax.axis_size("ch")
    length = devices * tokens
    rows = length // LANES
    lows = rows + 8
    features, order = filter_in.shape
    scale = 1.0 / math.sqrt(length)
    per = max(1, channels // devices)
    held = 4 * per
    step = max(8, held)
    width = tokens if 3 * per <= 8 else tokens + tokens // 2
    blocks = max(1, rows // 64)
    block = length // blocks
    small = blocks == 1
    limit = (24 if small else 56) * MIB
    sds = jax.ShapeDtypeStruct
    made = pltpu.VMEM if small else sds
    put = (lambda x: pltpu.with_memory_space_constraint(x, pltpu.VMEM)) if small else (lambda x: x)
    keep = lambda x: pltpu.with_memory_space_constraint(x, pltpu.HBM)

    packed = call(
        functools.partial(pack_kernel, per),
        sds((devices, held, tokens), BF16),
        limit,
        in_specs=[vmem] * 2,
    )(keep(proj), keep(cotangent))
    recv = lax.all_to_all(packed, "seq", split_axis=0, concat_axis=0, tiled=True)

    near, *lane_tables = feature_tables(length, features)
    near = near.reshape(2 * features, blocks, rows // blocks).transpose(1, 0, 2)
    tables = transform_tables(length)
    given = [tables[name] for name in ("first", "last", "middle", "turn")]
    given += [near, *lane_tables]
    given = [jnp.asarray(value) for value in given]
    given += [filter_in, filter_out.T, rates.reshape(1, channels), short_w.transpose(0, 2, 1)]
    hidden = tuple(pltpu.HBM((order, length), BF16) for _ in range(2))
    hidden += ((made if small else pltpu.HBM)((order, length), F32),)
    buffers = [pltpu.VMEM((order, block), kind) for kind in (BF16, BF16, F32)]
    *loaded, envelope, kernel_spec, sine_high, sine_low, cosine = call(
        functools.partial(filter_kernel, per, length, blocks),
        tuple(made(value.shape, value.dtype) for value in given)
        + (made((per * rows, LANES), F32), made((per * lows, 2 * LANES), F32))
        + hidden,
        limit,
        in_specs=[hbm] * len(given),
        out_specs=(vmem,) * (len(given) + 2) + (hbm, hbm, vmem if small else hbm),
        scratch_shapes=(buffers[:2] if small else buffers)
        + [
            pltpu.VMEM((8, block), F32),
            pltpu.VMEM((rows * 8, LANES), F32),
            pltpu.SemaphoreType.DMA((len(given),)),
            pltpu.SemaphoreType.DMA((3,)),
        ],
        flops=8 * length * order * 3 * features,
        moved=length * order * 8,
    )(*[keep(value) for value in given])
    first, last, middle, turn, _, _, grad_lane, grad_row = map(put, loaded[:8])
    _, out_rows, _, short_taps = map(put, loaded[8:])

    raw, mixed, spec, weighted, in_grad, *sines = call(
        functools.partial(signal_kernel, per, blocks),
        (
            made((rows * step, LANES), F32),
            made((2 * per, rows, LANES), F32),
            made((2 * per * lows, 2 * LANES), F32),
            made((8, length), F32),
            sds((features // 2, 2 * order), F32),
        )
        + ((made((order, length), BF16),) * 2 if small else ()),
        limit,
        in_specs=[vmem] * 10 + [vmem if small else hbm] + [hbm] * 2,
        scratch_shapes=([] if small else buffers[2:])
        + [pltpu.VMEM((rows * 8, LANES), F32), pltpu.SemaphoreType.DMA((2,))],
        flops=400 * length * LANES,
    )(
        put(recv),
        put(envelope),
        first,
        last,
        middle,
        turn,
        grad_lane,
        grad_row,
        out_rows,
        short_taps,
        put(cosine) if small else keep(cosine),
        keep(sine_high),
        keep(sine_low),
    )
    if not small:
        sines = [sine_high, sine_low]

    def exchange(value, by):
        return lax.ppermute(value, "ch", [(i, i ^ by) for i in range(groups)])

    steps = [1 << step for step in range(1, groups.bit_length() - 1)][::-1]
    for by in steps[:-1]:
        in_grad = in_grad + exchange(in_grad, by)
    others = [exchange(in_grad, by) for by in steps[-1:]]
    shape = (devices, 8, width + features // 8 * LANES + LANES)
    slab = call(
        functools.partial(proj_grad_kernel, per, blocks, scale),
        made(shape, BF16),
        limit,
        in_specs=[vmem] * 9 + [vmem if small else hbm] * 2,
        scratch_shapes=[pltpu.VMEM((rows * max(8, held), LANES), F32)]
        + ([] if small else [*buffers[:2], pltpu.SemaphoreType.DMA((2,))]),
        flops=400 * length * LANES,
    )(
        short_taps,
        put(raw),
        put(mixed),
        put(spec),
        put(kernel_spec),
        put(weighted),
        last,
        middle,
        turn,
        *[put(value) if small else keep(value) for value in sines],
    )
    slab = call(
        functools.partial(finish_kernel, scale),
        made(shape, BF16),
        limit,
        in_specs=[vmem] * (2 + len(others)),
        input_output_aliases={0: 0},
    )(put(slab), in_grad, *others)

    back = lax.all_to_all(slab, "seq", split_axis=0, concat_axis=0, tiled=True)
    in_sum = call(
        functools.partial(in_sum_kernel, channels // per),
        made((features // 2, 2 * order), F32),
        limit,
        in_specs=[vmem],
    )(back)
    in_other = exchange(in_sum, 1)
    grad_proj, grad_short, grad_out = call(
        functools.partial(unpack_kernel, per),
        (
            sds((3, channels, tokens), BF16),
            sds((3, 3, channels), F32),
            sds((channels, order), F32),
        ),
        limit,
        in_specs=[vmem],
    )(back)
    grad_in = call(
        in_grad_kernel,
        sds((features, order), F32),
        limit,
        in_specs=[vmem] * 2,
    )(put(in_sum), in_other)
    return grad_proj, grad_short.transpose(0, 2, 1), grad_out.T, grad_in


def solution(mesh):
    placed = (
        P(None, "ch", "seq"),
        P("ch", "seq"),
        P(None, "ch", None),
        P(),
        P(None, "ch"),
        P("ch"),
    )
    return jax.shard_map(
        shards,
        mesh=mesh,
        in_specs=placed,
        out_specs=(P(None, "ch", "seq"), P(None, "ch", None), P(None, "ch"), P()),
        check_vma=False,
    )
```
